32 devices in a mesh: rcv: 2 (over x), shot: 16 (over z, y, core).
Axes of the slice: x: 2, y: 2, z: 4, core: 2. Of those that a mesh axis runs over, the one named last changes fastest.
Arguments:
- record_data: float32 [16, 16, 128, 256], P(None, 'shot', None, 'rcv'), may hold values from -20 to 20
- offsets: int32 [256], replicated, may hold values from 0 to 240, as said below
- thresholds: float32 [128], replicated, may hold values from 0.3 to 1.5
Outputs:
- model: bfloat16 [256, 4, 128, 256], P('shot', None, None, 'rcv')
- residual: float32 [16, 16, 128, 256], P(None, 'shot', None, 'rcv')
The draws below stay inside these ranges and needn't reach their ends.
Inputs may be any that keep to these rules, and one draw needn't show every extreme that they name: offsets[s] + 3 < 256. Shot s belongs to shot group s // 16. Among the blocks of the 16 shots of one group, at most 6 land on record blocks of one owner (block g belongs to owner g % 16), and those cover at most 3 distinct record blocks; every group reaches both bounds at some owner.
All inputs are finite; a program needn't handle non-finite values.
Results may differ from the reference program's by a relative error of at most 0.0087.
Values may be sent and summed in bfloat16 or wider, within the bound.
No kernel may reach another device: no remote copies, remote signals or barrier semaphores. Data moves between devices by JAX's collectives and lax.ppermute only.
A program may use at most 64 MiB of HBM per device.

```python
import math
import jax
import jax.numpy as jnp
from jax import lax

BLOCK = 128
SHOT_DEV = 16
SHOT_BLK = 4
WIN_DEV = 16
OWNERS = 16
SHOTS = 256
RCV = 256
PAIR_SLOTS = 3
STRIDE = 5


def draw_offsets(key, part):
    key = jax.random.fold_in(key, 11)
    key_turn, key_shift, key_start, key_delay = jax.random.split(key, 4)
    pair_count = SHOT_DEV // 2
    turn = jax.random.randint(key_turn, (OWNERS, 1), 0, OWNERS)
    shift = jax.random.randint(key_shift, (OWNERS, PAIR_SLOTS), 0, STRIDE - SHOT_BLK)
    start = jax.random.randint(key_start, (OWNERS, PAIR_SLOTS), 0, WIN_DEV - 1)
    delay = jax.random.randint(key_delay, (OWNERS, pair_count), 0, 2)
    pair_ids = jnp.arange(pair_count, dtype=jnp.int32)
    position = pair_ids % PAIR_SLOTS
    round_ids = pair_ids // PAIR_SLOTS
    residue = (turn + position[None, :] * STRIDE + shift[:, position]) % OWNERS
    window = (start[:, position] + round_ids[None, :]) % (WIN_DEV - 1)
    first = window * OWNERS + residue
    both = jnp.stack([first, first + delay], axis=2)
    return both.reshape(-1).astype(jnp.int32)


def coloured_blocks(base, white, notch, power):
    middle = base[:, :, 1:-1, :]
    filtered = base[:, :, :-2, :] + 2.0 * notch * middle + base[:, :, 2:, :] + 0.4 * white
    norm = jnp.sqrt(2.0 + 4.0 * notch * notch + 0.16)
    return filtered / norm * power


def draw_record_data(key, part):
    key = jax.random.fold_in(key, 5)
    key_base = jax.random.fold_in(key, 0)
    key_windows = jax.random.fold_in(key, 2)
    key_notch = jax.random.fold_in(key, 3)
    key_white = jax.random.fold_in(key, 4)
    long_shape = (WIN_DEV, OWNERS, BLOCK + 2, RCV)
    shape = (WIN_DEV, OWNERS, BLOCK, RCV)
    ramp = 3.0 ** (jnp.arange(RCV, dtype=jnp.float32) / RCV - 0.5)
    notch = jax.random.uniform(key_notch, (WIN_DEV, OWNERS, 1, 1), jnp.float32, -1.0, 1.0)
    base = jnp.clip(jax.random.normal(key_base, long_shape, jnp.float32), -5.0, 5.0)
    white = jnp.clip(jax.random.normal(key_white, shape, jnp.float32), -5.0, 5.0)
    power = jnp.exp(jax.random.uniform(key_windows, (WIN_DEV, OWNERS, 1, 1), jnp.float32, math.log(0.35), math.log(2.8)))
    values = coloured_blocks(base, white, notch, power) * ramp
    return jnp.clip(values, -20.0, 20.0).astype(jnp.float32)


def setup_inputs(seed: int = 0) -> dict:
    splits = jax.random.split(jax.random.key(seed), 4)
    record_data = draw_record_data(jax.random.fold_in(splits[3], 71), 0)
    offsets = draw_offsets(jax.random.fold_in(splits[3], 71), 0)
    thresholds = jnp.clip(jnp.exp(jax.random.uniform(splits[2], (BLOCK,), jnp.float32, math.log(0.3), math.log(1.5))), 0.3, 1.5)
    return dict(record_data=record_data, offsets=offsets, thresholds=thresholds)


momentum = 0.5
epsilon = 1e-06

def cosine_table(length):
    rows = jnp.arange(length, dtype=jnp.float32)[:, None]
    cols = jnp.arange(length, dtype=jnp.float32)[None, :]
    table = jnp.cos(jnp.pi * (cols + 0.5) * rows / length) * jnp.sqrt(2.0 / length)
    return jnp.where(rows == 0, table * jnp.sqrt(0.5), table)

def analysis(table, values):
    return jnp.einsum('kn,sbnr->sbkr', table, values, precision=lax.Precision.HIGHEST)

def synthesis(table, coefficients):
    return jnp.einsum('kn,sbkr->sbnr', table, coefficients, precision=lax.Precision.HIGHEST)

def shrink(coefficients, thresholds):
    energy = lax.optimization_barrier(jnp.sum(coefficients * coefficients, axis=(1, 3))) / (SHOT_BLK * RCV)
    cutoff = (thresholds[None, :] * jnp.sqrt(energy + epsilon))[:, None, :, None]
    return coefficients - jnp.clip(coefficients, -cutoff, cutoff)

def reference(record_data, offsets, thresholds):
    total = WIN_DEV * OWNERS
    segment_traversals = jnp.arange(SHOT_BLK, dtype=jnp.int32)
    assigned_segments = (offsets[:, None] + segment_traversals[None, :]).reshape(-1).astype(jnp.int32)
    coverage = jax.ops.segment_sum(jnp.ones(assigned_segments.shape, jnp.float32), assigned_segments, num_segments=total)
    precondition = (1.0 / jnp.maximum(coverage, 1.0))[:, None, None]
    records = record_data.reshape(total, BLOCK, RCV)
    table = cosine_table(BLOCK)
    first_spread = (records * precondition).astype(jnp.bfloat16)
    first_update = first_spread[assigned_segments].astype(jnp.float32).reshape(SHOTS, SHOT_BLK, BLOCK, RCV)
    first_shrunk = shrink(analysis(table, first_update), thresholds)
    first_model = synthesis(table, first_shrunk)
    sent_model = first_model.astype(jnp.bfloat16)
    members = SHOT_DEV * SHOT_BLK
    group_placed = assigned_segments.reshape(OWNERS, members)
    same_block = (group_placed[:, :, None] == group_placed[:, None, :]).astype(jnp.float32)
    position = jnp.arange(members, dtype=jnp.int32)
    earlier = (position[None, :] < position[:, None])[None, :, :]
    leading = lax.optimization_barrier(jnp.sum(jnp.where(earlier & (same_block > 0.5), 1, 0), axis=2)) == 0
    group_blocks = sent_model.astype(jnp.float32).reshape(OWNERS, members, BLOCK * RCV)
    group_sum = jnp.einsum('gij,gjf->gif', same_block, group_blocks, precision=lax.Precision.HIGHEST).astype(jnp.bfloat16)
    kept = jnp.where(leading[:, :, None], group_sum.astype(jnp.float32), 0.0).reshape(-1, BLOCK, RCV)
    blended = jax.ops.segment_sum(kept, assigned_segments, num_segments=total)
    residual = records - (1.0 + momentum) * blended
    second_spread = (residual * precondition).astype(jnp.bfloat16)
    gathered = second_spread[assigned_segments].astype(jnp.float32).reshape(SHOTS, SHOT_BLK, BLOCK, RCV)
    second_update = (1.0 + momentum) * first_model + gathered
    second_shrunk = shrink(analysis(table, second_update), thresholds)
    model = synthesis(table, second_shrunk).astype(jnp.bfloat16)
    return (model, residual.reshape(WIN_DEV, OWNERS, BLOCK, RCV))
```

```python
import jax
import jax.numpy as jnp
import numpy as np
from jax import lax
from jax.experimental import pallas as pl
from jax.experimental.pallas import tpu as pltpu
from jax.sharding import PartitionSpec as P

SHOT_BLK = 4
momentum = 0.5
epsilon = 1e-06
step_size = 1.0 + momentum
VMEM_BYTES = 48 * 1024 * 1024


def cosine_table(length):
    rows = np.arange(length, dtype=np.float64)[:, None]
    cols = np.arange(length, dtype=np.float64)[None, :]
    table = np.cos(np.pi * (cols + 0.5) * rows / length) * np.sqrt(2.0 / length)
    return np.where(rows == 0, table * np.sqrt(0.5), table).astype(np.float32)


def split_bf16(values):
    high = values.astype(jnp.bfloat16)
    low = (values - high.astype(jnp.float32)).astype(jnp.bfloat16)
    return high, low


def full_vmem():
    return pl.BlockSpec(memory_space=pltpu.VMEM)


def full_smem():
    return pl.BlockSpec(memory_space=pltpu.SMEM)


def params(**kw):
    return pltpu.CompilerParams(vmem_limit_bytes=VMEM_BYTES, **kw)


def forward(high, low, values):
    dims = (((0,), (0,)), ((), ()))
    return lax.dot_general(
        values, high, dims, preferred_element_type=jnp.float32
    ) + lax.dot_general(values, low, dims, preferred_element_type=jnp.float32)


def backward(both, coefficients):
    doubled = jnp.concatenate([coefficients, coefficients], axis=1)
    return lax.dot_general(
        both, doubled, (((1,), (1,)), ((), ())), preferred_element_type=jnp.float32
    )


def head(records, offsets, me, owners, high, low):
    windows, block, rcv = records.shape
    shots = offsets.shape[0]
    step = 8

    def body(me_ref, off_ref, rec_ref, high_ref, low_ref, sent_ref, coef_ref, energy_ref):
        base = pl.program_id(0) * step
        ids = (base + lax.broadcasted_iota(jnp.int32, (step, shots), 0)) * owners + me_ref[0]
        lag = ids - off_ref[...]
        cover = jnp.sum(
            jnp.where((lag >= 0) & (lag < SHOT_BLK), 1.0, 0.0), axis=1, keepdims=True
        )
        scale = 1.0 / jnp.maximum(cover, 1.0)
        for w in range(step):
            spread = (rec_ref[w] * scale[w : w + 1, 0:1]).astype(jnp.bfloat16)
            coef = forward(high_ref[...], low_ref[...], spread)
            coef_ref[w] = coef
            sent_ref[w] = coef.astype(jnp.bfloat16)
            energy_ref[w : w + 1, :] = jnp.sum(coef * coef, axis=0, keepdims=True)

    return pl.pallas_call(
        body,
        grid=(windows // step,),
        in_specs=[
            full_smem(),
            full_vmem(),
            pl.BlockSpec((step, block, rcv), lambda i: (i, 0, 0)),
            full_vmem(),
            full_vmem(),
        ],
        out_specs=[
            pl.BlockSpec((step, rcv, block), lambda i: (i, 0, 0)),
            pl.BlockSpec((step, rcv, block), lambda i: (i, 0, 0)),
            pl.BlockSpec((step, block), lambda i: (i, 0)),
        ],
        out_shape=[
            jax.ShapeDtypeStruct((windows, rcv, block), jnp.bfloat16),
            jax.ShapeDtypeStruct((windows, rcv, block), jnp.float32),
            jax.ShapeDtypeStruct((windows, block), jnp.float32),
        ],
        compiler_params=params(),
        name="analysis_of_records",
    )(me[None], offsets[None, :], records, high, low)


def pack(table, sent, energy, owners, capacity):
    windows, rcv, block = sent.shape
    rows = capacity * rcv + 2 * windows
    step = 4

    def body(table_ref, sent_ref, energy_ref, out_ref):
        first = pl.program_id(0) * step
        high, low = split_bf16(energy_ref[...])
        for h in range(step):
            for i in range(capacity):
                window = table_ref[(first + h) * capacity + i]
                out_ref[h, i * rcv : (i + 1) * rcv, :] = sent_ref[window]
            out_ref[h, capacity * rcv : capacity * rcv + windows, :] = high
            out_ref[h, capacity * rcv + windows : rows, :] = low

    return pl.pallas_call(
        body,
        grid=(owners // step,),
        in_specs=[full_smem(), full_vmem(), full_vmem()],
        out_specs=pl.BlockSpec((step, rows, block), lambda i: (i, 0, 0)),
        out_shape=jax.ShapeDtypeStruct((owners, rows, block), jnp.bfloat16),
        compiler_params=params(),
        name="pack_blocks",
    )(table, sent, energy)


def clipped_sum(coef, cut_ref, low, high):
    def add(row, total):
        cut = cut_ref[row][None]
        return total + jnp.minimum(jnp.maximum(coef, -cut), cut)

    return lax.fori_loop(low, high, add, jnp.zeros_like(coef))


def second(arrived, hits, thresholds, lows, highs, scales, slots, capacity, windows, receivers):
    owners, rows, block = arrived.shape
    rcv = (rows - 2 * windows) // capacity
    tiles = rcv // 8
    shot_dev = slots.shape[0] // SHOT_BLK
    shots = hits.shape[0] - shot_dev
    step = min(4, shot_dev)
    count = owners * capacity

    def body(
        low_ref, high_ref, scale_ref, slot_ref, in_ref, hit_ref, thr_ref,
        out_ref, energy_ref, cuts_ref, wide_ref, diff_ref,
    ):
        def block_of(slot):
            owner = slot // capacity
            start = pl.multiple_of((slot - owner * capacity) * rcv, rcv)
            values = in_ref[owner, pl.ds(start, rcv), :].astype(jnp.float32)
            return values.reshape(tiles, 8, block)

        @pl.when(pl.program_id(0) == 0)
        def _():
            at = capacity * rcv
            both = jnp.concatenate(
                [
                    in_ref[:, at : at + windows, :].reshape(owners * windows, block),
                    in_ref[:, at + windows :, :].reshape(owners * windows, block),
                ],
                axis=1,
            )
            sums = jnp.dot(hit_ref[...], both, preferred_element_type=jnp.float32)
            energy = sums[:, :block] + sums[:, block:]
            cuts_ref[...] = thr_ref[...] * jnp.sqrt(energy / (SHOT_BLK * receivers) + epsilon)

            def widen(i, _):
                part = cuts_ref[pl.ds(pl.multiple_of(i * 8, 8), 8), :]
                wide_ref[pl.ds(pl.multiple_of(i * 8, 8), 8)] = jnp.broadcast_to(
                    part[:, None, :], (8, 8, block)
                )
                return 0

            lax.fori_loop(0, (shots + shot_dev) // 8, widen, 0)

            def difference(slot, _):
                low, high = low_ref[slot], high_ref[slot]
                coef = block_of(slot)
                clipped = clipped_sum(coef, wide_ref, low, high)
                many = (high - low).astype(jnp.float32)
                diff_ref[slot] = coef - scale_ref[slot] * (many * coef - clipped)
                return 0

            lax.fori_loop(0, count, difference, 0)

        def one_shot(i, _):
            shot = pl.program_id(0) * step + i
            cut = wide_ref[shots + shot][None]
            energy = jnp.zeros((8, block), jnp.float32)
            for q in range(SHOT_BLK):
                slot = slot_ref[shot * SHOT_BLK + q]
                coef = block_of(slot)
                shrunk = coef - jnp.minimum(jnp.maximum(coef, -cut), cut)
                value = step_size * shrunk + diff_ref[slot]
                out_ref[i, q] = value.reshape(rcv, block)
                energy = energy + jnp.sum(value * value, axis=0)
            energy_ref[pl.ds(shot, 1), :] = jnp.sum(energy, axis=0, keepdims=True)
            return 0

        lax.fori_loop(0, step, one_shot, 0)

    return pl.pallas_call(
        body,
        grid=(shot_dev // step,),
        in_specs=[full_smem()] * 4 + [full_vmem()] * 3,
        out_specs=[
            pl.BlockSpec((step, SHOT_BLK, rcv, block), lambda i: (i, 0, 0, 0)),
            full_vmem(),
            full_vmem(),
        ],
        out_shape=[
            jax.ShapeDtypeStruct((shot_dev, SHOT_BLK, rcv, block), jnp.float32),
            jax.ShapeDtypeStruct((shot_dev, block), jnp.float32),
            jax.ShapeDtypeStruct((shots + shot_dev, block), jnp.float32),
        ],
        scratch_shapes=[
            pltpu.VMEM((shots + shot_dev, 8, block), jnp.float32),
            pltpu.VMEM((count, tiles, 8, block), jnp.float32),
        ],
        compiler_params=params(),
        cost_estimate=pl.CostEstimate(flops=1, bytes_accessed=12 << 20, transcendentals=0),
        name="second_coefficients",
    )(lows, highs, scales, slots, arrived, hits, thresholds)


def remainder(records, coefs, cuts, lows, highs, both):
    windows, block, rcv = records.shape
    shots = cuts.shape[0]
    tiles = rcv // 8
    step = 4

    def body(low_ref, high_ref, rec_ref, coef_ref, cuts_ref, both_ref, out_ref, wide_ref):
        @pl.when(pl.program_id(0) == 0)
        def _():
            def widen(i, _):
                part = cuts_ref[pl.ds(pl.multiple_of(i * 8, 8), 8), :]
                wide_ref[pl.ds(pl.multiple_of(i * 8, 8), 8)] = jnp.broadcast_to(
                    part[:, None, :], (8, 8, block)
                )
                return 0

            lax.fori_loop(0, shots // 8, widen, 0)

        for w in range(step):
            window = pl.program_id(0) * step + w
            low, high = low_ref[window], high_ref[window]
            coef = coef_ref[w].reshape(tiles, 8, block)
            clipped = clipped_sum(coef, wide_ref, low, high)
            shrunk = ((high - low).astype(jnp.float32) * coef - clipped).reshape(rcv, block)
            part, rest = split_bf16(shrunk)
            blended = backward(both_ref[...], part) + lax.dot_general(
                both_ref[:, :block], rest, (((1,), (1,)), ((), ())),
                preferred_element_type=jnp.float32,
            )
            out_ref[w] = rec_ref[w] - step_size * blended

    return pl.pallas_call(
        body,
        grid=(windows // step,),
        in_specs=[
            full_smem(),
            full_smem(),
            pl.BlockSpec((step, block, rcv), lambda i: (i, 0, 0)),
            pl.BlockSpec((step, rcv, block), lambda i: (i, 0, 0)),
            full_vmem(),
            full_vmem(),
        ],
        out_specs=pl.BlockSpec((step, block, rcv), lambda i: (i, 0, 0)),
        out_shape=jax.ShapeDtypeStruct((windows, block, rcv), jnp.float32),
        scratch_shapes=[pltpu.VMEM((shots, 8, block), jnp.float32)],
        compiler_params=params(),
        cost_estimate=pl.CostEstimate(flops=1, bytes_accessed=6 << 20, transcendentals=0),
        name="residual_of_records",
    )(lows, highs, records, coefs, cuts, both)


def finish(values, energies, thresholds, both, receivers):
    shot_dev, _, rcv, block = values.shape
    step = min(4, shot_dev)

    def body(*refs):
        in_ref, thr_ref, both_ref = refs[:3]
        out_ref = refs[-1]
        energy = refs[3][...]
        for ref in refs[4:-1]:
            energy = energy + ref[...]
        cuts = thr_ref[...] * jnp.sqrt(energy / (SHOT_BLK * receivers) + epsilon)
        for i in range(step):
            cut = cuts[i : i + 1, :]
            for q in range(SHOT_BLK):
                value = in_ref[i, q]
                shrunk = value - jnp.minimum(jnp.maximum(value, -cut), cut)
                out_ref[i, q] = backward(both_ref[...], shrunk.astype(jnp.bfloat16)).astype(
                    jnp.bfloat16
                )

    shape = (shot_dev // step, step, block)
    energies = [energy.reshape(shape) for energy in energies]
    return pl.pallas_call(
        body,
        grid=(shot_dev // step,),
        in_specs=[
            pl.BlockSpec((step, SHOT_BLK, rcv, block), lambda i: (i, 0, 0, 0)),
            full_vmem(),
            full_vmem(),
        ]
        + [pl.BlockSpec((None, step, block), lambda i: (i, 0, 0))] * len(energies),
        out_specs=pl.BlockSpec((step, SHOT_BLK, block, rcv), lambda i: (i, 0, 0, 0)),
        out_shape=jax.ShapeDtypeStruct((shot_dev, SHOT_BLK, block, rcv), jnp.bfloat16),
        compiler_params=params(),
        name="model_of_shots",
    )(values, thresholds, both, *energies)


def over_receivers(values):
    if lax.axis_size("rcv") == 2:
        return [values, lax.ppermute(values, "rcv", [(0, 1), (1, 0)])]
    return [lax.psum(values, "rcv")]


def local(record_data, offsets, thresholds):
    owners = lax.axis_size("shot")
    me = lax.axis_index("shot")
    windows, _, block, rcv = record_data.shape
    shots = offsets.shape[0]
    shot_dev = shots // owners
    pairs = shot_dev // 2
    pair_slots = min(pairs, owners // (SHOT_BLK + 1))
    capacity = (pairs + pair_slots - 1) // pair_slots
    receivers = rcv * lax.axis_size("rcv")

    table = jnp.asarray(cosine_table(block).T)
    high, low = split_bf16(table)
    both = jnp.concatenate([high, low], axis=1)
    records = record_data.reshape(windows, block, rcv)
    thr = thresholds[None, :]
    window_ids = jnp.arange(windows, dtype=jnp.int32)

    sent, coefs, energy = head(records, offsets, me, owners, high, low)
    energy = sum(over_receivers(energy))

    def ranks(present, axis):
        before = (window_ids[:, None] < window_ids[None, :]).astype(jnp.int32)
        return jnp.sum(present[..., :, None] * before, axis=axis)

    own_ids = window_ids * owners + me
    lag = own_ids[None, None, :] - offsets.reshape(owners, shot_dev)[:, :, None]
    present = jnp.max(((lag >= 0) & (lag < SHOT_BLK)).astype(jnp.int32), axis=1)
    rank = ranks(present, 1)
    slot_ids = jnp.arange(capacity, dtype=jnp.int32)
    chosen = (rank[:, None, :] == slot_ids[None, :, None]) & (present[:, None, :] > 0)
    send_table = jnp.sum(jnp.where(chosen, window_ids[None, None, :], 0), axis=2)
    packed = pack(send_table.reshape(-1), sent, energy, owners, capacity)
    arrived = lax.all_to_all(packed, "shot", split_axis=0, concat_axis=0, tiled=True)

    index = jnp.arange(shots, dtype=jnp.int32)
    ahead = (offsets[None, :] < offsets[:, None]) | (
        (offsets[None, :] == offsets[:, None]) & (index[None, :] < index[:, None])
    )
    place = jnp.sum(ahead.astype(jnp.int32), axis=1)
    ordered = jnp.sum(jnp.where(place[None, :] == index[:, None], offsets[None, :], 0), axis=1)
    mine = lax.dynamic_slice(offsets, (me * shot_dev,), (shot_dev,))
    all_offsets = jnp.concatenate([ordered, mine])
    grid_ids = (
        window_ids[None, :] * owners + jnp.arange(owners, dtype=jnp.int32)[:, None]
    )
    hit = grid_ids.reshape(-1)[None, :] - all_offsets[:, None]
    hits = ((hit >= 0) & (hit < SHOT_BLK)).astype(jnp.bfloat16)

    def bounds(ids):
        below = jnp.sum((offsets < ids[..., None] - (SHOT_BLK - 1)).astype(jnp.int32), axis=-1)
        upto = jnp.sum((offsets <= ids[..., None]).astype(jnp.int32), axis=-1)
        return below, upto

    near = grid_ids[:, :, None] - mine[None, None, :]
    held = jnp.max(((near >= 0) & (near < SHOT_BLK)).astype(jnp.int32), axis=2)
    held_rank = ranks(held, 1)
    taken = (held_rank[:, None, :] == slot_ids[None, :, None]) & (held[:, None, :] > 0)
    held_ids = jnp.sum(jnp.where(taken, grid_ids[:, None, :], 0), axis=2)
    valid = jnp.sum(taken.astype(jnp.int32), axis=2)
    lows, highs = bounds(held_ids)
    lows, highs = lows * valid, highs * valid
    scales = step_size / jnp.maximum((highs - lows).astype(jnp.float32), 1.0)
    targets = mine[:, None] + jnp.arange(SHOT_BLK, dtype=jnp.int32)[None, :]
    slot_of = jnp.arange(owners, dtype=jnp.int32)[:, None] * capacity + held_rank
    slots = jnp.sum(
        jnp.where(targets[:, :, None, None] == grid_ids[None, None], slot_of[None, None], 0),
        axis=(2, 3),
    )
    own_lows, own_highs = bounds(own_ids)

    values, energy2, cuts = second(
        arrived, hits, thr, lows.reshape(-1), highs.reshape(-1), scales.reshape(-1),
        slots.reshape(-1), capacity, windows, receivers,
    )
    energies = over_receivers(energy2)
    residual = remainder(records, coefs, cuts, own_lows, own_highs, both)
    model = finish(values, energies, thr, both, receivers)
    return (model, residual.reshape(windows, 1, block, rcv))


def solution(mesh):
    return jax.shard_map(
        local,
        mesh=mesh,
        in_specs=(P(None, "shot", None, "rcv"), P(), P()),
        out_specs=(P("shot", None, None, "rcv"), P(None, "shot", None, "rcv")),
        check_vma=False,
    )
```

```python
import jax
import jax.numpy as jnp
import numpy as np
from jax import lax
from jax.experimental import pallas as pl
from jax.experimental.pallas import tpu as pltpu
from jax.sharding import PartitionSpec as P

SHOT_BLK = 4
momentum = 0.5
epsilon = 1e-06
step_size = 1.0 + momentum
VMEM_BYTES = 48 * 1024 * 1024


def cosine_table(length):
    rows = np.arange(length, dtype=np.float64)[:, None]
    cols = np.arange(length, dtype=np.float64)[None, :]
    table = np.cos(np.pi * (cols + 0.5) * rows / length) * np.sqrt(2.0 / length)
    return np.where(rows == 0, table * np.sqrt(0.5), table).astype(np.float32)


def split_bf16(values):
    high = values.astype(jnp.bfloat16)
    low = (values - high.astype(jnp.float32)).astype(jnp.bfloat16)
    return high, low


def full_vmem():
    return pl.BlockSpec(memory_space=pltpu.VMEM)


def full_smem():
    return pl.BlockSpec(memory_space=pltpu.SMEM)


def params(**kw):
    return pltpu.CompilerParams(vmem_limit_bytes=VMEM_BYTES, **kw)


def forward(both, values):
    block = values.shape[0]
    parts = lax.dot_general(
        values, both, (((0,), (0,)), ((), ())), preferred_element_type=jnp.float32
    )
    return parts[:, :block] + parts[:, block:]


def backward(both, coefficients):
    doubled = jnp.concatenate([coefficients, coefficients], axis=1)
    return lax.dot_general(
        both, doubled, (((1,), (1,)), ((), ())), preferred_element_type=jnp.float32
    )


def landed(ids, offsets):
    lag = ids - offsets
    return (lag >= 0) & (lag < SHOT_BLK)


def head(records, offsets, me, owners, capacity, both):
    windows, block, rcv = records.shape
    shots = offsets.shape[0]
    shot_dev = shots // owners
    chunk = 4
    chunks = windows // chunk
    f32, bf16 = jnp.float32, jnp.bfloat16

    def body(
        me_ref, off_hbm, rec_hbm, both_hbm, out_ref, energy_ref,
        off_ref, rec_ref, both_ref, sent_ref, table_ref, table_smem,
        small_sem, rec_sem, out_sem,
    ):
        get_off = pltpu.make_async_copy(off_hbm, off_ref, small_sem.at[0])
        get_both = pltpu.make_async_copy(both_hbm, both_ref, small_sem.at[1])
        get_rec = [
            pltpu.make_async_copy(
                rec_hbm.at[pl.ds(c * chunk, chunk)],
                rec_ref.at[pl.ds(c * chunk, chunk)],
                rec_sem.at[c],
            )
            for c in range(chunks)
        ]
        get_off.start()
        get_both.start()
        for copy in get_rec:
            copy.start()
        get_off.wait()

        ids = lax.broadcasted_iota(jnp.int32, (windows, shots), 0) * owners + me_ref[0]
        hits = jnp.where(landed(ids, off_ref[...]), 1.0, 0.0)
        cover = jnp.sum(hits, axis=1, keepdims=True)
        scale = 1.0 / jnp.maximum(cover, 1.0)

        shot = lax.broadcasted_iota(jnp.int32, (shots, owners), 0)
        first = lax.broadcasted_iota(jnp.int32, (shots, owners), 1) * shot_dev
        member = jnp.where((shot >= first) & (shot < first + shot_dev), 1.0, 0.0)
        counts = jnp.dot(hits.astype(bf16), member.astype(bf16), preferred_element_type=f32)
        present = jnp.where(counts > 0.5, 1.0, 0.0)
        after = lax.broadcasted_iota(jnp.int32, (windows, windows), 0)
        before = lax.broadcasted_iota(jnp.int32, (windows, windows), 1)
        lower = jnp.where(before < after, 1.0, 0.0)
        rank = jnp.dot(lower.astype(bf16), present.astype(bf16), preferred_element_type=f32)
        rank = rank.astype(jnp.int32)
        window = lax.broadcasted_iota(jnp.int32, (windows, owners), 0)
        for i in range(capacity):
            here = (rank == i) & (present > 0.5)
            table_ref[i : i + 1, :owners] = jnp.sum(
                jnp.where(here, window, 0), axis=0, keepdims=True
            )
        put_table = pltpu.make_async_copy(table_ref, table_smem, small_sem.at[2])
        put_table.start()

        get_both.wait()
        for c in range(chunks):
            get_rec[c].wait()
            for w in range(c * chunk, (c + 1) * chunk):
                spread = (rec_ref[w] * scale[w : w + 1, 0:1]).astype(bf16)
                coef = forward(both_ref[...], spread)
                sent_ref[w] = coef.astype(bf16)
                energy_ref[w : w + 1, :] = jnp.sum(coef * coef, axis=0, keepdims=True)

        put_table.wait()

        def send(h, i):
            return pltpu.make_async_copy(
                sent_ref.at[table_smem[i, h]],
                out_ref.at[h, pl.ds(i * rcv, rcv), :],
                out_sem.at[h * capacity + i],
            )

        for h in range(owners):
            for i in range(capacity):
                send(h, i).start()
        for h in range(owners):
            for i in range(capacity):
                send(h, i).wait()

    hbm = pl.BlockSpec(memory_space=pltpu.HBM)
    table_shape = (8, 128)
    return pl.pallas_call(
        body,
        in_specs=[full_smem(), hbm, hbm, hbm],
        out_specs=[pl.BlockSpec(memory_space=pl.ANY), full_vmem()],
        out_shape=[
            jax.ShapeDtypeStruct((owners, capacity * rcv, block), bf16),
            jax.ShapeDtypeStruct((windows, block), f32),
        ],
        scratch_shapes=[
            pltpu.VMEM((1, shots), jnp.int32),
            pltpu.VMEM((windows, block, rcv), f32),
            pltpu.VMEM((block, 2 * block), bf16),
            pltpu.VMEM((windows, rcv, block), bf16),
            pltpu.VMEM(table_shape, jnp.int32),
            pltpu.SMEM(table_shape, jnp.int32),
            pltpu.SemaphoreType.DMA((3,)),
            pltpu.SemaphoreType.DMA((chunks,)),
            pltpu.SemaphoreType.DMA((owners * capacity,)),
        ],
        compiler_params=params(),
        name="pack_coefficients",
    )(me[None], offsets[None, :], records, both)


def cutoffs(energies, hits, thresholds, receivers):
    rows = hits.shape[0]
    block = thresholds.shape[1]

    def body(*refs):
        hit_ref, thr_ref = refs[:2]
        out_ref, cuts_ref = refs[-2:]
        energy = refs[2][...]
        for ref in refs[3:-2]:
            energy = energy + ref[...]
        high, low = split_bf16(energy)
        sums = jnp.dot(hit_ref[...], high, preferred_element_type=jnp.float32) + jnp.dot(
            hit_ref[...], low, preferred_element_type=jnp.float32
        )
        cuts_ref[...] = thr_ref[...] * jnp.sqrt(sums / (SHOT_BLK * receivers) + epsilon)

        def widen(i, _):
            at = pl.multiple_of(i * 8, 8)
            out_ref[pl.ds(at, 8)] = jnp.broadcast_to(
                cuts_ref[pl.ds(at, 8), :][:, None, :], (8, 8, block)
            )
            return 0

        lax.fori_loop(0, rows // 8, widen, 0)

    return pl.pallas_call(
        body,
        in_specs=[full_vmem()] * (2 + len(energies)),
        out_specs=full_vmem(),
        out_shape=jax.ShapeDtypeStruct((rows, 8, block), jnp.float32),
        scratch_shapes=[pltpu.VMEM((rows, block), jnp.float32)],
        compiler_params=params(),
        name="first_cutoffs",
    )(hits, thresholds, *energies)


def clipped_sum(coef, cut_ref, low, high):
    def add(row, total):
        cut = cut_ref[row][None]
        return total + jnp.minimum(jnp.maximum(coef, -cut), cut)

    return lax.fori_loop(low, high, add, jnp.zeros_like(coef))


def second(arrived, cuts, lows, highs, scales, slots, capacity):
    owners, rows, block = arrived.shape
    rcv = rows // capacity
    tiles = rcv // 8
    shot_dev = slots.shape[0] // SHOT_BLK
    shots = cuts.shape[0] - shot_dev
    step = min(4, shot_dev)
    count = owners * capacity

    def body(
        low_ref, high_ref, scale_ref, slot_ref, in_ref, cut_ref, out_ref, energy_ref, diff_ref
    ):
        def block_of(slot):
            owner = slot // capacity
            start = pl.multiple_of((slot - owner * capacity) * rcv, rcv)
            values = in_ref[owner, pl.ds(start, rcv), :].astype(jnp.float32)
            return values.reshape(tiles, 8, block)

        @pl.when(pl.program_id(0) == 0)
        def _():
            def difference(slot, _):
                low, high = low_ref[slot], high_ref[slot]
                coef = block_of(slot)
                clipped = clipped_sum(coef, cut_ref, low, high)
                many = (high - low).astype(jnp.float32)
                diff_ref[slot] = coef - scale_ref[slot] * (many * coef - clipped)
                return 0

            lax.fori_loop(0, count, difference, 0)

        def one_shot(i, _):
            shot = pl.program_id(0) * step + i
            cut = cut_ref[shots + shot][None]
            energy = jnp.zeros((8, block), jnp.float32)
            for q in range(SHOT_BLK):
                slot = slot_ref[shot * SHOT_BLK + q]
                coef = block_of(slot)
                shrunk = coef - jnp.minimum(jnp.maximum(coef, -cut), cut)
                value = step_size * shrunk + diff_ref[slot]
                out_ref[i, q] = value.reshape(rcv, block)
                energy = energy + jnp.sum(value * value, axis=0)
            energy_ref[pl.ds(shot, 1), :] = jnp.sum(energy, axis=0, keepdims=True)
            return 0

        lax.fori_loop(0, step, one_shot, 0)

    return pl.pallas_call(
        body,
        grid=(shot_dev // step,),
        in_specs=[full_smem()] * 4 + [full_vmem()] * 2,
        out_specs=[
            pl.BlockSpec((step, SHOT_BLK, rcv, block), lambda i: (i, 0, 0, 0)),
            full_vmem(),
        ],
        out_shape=[
            jax.ShapeDtypeStruct((shot_dev, SHOT_BLK, rcv, block), jnp.float32),
            jax.ShapeDtypeStruct((shot_dev, block), jnp.float32),
        ],
        scratch_shapes=[pltpu.VMEM((count, tiles, 8, block), jnp.float32)],
        compiler_params=params(),
        cost_estimate=pl.CostEstimate(flops=1, bytes_accessed=12 << 20, transcendentals=0),
        name="second_coefficients",
    )(lows, highs, scales, slots, arrived, cuts)


def remainder(records, cuts, lows, highs, both):
    windows, block, rcv = records.shape
    tiles = rcv // 8
    step = 4

    def body(low_ref, high_ref, rec_ref, cut_ref, both_ref, out_ref):
        for w in range(step):
            window = pl.program_id(0) * step + w
            low, high = low_ref[window], high_ref[window]
            many = (high - low).astype(jnp.float32)
            scale = 1.0 / jnp.maximum(jnp.full((1, rcv), many, jnp.float32), 1.0)
            spread = (rec_ref[w] * scale).astype(jnp.bfloat16)
            coef = forward(both_ref[...], spread)
            clipped = clipped_sum(coef.reshape(tiles, 8, block), cut_ref, low, high)
            part, rest = split_bf16(many * coef - clipped.reshape(rcv, block))
            blended = backward(both_ref[...], part) + lax.dot_general(
                both_ref[:, :block], rest, (((1,), (1,)), ((), ())),
                preferred_element_type=jnp.float32,
            )
            out_ref[w] = rec_ref[w] - step_size * blended

    return pl.pallas_call(
        body,
        grid=(windows // step,),
        in_specs=[
            full_smem(),
            full_smem(),
            pl.BlockSpec((step, block, rcv), lambda i: (i, 0, 0)),
            full_vmem(),
            full_vmem(),
        ],
        out_specs=pl.BlockSpec((step, block, rcv), lambda i: (i, 0, 0)),
        out_shape=jax.ShapeDtypeStruct((windows, block, rcv), jnp.float32),
        compiler_params=params(),
        cost_estimate=pl.CostEstimate(flops=1, bytes_accessed=6 << 20, transcendentals=0),
        name="residual_of_records",
    )(lows, highs, records, cuts, both)


def finish(values, energies, thresholds, both, receivers):
    shot_dev, _, rcv, block = values.shape
    step = min(4, shot_dev)

    def body(*refs):
        in_ref, thr_ref, both_ref = refs[:3]
        out_ref = refs[-1]
        energy = refs[3][...]
        for ref in refs[4:-1]:
            energy = energy + ref[...]
        cuts = thr_ref[...] * jnp.sqrt(energy / (SHOT_BLK * receivers) + epsilon)
        for i in range(step):
            cut = cuts[i : i + 1, :]
            for q in range(SHOT_BLK):
                value = in_ref[i, q]
                shrunk = value - jnp.minimum(jnp.maximum(value, -cut), cut)
                out_ref[i, q] = backward(both_ref[...], shrunk.astype(jnp.bfloat16)).astype(
                    jnp.bfloat16
                )

    shape = (shot_dev // step, step, block)
    energies = [energy.reshape(shape) for energy in energies]
    return pl.pallas_call(
        body,
        grid=(shot_dev // step,),
        in_specs=[
            pl.BlockSpec((step, SHOT_BLK, rcv, block), lambda i: (i, 0, 0, 0)),
            full_vmem(),
            full_vmem(),
        ]
        + [pl.BlockSpec((None, step, block), lambda i: (i, 0, 0))] * len(energies),
        out_specs=pl.BlockSpec((step, SHOT_BLK, block, rcv), lambda i: (i, 0, 0, 0)),
        out_shape=jax.ShapeDtypeStruct((shot_dev, SHOT_BLK, block, rcv), jnp.bfloat16),
        compiler_params=params(),
        name="model_of_shots",
    )(values, thresholds, both, *energies)


def over_receivers(values):
    if lax.axis_size("rcv") == 2:
        return [values, lax.ppermute(values, "rcv", [(0, 1), (1, 0)])]
    return [lax.psum(values, "rcv")]


def rotate(values, stride, by, size):
    n = lax.axis_size("shot")
    pairs = []
    for i in range(n):
        place = (i // stride) % size
        pairs.append((i, i + ((place + by) % size - place) * stride))
    return lax.ppermute(values, "shot", pairs)


def local(record_data, offsets, thresholds):
    owners = lax.axis_size("shot")
    me = lax.axis_index("shot")
    windows, _, block, rcv = record_data.shape
    shots = offsets.shape[0]
    shot_dev = shots // owners
    pairs = shot_dev // 2
    pair_slots = min(pairs, owners // (SHOT_BLK + 1))
    capacity = (pairs + pair_slots - 1) // pair_slots
    receivers = rcv * lax.axis_size("rcv")
    near = min(4, owners)
    far = owners // near

    high, low = split_bf16(jnp.asarray(cosine_table(block).T))
    both = jnp.concatenate([high, low], axis=1)
    records = record_data.reshape(windows, block, rcv)
    thr = thresholds[None, :]
    window_ids = jnp.arange(windows, dtype=jnp.int32)

    packed, energy = head(records, offsets, me, owners, capacity, both)
    remote = [rotate(energy, near, j, far) for j in range(1, far)]
    packed, *remote = lax.optimization_barrier((packed, *remote))
    arrived = lax.all_to_all(packed, "shot", split_axis=0, concat_axis=0, tiled=True)

    energy = jnp.concatenate([energy, *remote])
    energy = jnp.concatenate([energy] + [rotate(energy, 1, j, near) for j in range(1, near)])
    energies = over_receivers(energy)
    back = jnp.arange(far, dtype=jnp.int32)[None, :]
    side = jnp.arange(near, dtype=jnp.int32)[:, None]
    origin = (me // near - back + far) % far * near + (me % near - side + near) % near
    energy_ids = (window_ids * owners + origin[:, :, None]).reshape(-1)

    index = jnp.arange(shots, dtype=jnp.int32)
    ahead = (offsets[None, :] < offsets[:, None]) | (
        (offsets[None, :] == offsets[:, None]) & (index[None, :] < index[:, None])
    )
    place = jnp.sum(ahead.astype(jnp.int32), axis=1)
    ordered = jnp.sum(jnp.where(place[None, :] == index[:, None], offsets[None, :], 0), axis=1)
    mine = lax.dynamic_slice(offsets, (me * shot_dev,), (shot_dev,))
    all_offsets = jnp.concatenate([ordered, mine])
    hits = landed(energy_ids[None, :], all_offsets[:, None]).astype(jnp.bfloat16)
    cuts = cutoffs(energies, hits, thr, receivers)

    def bounds(ids):
        below = jnp.sum((offsets < ids[..., None] - (SHOT_BLK - 1)).astype(jnp.int32), axis=-1)
        upto = jnp.sum((offsets <= ids[..., None]).astype(jnp.int32), axis=-1)
        return below, upto

    residual = remainder(records, cuts, *bounds(window_ids * owners + me), both)

    grid_ids = window_ids[None, :] * owners + jnp.arange(owners, dtype=jnp.int32)[:, None]
    slot_ids = jnp.arange(capacity, dtype=jnp.int32)
    held = jnp.max(landed(grid_ids[:, :, None], mine).astype(jnp.int32), axis=2)
    before = (window_ids[:, None] < window_ids[None, :]).astype(jnp.int32)
    held_rank = jnp.sum(held[:, :, None] * before, axis=1)
    taken = (held_rank[:, None, :] == slot_ids[None, :, None]) & (held[:, None, :] > 0)
    held_ids = jnp.sum(jnp.where(taken, grid_ids[:, None, :], 0), axis=2)
    valid = jnp.sum(taken.astype(jnp.int32), axis=2)
    lows, highs = bounds(held_ids)
    lows, highs = lows * valid, highs * valid
    scales = step_size / jnp.maximum((highs - lows).astype(jnp.float32), 1.0)
    targets = mine[:, None] + jnp.arange(SHOT_BLK, dtype=jnp.int32)[None, :]
    slot_of = jnp.arange(owners, dtype=jnp.int32)[:, None] * capacity + held_rank
    slots = jnp.sum(
        jnp.where(targets[:, :, None, None] == grid_ids[None, None], slot_of[None, None], 0),
        axis=(2, 3),
    )

    values, energy2 = second(
        arrived, cuts, lows.reshape(-1), highs.reshape(-1), scales.reshape(-1),
        slots.reshape(-1), capacity,
    )
    model = finish(values, over_receivers(energy2), thr, both, receivers)
    return (model, residual.reshape(windows, 1, block, rcv))


def solution(mesh):
    return jax.shard_map(
        local,
        mesh=mesh,
        in_specs=(P(None, "shot", None, "rcv"), P(), P()),
        out_specs=(P("shot", None, None, "rcv"), P(None, "shot", None, "rcv")),
        check_vma=False,
    )
```

```python
import jax
import jax.numpy as jnp
import numpy as np
from jax import lax
from jax.experimental import pallas as pl
from jax.experimental.pallas import tpu as pltpu
from jax.sharding import PartitionSpec as P

SHOT_BLK = 4
momentum = 0.5
epsilon = 1e-06
step_size = 1.0 + momentum
VMEM_BYTES = 16 * 1024 * 1024
HEAD_VMEM_BYTES = 60 * 1024 * 1024


def cosine_table(length):
    rows = np.arange(length, dtype=np.float64)[:, None]
    cols = np.arange(length, dtype=np.float64)[None, :]
    table = np.cos(np.pi * (cols + 0.5) * rows / length) * np.sqrt(2.0 / length)
    return np.where(rows == 0, table * np.sqrt(0.5), table).astype(np.float32)


def split_bf16(values):
    high = values.astype(jnp.bfloat16)
    low = (values - high.astype(jnp.float32)).astype(jnp.bfloat16)
    return high, low


def full_vmem():
    return pl.BlockSpec(memory_space=pltpu.VMEM)


def full_smem():
    return pl.BlockSpec(memory_space=pltpu.SMEM)


def params(vmem=VMEM_BYTES):
    return pltpu.CompilerParams(vmem_limit_bytes=vmem)


def forward(both, values):
    block = values.shape[0]
    parts = lax.dot_general(
        values, both, (((0,), (0,)), ((), ())), preferred_element_type=jnp.float32
    )
    return parts[:, :block] + parts[:, block:]


def backward(both, coefficients):
    doubled = jnp.concatenate([coefficients, coefficients], axis=1)
    return lax.dot_general(
        both, doubled, (((1,), (1,)), ((), ())), preferred_element_type=jnp.float32
    )


def landed(ids, offsets):
    lag = ids - offsets
    return (lag >= 0) & (lag < SHOT_BLK)


def head(records, offsets, me, owners, capacity, both):
    windows, block, rcv = records.shape
    shots = offsets.shape[0]
    shot_dev = shots // owners
    chunk = 4
    chunks = windows // chunk
    f32, bf16 = jnp.float32, jnp.bfloat16

    def body(
        me_ref, off_hbm, rec_hbm, both_hbm, out_ref, energy_ref,
        off_ref, rec_ref, both_ref, sent_ref, table_ref, table_smem,
        small_sem, rec_sem, out_sem,
    ):
        get_off = pltpu.make_async_copy(off_hbm, off_ref, small_sem.at[0])
        get_both = pltpu.make_async_copy(both_hbm, both_ref, small_sem.at[1])
        get_rec = [
            pltpu.make_async_copy(
                rec_hbm.at[pl.ds(c * chunk, chunk)],
                rec_ref.at[pl.ds(c * chunk, chunk)],
                rec_sem.at[c],
            )
            for c in range(chunks)
        ]
        get_off.start()
        get_both.start()
        for copy in get_rec:
            copy.start()
        get_off.wait()

        ids = lax.broadcasted_iota(jnp.int32, (windows, shots), 0) * owners + me_ref[0]
        hits = jnp.where(landed(ids, off_ref[...]), 1.0, 0.0)
        cover = jnp.sum(hits, axis=1, keepdims=True)
        scale = 1.0 / jnp.maximum(cover, 1.0)

        shot = lax.broadcasted_iota(jnp.int32, (shots, owners), 0)
        first = lax.broadcasted_iota(jnp.int32, (shots, owners), 1) * shot_dev
        member = jnp.where((shot >= first) & (shot < first + shot_dev), 1.0, 0.0)
        counts = jnp.dot(hits.astype(bf16), member.astype(bf16), preferred_element_type=f32)
        present = jnp.where(counts > 0.5, 1.0, 0.0)
        after = lax.broadcasted_iota(jnp.int32, (windows, windows), 0)
        before = lax.broadcasted_iota(jnp.int32, (windows, windows), 1)
        lower = jnp.where(before < after, 1.0, 0.0)
        rank = jnp.dot(lower.astype(bf16), present.astype(bf16), preferred_element_type=f32)
        rank = rank.astype(jnp.int32)
        window = lax.broadcasted_iota(jnp.int32, (windows, owners), 0)
        for i in range(capacity):
            here = (rank == i) & (present > 0.5)
            table_ref[i : i + 1, :owners] = jnp.sum(
                jnp.where(here, window, 0), axis=0, keepdims=True
            )
        put_table = pltpu.make_async_copy(table_ref, table_smem, small_sem.at[2])
        put_table.start()

        get_both.wait()
        for c in range(chunks):
            get_rec[c].wait()
            for w in range(c * chunk, (c + 1) * chunk):
                spread = (rec_ref[w] * scale[w : w + 1, 0:1]).astype(bf16)
                coef = forward(both_ref[...], spread)
                sent_ref[w] = coef.astype(bf16)
                energy_ref[w : w + 1, :] = jnp.sum(coef * coef, axis=0, keepdims=True)

        put_table.wait()

        def send(h, i):
            return pltpu.make_async_copy(
                sent_ref.at[table_smem[i, h]],
                out_ref.at[h, pl.ds(i * rcv, rcv), :],
                out_sem.at[h * capacity + i],
            )

        for h in range(owners):
            for i in range(capacity):
                send(h, i).start()
        for h in range(owners):
            for i in range(capacity):
                send(h, i).wait()

    hbm = pl.BlockSpec(memory_space=pltpu.HBM)
    table_shape = (8, 128)
    return pl.pallas_call(
        body,
        in_specs=[full_smem(), hbm, hbm, hbm],
        out_specs=[pl.BlockSpec(memory_space=pl.ANY), full_vmem()],
        out_shape=[
            jax.ShapeDtypeStruct((owners, capacity * rcv, block), bf16),
            jax.ShapeDtypeStruct((windows, block), f32),
        ],
        scratch_shapes=[
            pltpu.VMEM((1, shots), jnp.int32),
            pltpu.VMEM((windows, block, rcv), f32),
            pltpu.VMEM((block, 2 * block), bf16),
            pltpu.VMEM((windows, rcv, block), bf16),
            pltpu.VMEM(table_shape, jnp.int32),
            pltpu.SMEM(table_shape, jnp.int32),
            pltpu.SemaphoreType.DMA((3,)),
            pltpu.SemaphoreType.DMA((chunks,)),
            pltpu.SemaphoreType.DMA((owners * capacity,)),
        ],
        compiler_params=params(HEAD_VMEM_BYTES),
        name="pack_coefficients",
    )(me[None], offsets[None, :], records, both)


def cutoffs(energies, hits, thresholds, receivers):
    rows = hits.shape[0]
    block = thresholds.shape[1]

    def body(*refs):
        hit_ref, thr_ref = refs[:2]
        out_ref, cuts_ref = refs[-2:]
        energy = refs[2][...]
        for ref in refs[3:-2]:
            energy = energy + ref[...]
        high, low = split_bf16(energy)
        sums = jnp.dot(hit_ref[...], high, preferred_element_type=jnp.float32) + jnp.dot(
            hit_ref[...], low, preferred_element_type=jnp.float32
        )
        cuts_ref[...] = thr_ref[...] * jnp.sqrt(sums / (SHOT_BLK * receivers) + epsilon)

        def widen(i, _):
            at = pl.multiple_of(i * 8, 8)
            out_ref[pl.ds(at, 8)] = jnp.broadcast_to(
                cuts_ref[pl.ds(at, 8), :][:, None, :], (8, 8, block)
            )
            return 0

        lax.fori_loop(0, rows // 8, widen, 0)

    return pl.pallas_call(
        body,
        in_specs=[full_vmem()] * (2 + len(energies)),
        out_specs=full_vmem(),
        out_shape=jax.ShapeDtypeStruct((rows, 8, block), jnp.float32),
        scratch_shapes=[pltpu.VMEM((rows, block), jnp.float32)],
        compiler_params=params(),
        name="first_cutoffs",
    )(hits, thresholds, *energies)


def clipped_sum(coef, cut_ref, low, high):
    def add(row, total):
        cut = cut_ref[row][None]
        return total + jnp.minimum(jnp.maximum(coef, -cut), cut)

    return lax.fori_loop(low, high, add, jnp.zeros_like(coef))


def second(arrived, cuts, lows, highs, scales, slots, capacity):
    owners, rows, block = arrived.shape
    rcv = rows // capacity
    tiles = rcv // 8
    shot_dev = slots.shape[0] // SHOT_BLK
    shots = cuts.shape[0] - shot_dev
    step = min(4, shot_dev)
    count = owners * capacity

    def body(
        low_ref, high_ref, scale_ref, slot_ref, in_ref, cut_ref, out_ref, energy_ref, diff_ref
    ):
        def block_of(slot):
            owner = slot // capacity
            start = pl.multiple_of((slot - owner * capacity) * rcv, rcv)
            values = in_ref[owner, pl.ds(start, rcv), :].astype(jnp.float32)
            return values.reshape(tiles, 8, block)

        @pl.when(pl.program_id(0) == 0)
        def _():
            def difference(slot, _):
                low, high = low_ref[slot], high_ref[slot]
                coef = block_of(slot)
                clipped = clipped_sum(coef, cut_ref, low, high)
                many = (high - low).astype(jnp.float32)
                diff_ref[slot] = coef - scale_ref[slot] * (many * coef - clipped)
                return 0

            lax.fori_loop(0, count, difference, 0)

        def one_shot(i, _):
            shot = pl.program_id(0) * step + i
            cut = cut_ref[shots + shot][None]
            energy = jnp.zeros((8, block), jnp.float32)
            for q in range(SHOT_BLK):
                slot = slot_ref[shot * SHOT_BLK + q]
                coef = block_of(slot)
                shrunk = coef - jnp.minimum(jnp.maximum(coef, -cut), cut)
                value = step_size * shrunk + diff_ref[slot]
                out_ref[i, q] = value.reshape(rcv, block)
                energy = energy + jnp.sum(value * value, axis=0)
            energy_ref[pl.ds(shot, 1), :] = jnp.sum(energy, axis=0, keepdims=True)
            return 0

        lax.fori_loop(0, step, one_shot, 0)

    return pl.pallas_call(
        body,
        grid=(shot_dev // step,),
        in_specs=[full_smem()] * 4 + [full_vmem()] * 2,
        out_specs=[
            pl.BlockSpec((step, SHOT_BLK, rcv, block), lambda i: (i, 0, 0, 0)),
            full_vmem(),
        ],
        out_shape=[
            jax.ShapeDtypeStruct((shot_dev, SHOT_BLK, rcv, block), jnp.float32),
            jax.ShapeDtypeStruct((shot_dev, block), jnp.float32),
        ],
        scratch_shapes=[pltpu.VMEM((count, tiles, 8, block), jnp.float32)],
        compiler_params=params(),
        cost_estimate=pl.CostEstimate(flops=1, bytes_accessed=12 << 20, transcendentals=0),
        name="second_coefficients",
    )(lows, highs, scales, slots, arrived, cuts)


def remainder(records, cuts, lows, highs, both):
    windows, block, rcv = records.shape
    tiles = rcv // 8
    step = 4

    def body(low_ref, high_ref, rec_ref, cut_ref, both_ref, out_ref):
        for w in range(step):
            window = pl.program_id(0) * step + w
            low, high = low_ref[window], high_ref[window]
            many = (high - low).astype(jnp.float32)
            scale = 1.0 / jnp.maximum(jnp.full((1, rcv), many, jnp.float32), 1.0)
            spread = (rec_ref[w] * scale).astype(jnp.bfloat16)
            coef = forward(both_ref[...], spread)
            clipped = clipped_sum(coef.reshape(tiles, 8, block), cut_ref, low, high)
            part, rest = split_bf16(many * coef - clipped.reshape(rcv, block))
            blended = backward(both_ref[...], part) + lax.dot_general(
                both_ref[:, :block], rest, (((1,), (1,)), ((), ())),
                preferred_element_type=jnp.float32,
            )
            out_ref[w] = rec_ref[w] - step_size * blended

    return pl.pallas_call(
        body,
        grid=(windows // step,),
        in_specs=[
            full_smem(),
            full_smem(),
            pl.BlockSpec((step, block, rcv), lambda i: (i, 0, 0)),
            full_vmem(),
            full_vmem(),
        ],
        out_specs=pl.BlockSpec((step, block, rcv), lambda i: (i, 0, 0)),
        out_shape=jax.ShapeDtypeStruct((windows, block, rcv), jnp.float32),
        compiler_params=params(),
        cost_estimate=pl.CostEstimate(flops=1, bytes_accessed=6 << 20, transcendentals=0),
        name="residual_of_records",
    )(lows, highs, records, cuts, both)


def finish(values, energies, thresholds, both, receivers):
    shot_dev, _, rcv, block = values.shape
    step = min(4, shot_dev)

    def body(*refs):
        in_ref, thr_ref, both_ref = refs[:3]
        out_ref = refs[-1]
        energy = refs[3][...]
        for ref in refs[4:-1]:
            energy = energy + ref[...]
        cuts = thr_ref[...] * jnp.sqrt(energy / (SHOT_BLK * receivers) + epsilon)
        for i in range(step):
            cut = cuts[i : i + 1, :]
            for q in range(SHOT_BLK):
                value = in_ref[i, q]
                shrunk = value - jnp.minimum(jnp.maximum(value, -cut), cut)
                out_ref[i, q] = backward(both_ref[...], shrunk.astype(jnp.bfloat16)).astype(
                    jnp.bfloat16
                )

    shape = (shot_dev // step, step, block)
    energies = [energy.reshape(shape) for energy in energies]
    return pl.pallas_call(
        body,
        grid=(shot_dev // step,),
        in_specs=[
            pl.BlockSpec((step, SHOT_BLK, rcv, block), lambda i: (i, 0, 0, 0)),
            full_vmem(),
            full_vmem(),
        ]
        + [pl.BlockSpec((None, step, block), lambda i: (i, 0, 0))] * len(energies),
        out_specs=pl.BlockSpec((step, SHOT_BLK, block, rcv), lambda i: (i, 0, 0, 0)),
        out_shape=jax.ShapeDtypeStruct((shot_dev, SHOT_BLK, block, rcv), jnp.bfloat16),
        compiler_params=params(),
        name="model_of_shots",
    )(values, thresholds, both, *energies)


def over_receivers(values):
    if lax.axis_size("rcv") == 2:
        return [values, lax.ppermute(values, "rcv", [(0, 1), (1, 0)])]
    return [lax.psum(values, "rcv")]


def rotate(values, stride, by, size):
    n = lax.axis_size("shot")
    pairs = []
    for i in range(n):
        place = (i // stride) % size
        pairs.append((i, i + ((place + by) % size - place) * stride))
    return lax.ppermute(values, "shot", pairs)


def local(record_data, offsets, thresholds):
    owners = lax.axis_size("shot")
    me = lax.axis_index("shot")
    windows, _, block, rcv = record_data.shape
    shots = offsets.shape[0]
    shot_dev = shots // owners
    pairs = shot_dev // 2
    pair_slots = min(pairs, owners // (SHOT_BLK + 1))
    capacity = (pairs + pair_slots - 1) // pair_slots
    receivers = rcv * lax.axis_size("rcv")
    near = min(4, owners)
    far = owners // near

    high, low = split_bf16(jnp.asarray(cosine_table(block).T))
    both = jnp.concatenate([high, low], axis=1)
    records = record_data.reshape(windows, block, rcv)
    thr = thresholds[None, :]
    window_ids = jnp.arange(windows, dtype=jnp.int32)

    packed, energy = head(records, offsets, me, owners, capacity, both)
    remote = [rotate(energy, near, j, far) for j in range(1, far)]
    packed, *remote = lax.optimization_barrier((packed, *remote))
    arrived = lax.all_to_all(packed, "shot", split_axis=0, concat_axis=0, tiled=True)

    energy = jnp.concatenate([energy, *remote])
    energy = jnp.concatenate([energy] + [rotate(energy, 1, j, near) for j in range(1, near)])
    energies = over_receivers(energy)
    back = jnp.arange(far, dtype=jnp.int32)[None, :]
    side = jnp.arange(near, dtype=jnp.int32)[:, None]
    origin = (me // near - back + far) % far * near + (me % near - side + near) % near
    energy_ids = (window_ids * owners + origin[:, :, None]).reshape(-1)

    index = jnp.arange(shots, dtype=jnp.int32)
    ahead = (offsets[None, :] < offsets[:, None]) | (
        (offsets[None, :] == offsets[:, None]) & (index[None, :] < index[:, None])
    )
    place = jnp.sum(ahead.astype(jnp.int32), axis=1)
    ordered = jnp.sum(jnp.where(place[None, :] == index[:, None], offsets[None, :], 0), axis=1)
    mine = lax.dynamic_slice(offsets, (me * shot_dev,), (shot_dev,))
    all_offsets = jnp.concatenate([ordered, mine])
    hits = landed(energy_ids[None, :], all_offsets[:, None]).astype(jnp.bfloat16)
    cuts = cutoffs(energies, hits, thr, receivers)

    def bounds(ids):
        below = jnp.sum((offsets < ids[..., None] - (SHOT_BLK - 1)).astype(jnp.int32), axis=-1)
        upto = jnp.sum((offsets <= ids[..., None]).astype(jnp.int32), axis=-1)
        return below, upto

    residual = remainder(records, cuts, *bounds(window_ids * owners + me), both)
    cuts, residual = lax.optimization_barrier((cuts, residual))

    grid_ids = window_ids[None, :] * owners + jnp.arange(owners, dtype=jnp.int32)[:, None]
    slot_ids = jnp.arange(capacity, dtype=jnp.int32)
    held = jnp.max(landed(grid_ids[:, :, None], mine).astype(jnp.int32), axis=2)
    before = (window_ids[:, None] < window_ids[None, :]).astype(jnp.int32)
    held_rank = jnp.sum(held[:, :, None] * before, axis=1)
    taken = (held_rank[:, None, :] == slot_ids[None, :, None]) & (held[:, None, :] > 0)
    held_ids = jnp.sum(jnp.where(taken, grid_ids[:, None, :], 0), axis=2)
    valid = jnp.sum(taken.astype(jnp.int32), axis=2)
    lows, highs = bounds(held_ids)
    lows, highs = lows * valid, highs * valid
    scales = step_size / jnp.maximum((highs - lows).astype(jnp.float32), 1.0)
    targets = mine[:, None] + jnp.arange(SHOT_BLK, dtype=jnp.int32)[None, :]
    slot_of = jnp.arange(owners, dtype=jnp.int32)[:, None] * capacity + held_rank
    slots = jnp.sum(
        jnp.where(targets[:, :, None, None] == grid_ids[None, None], slot_of[None, None], 0),
        axis=(2, 3),
    )

    values, energy2 = second(
        arrived, cuts, lows.reshape(-1), highs.reshape(-1), scales.reshape(-1),
        slots.reshape(-1), capacity,
    )
    model = finish(values, over_receivers(energy2), thr, both, receivers)
    return (model, residual.reshape(windows, 1, block, rcv))


def solution(mesh):
    return jax.shard_map(
        local,
        mesh=mesh,
        in_specs=(P(None, "shot", None, "rcv"), P(), P()),
        out_specs=(P("shot", None, None, "rcv"), P(None, "shot", None, "rcv")),
        check_vma=False,
    )
```

```python
import jax
import jax.numpy as jnp
import numpy as np
from jax import lax
from jax.experimental import pallas as pl
from jax.experimental.pallas import tpu as pltpu
from jax.sharding import PartitionSpec as P

SHOT_BLK = 4
momentum = 0.5
epsilon = 1e-06
step_size = 1.0 + momentum
VMEM_BYTES = 16 * 1024 * 1024
HEAD_VMEM_BYTES = 60 * 1024 * 1024


def cosine_table(length):
    rows = np.arange(length, dtype=np.float64)[:, None]
    cols = np.arange(length, dtype=np.float64)[None, :]
    table = np.cos(np.pi * (cols + 0.5) * rows / length) * np.sqrt(2.0 / length)
    return np.where(rows == 0, table * np.sqrt(0.5), table).astype(np.float32)


def split_bf16(values):
    high = values.astype(jnp.bfloat16)
    low = (values - high.astype(jnp.float32)).astype(jnp.bfloat16)
    return high, low


def full_vmem():
    return pl.BlockSpec(memory_space=pltpu.VMEM)


def full_smem():
    return pl.BlockSpec(memory_space=pltpu.SMEM)


def params(vmem=VMEM_BYTES):
    return pltpu.CompilerParams(vmem_limit_bytes=vmem)


def forward(both, values):
    block = values.shape[0]
    parts = lax.dot_general(
        values, both, (((0,), (0,)), ((), ())), preferred_element_type=jnp.float32
    )
    return parts[:, :block] + parts[:, block:]


def backward(both, coefficients):
    doubled = jnp.concatenate([coefficients, coefficients], axis=1)
    return lax.dot_general(
        both, doubled, (((1,), (1,)), ((), ())), preferred_element_type=jnp.float32
    )


def landed(ids, offsets):
    lag = ids - offsets
    return (lag >= 0) & (lag < SHOT_BLK)


def owned(records, offsets, me, owners, capacity, both):
    windows, block, rcv = records.shape
    shots = offsets.shape[0]
    shot_dev = shots // owners
    chunk = 4
    chunks = windows // chunk
    f32, bf16 = jnp.float32, jnp.bfloat16

    def body(
        me_ref, off_hbm, rec_hbm, both_hbm, sent_ref, energy_ref, table_ref,
        off_ref, rec_ref, both_ref, small_sem, rec_sem,
    ):
        get_off = pltpu.make_async_copy(off_hbm, off_ref, small_sem.at[0])
        get_both = pltpu.make_async_copy(both_hbm, both_ref, small_sem.at[1])
        get_rec = [
            pltpu.make_async_copy(
                rec_hbm.at[pl.ds(c * chunk, chunk)],
                rec_ref.at[pl.ds(c * chunk, chunk)],
                rec_sem.at[c],
            )
            for c in range(chunks)
        ]
        get_off.start()
        get_both.start()
        for copy in get_rec:
            copy.start()
        get_off.wait()

        ids = lax.broadcasted_iota(jnp.int32, (windows, shots), 0) * owners + me_ref[0]
        hits = jnp.where(landed(ids, off_ref[...]), 1.0, 0.0)
        cover = jnp.sum(hits, axis=1, keepdims=True)
        scale = 1.0 / jnp.maximum(cover, 1.0)

        shot = lax.broadcasted_iota(jnp.int32, (shots, owners), 0)
        first = lax.broadcasted_iota(jnp.int32, (shots, owners), 1) * shot_dev
        member = jnp.where((shot >= first) & (shot < first + shot_dev), 1.0, 0.0)
        counts = jnp.dot(hits.astype(bf16), member.astype(bf16), preferred_element_type=f32)
        present = jnp.where(counts > 0.5, 1.0, 0.0)
        after = lax.broadcasted_iota(jnp.int32, (windows, windows), 0)
        before = lax.broadcasted_iota(jnp.int32, (windows, windows), 1)
        lower = jnp.where(before < after, 1.0, 0.0)
        rank = jnp.dot(lower.astype(bf16), present.astype(bf16), preferred_element_type=f32)
        rank = rank.astype(jnp.int32)
        window = lax.broadcasted_iota(jnp.int32, (windows, owners), 0)
        for i in range(capacity):
            here = (rank == i) & (present > 0.5)
            table_ref[i : i + 1, :owners] = jnp.sum(
                jnp.where(here, window, 0), axis=0, keepdims=True
            )

        get_both.wait()
        for c in range(chunks):
            get_rec[c].wait()
            for w in range(c * chunk, (c + 1) * chunk):
                spread = (rec_ref[w] * scale[w : w + 1, 0:1]).astype(bf16)
                coef = forward(both_ref[...], spread)
                sent_ref[w] = coef.astype(bf16)
                energy_ref[w : w + 1, :] = jnp.sum(coef * coef, axis=0, keepdims=True)

    hbm = pl.BlockSpec(memory_space=pltpu.HBM)
    return pl.pallas_call(
        body,
        in_specs=[full_smem(), hbm, hbm, hbm],
        out_specs=[full_vmem()] * 3,
        out_shape=[
            jax.ShapeDtypeStruct((windows, rcv, block), bf16),
            jax.ShapeDtypeStruct((windows, block), f32),
            jax.ShapeDtypeStruct((8, 128), jnp.int32),
        ],
        scratch_shapes=[
            pltpu.VMEM((1, shots), jnp.int32),
            pltpu.VMEM((windows, block, rcv), f32),
            pltpu.VMEM((block, 2 * block), bf16),
            pltpu.SemaphoreType.DMA((2,)),
            pltpu.SemaphoreType.DMA((chunks,)),
        ],
        compiler_params=params(HEAD_VMEM_BYTES),
        name="owned_coefficients",
    )(me[None], offsets[None, :], records, both)


def pack(sent, table, energies, owners, capacity):
    windows, rcv, block = sent.shape
    rows = capacity * rcv + windows

    def body(table_ref, sent_ref, *refs):
        out_ref, energy_ref, block_sem, energy_sem = refs[-4:]
        energy = refs[0][...]
        for ref in refs[1:-4]:
            energy = energy + ref[...]
        energy_ref[...] = energy.astype(jnp.bfloat16)

        def blocks(h, i):
            return pltpu.make_async_copy(
                sent_ref.at[table_ref[i, h]],
                out_ref.at[h, pl.ds(i * rcv, rcv), :],
                block_sem.at[h * capacity + i],
            )

        def rest(h):
            return pltpu.make_async_copy(
                energy_ref, out_ref.at[h, pl.ds(capacity * rcv, windows), :], energy_sem.at[h]
            )

        for h in range(owners):
            for i in range(capacity):
                blocks(h, i).start()
            rest(h).start()
        for h in range(owners):
            for i in range(capacity):
                blocks(h, i).wait()
            rest(h).wait()

    return pl.pallas_call(
        body,
        in_specs=[full_smem(), pl.BlockSpec(memory_space=pl.ANY)] + [full_vmem()] * len(energies),
        out_specs=pl.BlockSpec(memory_space=pl.ANY),
        out_shape=jax.ShapeDtypeStruct((owners, rows, block), jnp.bfloat16),
        scratch_shapes=[
            pltpu.VMEM((windows, block), jnp.bfloat16),
            pltpu.SemaphoreType.DMA((owners * capacity,)),
            pltpu.SemaphoreType.DMA((owners,)),
        ],
        compiler_params=params(),
        name="pack_blocks",
    )(table, sent, *energies)


def clipped_sum(coef, cut_ref, low, high, none):
    size = jnp.abs(coef)
    unroll = 2

    def add(j, total):
        for u in range(unroll):
            row = low + j * unroll + u
            if u:
                row = jnp.where(row < high, row, none)
            total = total + jnp.minimum(size, cut_ref[row][None])
        return total

    trips = lax.div(high - low + unroll - 1, unroll)
    total = lax.fori_loop(0, trips, add, jnp.zeros_like(coef))
    return jnp.where(coef < 0, -total, total)


def second(arrived, hits, thresholds, lows, highs, scales, slots, capacity, windows, receivers):
    owners, rows, block = arrived.shape
    rcv = (rows - windows) // capacity
    tiles = rcv // 8
    shot_dev = slots.shape[0] // SHOT_BLK
    count = owners * capacity
    cut_rows = hits.shape[0]
    shots = cut_rows - shot_dev

    def body(
        low_ref, high_ref, scale_ref, slot_ref, in_ref, hit_ref, thr_ref,
        out_ref, energy_ref, wide_ref, cuts_ref, diff_ref,
    ):
        energy = in_ref[:, capacity * rcv :, :].reshape(owners * windows, block)
        sums = jnp.dot(hit_ref[...], energy, preferred_element_type=jnp.float32)
        cuts_ref[...] = thr_ref[...] * jnp.sqrt(sums / (SHOT_BLK * receivers) + epsilon)

        def widen(i, _):
            at = pl.multiple_of(i * 8, 8)
            wide_ref[pl.ds(at, 8)] = jnp.broadcast_to(
                cuts_ref[pl.ds(at, 8), :][:, None, :], (8, 8, block)
            )
            return 0

        lax.fori_loop(0, cut_rows // 8, widen, 0, unroll=2)
        wide_ref[cut_rows] = jnp.zeros((8, block), jnp.float32)

        def block_of(slot):
            owner = slot // capacity
            start = pl.multiple_of((slot - owner * capacity) * rcv, rcv)
            values = in_ref[owner, pl.ds(start, rcv), :].astype(jnp.float32)
            return values.reshape(tiles, 8, block)

        def difference(slot, _):
            low, high = low_ref[slot], high_ref[slot]

            @pl.when(high > low)
            def _():
                coef = block_of(slot)
                clipped = clipped_sum(coef, wide_ref, low, high, cut_rows)
                scale = scale_ref[slot]
                kept = 1.0 - scale * (high - low).astype(jnp.float32)
                diff_ref[slot] = kept * coef + scale * clipped

            return 0

        lax.fori_loop(0, count, difference, 0)

        def one_shot(shot, _):
            cut = wide_ref[shots + shot][None]
            energy = jnp.zeros((8, block), jnp.float32)
            for q in range(SHOT_BLK):
                slot = slot_ref[shot * SHOT_BLK + q]
                coef = block_of(slot)
                shrunk = coef - jnp.minimum(jnp.maximum(coef, -cut), cut)
                value = step_size * shrunk + diff_ref[slot]
                out_ref[shot, q] = value.reshape(rcv, block)
                energy = energy + jnp.sum(value * value, axis=0)
            energy_ref[pl.ds(shot, 1), :] = jnp.sum(energy, axis=0, keepdims=True)
            return 0

        lax.fori_loop(0, shot_dev, one_shot, 0)

    return pl.pallas_call(
        body,
        in_specs=[full_smem()] * 4 + [full_vmem()] * 3,
        out_specs=[full_vmem()] * 3,
        out_shape=[
            jax.ShapeDtypeStruct((shot_dev, SHOT_BLK, rcv, block), jnp.float32),
            jax.ShapeDtypeStruct((shot_dev, block), jnp.float32),
            jax.ShapeDtypeStruct((cut_rows + 1, 8, block), jnp.float32),
        ],
        scratch_shapes=[
            pltpu.VMEM((cut_rows, block), jnp.float32),
            pltpu.VMEM((count, tiles, 8, block), jnp.float32),
        ],
        compiler_params=params(),
        cost_estimate=pl.CostEstimate(flops=1, bytes_accessed=12 << 20, transcendentals=0),
        name="second_coefficients",
    )(lows, highs, scales, slots, arrived, hits, thresholds)


def again(records, lows, highs, both):
    windows, block, rcv = records.shape

    def body(low_ref, high_ref, rec_ref, both_ref, out_ref):
        for w in range(windows):
            many = jnp.full((1, rcv), (high_ref[w] - low_ref[w]).astype(jnp.float32))
            spread = (rec_ref[w] * (1.0 / jnp.maximum(many, 1.0))).astype(jnp.bfloat16)
            out_ref[w] = forward(both_ref[...], spread)

    return pl.pallas_call(
        body,
        in_specs=[full_smem()] * 2 + [full_vmem()] * 2,
        out_specs=full_vmem(),
        out_shape=jax.ShapeDtypeStruct((windows, rcv, block), jnp.float32),
        compiler_params=params(),
        cost_estimate=pl.CostEstimate(flops=1, bytes_accessed=6 << 20, transcendentals=0),
        name="owned_again",
    )(lows, highs, records, both)


def remainder(records, coefs, cuts, lows, highs, both):
    windows, block, rcv = records.shape
    tiles = rcv // 8
    none = cuts.shape[0] - 1
    group = 4

    def body(
        low_ref, high_ref, rec_ref, coef_ref, cut_ref, both_ref, out_hbm, sum_ref, out_ref, sem
    ):
        copies = []
        for at in range(0, windows, group):
            for w in range(at, at + group):
                low, high = low_ref[w], high_ref[w]
                coef = coef_ref[w].reshape(tiles, 8, block)
                clipped = clipped_sum(coef, cut_ref, low, high, none)
                shrunk = (high - low).astype(jnp.float32) * coef - clipped
                sum_ref[pl.ds((w - at) * rcv, rcv), :] = shrunk.reshape(rcv, block).astype(
                    jnp.bfloat16
                )
            blended = backward(both_ref[...], sum_ref[...])
            for w in range(at, at + group):
                part = blended[:, (w - at) * rcv : (w - at + 1) * rcv]
                out_ref[w] = rec_ref[w] - step_size * part
            copy = pltpu.make_async_copy(
                out_ref.at[pl.ds(at, group)], out_hbm.at[pl.ds(at, group)], sem.at[at // group]
            )
            copy.start()
            copies.append(copy)
        for copy in copies:
            copy.wait()

    return pl.pallas_call(
        body,
        in_specs=[full_smem()] * 2 + [full_vmem()] * 4,
        out_specs=pl.BlockSpec(memory_space=pl.ANY),
        out_shape=jax.ShapeDtypeStruct((windows, block, rcv), jnp.float32),
        scratch_shapes=[
            pltpu.VMEM((group * rcv, block), jnp.bfloat16),
            pltpu.VMEM((windows, block, rcv), jnp.float32),
            pltpu.SemaphoreType.DMA((windows // group,)),
        ],
        compiler_params=params(),
        cost_estimate=pl.CostEstimate(flops=1, bytes_accessed=6 << 20, transcendentals=0),
        name="residual_of_records",
    )(lows, highs, records, coefs, cuts, both)


def finish(values, energies, thresholds, both, receivers):
    shot_dev, _, rcv, block = values.shape
    step = min(2, shot_dev)

    def body(in_ref, thr_ref, both_ref, *refs):
        out_hbm, out_ref, sem = refs[-3:]
        energy = refs[0][...]
        for ref in refs[1:-3]:
            energy = energy + ref[...]
        cuts = thr_ref[...] * jnp.sqrt(energy / (SHOT_BLK * receivers) + epsilon)
        copies = []
        for at in range(0, shot_dev, step):
            for i in range(at, at + step):
                cut = cuts[i : i + 1, :]
                value = in_ref[i].reshape(SHOT_BLK * rcv, block)
                shrunk = value - jnp.minimum(jnp.maximum(value, -cut), cut)
                model = lax.dot_general(
                    both_ref[:, :block], shrunk.astype(jnp.bfloat16), (((1,), (1,)), ((), ())),
                    preferred_element_type=jnp.float32,
                )
                for q in range(SHOT_BLK):
                    out_ref[i, q] = model[:, q * rcv : (q + 1) * rcv].astype(jnp.bfloat16)
            copy = pltpu.make_async_copy(
                out_ref.at[pl.ds(at, step)], out_hbm.at[pl.ds(at, step)], sem.at[at // step]
            )
            copy.start()
            copies.append(copy)
        for copy in copies:
            copy.wait()

    return pl.pallas_call(
        body,
        in_specs=[full_vmem()] * (3 + len(energies)),
        out_specs=pl.BlockSpec(memory_space=pl.ANY),
        out_shape=jax.ShapeDtypeStruct((shot_dev, SHOT_BLK, block, rcv), jnp.bfloat16),
        scratch_shapes=[
            pltpu.VMEM((shot_dev, SHOT_BLK, block, rcv), jnp.bfloat16),
            pltpu.SemaphoreType.DMA((shot_dev // step,)),
        ],
        compiler_params=params(),
        name="model_of_shots",
    )(values, thresholds, both, *energies)


def over_receivers(values):
    if lax.axis_size("rcv") == 2:
        return [values, lax.ppermute(values, "rcv", [(0, 1), (1, 0)])]
    return [lax.psum(values, "rcv")]


def local(record_data, offsets, thresholds):
    owners = lax.axis_size("shot")
    me = lax.axis_index("shot")
    windows, _, block, rcv = record_data.shape
    shots = offsets.shape[0]
    shot_dev = shots // owners
    pairs = shot_dev // 2
    pair_slots = min(pairs, owners // (SHOT_BLK + 1))
    capacity = (pairs + pair_slots - 1) // pair_slots
    receivers = rcv * lax.axis_size("rcv")

    high, low = split_bf16(jnp.asarray(cosine_table(block).T))
    both = jnp.concatenate([high, low], axis=1)
    records = record_data.reshape(windows, block, rcv)
    thr = thresholds[None, :]
    window_ids = jnp.arange(windows, dtype=jnp.int32)

    sent, energy, table = owned(records, offsets, me, owners, capacity, both)
    packed = pack(sent, table, over_receivers(energy), owners, capacity)
    arrived = lax.all_to_all(packed, "shot", split_axis=0, concat_axis=0, tiled=True)

    index = jnp.arange(shots, dtype=jnp.int32)
    ahead = (offsets[None, :] < offsets[:, None]) | (
        (offsets[None, :] == offsets[:, None]) & (index[None, :] < index[:, None])
    )
    place = jnp.sum(ahead.astype(jnp.int32), axis=1)
    ordered = jnp.sum(jnp.where(place[None, :] == index[:, None], offsets[None, :], 0), axis=1)
    mine = lax.dynamic_slice(offsets, (me * shot_dev,), (shot_dev,))
    all_offsets = jnp.concatenate([ordered, mine])
    grid_ids = window_ids[None, :] * owners + jnp.arange(owners, dtype=jnp.int32)[:, None]
    hits = landed(grid_ids.reshape(-1)[None, :], all_offsets[:, None]).astype(jnp.bfloat16)

    def bounds(ids):
        below = jnp.sum((offsets < ids[..., None] - (SHOT_BLK - 1)).astype(jnp.int32), axis=-1)
        upto = jnp.sum((offsets <= ids[..., None]).astype(jnp.int32), axis=-1)
        return below, upto

    own_lows, own_highs = bounds(window_ids * owners + me)
    coefs = again(records, own_lows, own_highs, both)

    slot_ids = jnp.arange(capacity, dtype=jnp.int32)
    held = jnp.max(landed(grid_ids[:, :, None], mine).astype(jnp.int32), axis=2)
    before = (window_ids[:, None] < window_ids[None, :]).astype(jnp.int32)
    held_rank = jnp.sum(held[:, :, None] * before, axis=1)
    taken = (held_rank[:, None, :] == slot_ids[None, :, None]) & (held[:, None, :] > 0)
    held_ids = jnp.sum(jnp.where(taken, grid_ids[:, None, :], 0), axis=2)
    valid = jnp.sum(taken.astype(jnp.int32), axis=2)
    lows, highs = bounds(held_ids)
    lows, highs = lows * valid, highs * valid
    scales = step_size / jnp.maximum((highs - lows).astype(jnp.float32), 1.0)
    targets = mine[:, None] + jnp.arange(SHOT_BLK, dtype=jnp.int32)[None, :]
    slot_of = jnp.arange(owners, dtype=jnp.int32)[:, None] * capacity + held_rank
    slots = jnp.sum(
        jnp.where(targets[:, :, None, None] == grid_ids[None, None], slot_of[None, None], 0),
        axis=(2, 3),
    )

    hits, coefs = lax.optimization_barrier((hits, coefs))
    values, energy2, cuts = second(
        arrived, hits, thr, lows.reshape(-1), highs.reshape(-1), scales.reshape(-1),
        slots.reshape(-1), capacity, windows, receivers,
    )
    energies = over_receivers(energy2)
    residual = remainder(records, coefs, cuts, own_lows, own_highs, both)
    model = finish(values, energies, thr, both, receivers)
    return (model, residual.reshape(windows, 1, block, rcv))


def solution(mesh):
    return jax.shard_map(
        local,
        mesh=mesh,
        in_specs=(P(None, "shot", None, "rcv"), P(), P()),
        out_specs=(P("shot", None, None, "rcv"), P(None, "shot", None, "rcv")),
        check_vma=False,
    )
```

```python
import jax
import jax.numpy as jnp
import numpy as np
from jax import lax
from jax.experimental import pallas as pl
from jax.experimental.pallas import tpu as pltpu
from jax.sharding import PartitionSpec as P

SHOT_BLK = 4
momentum = 0.5
epsilon = 1e-06
step_size = 1.0 + momentum
VMEM_BYTES = 16 * 1024 * 1024
HEAD_VMEM_BYTES = 60 * 1024 * 1024


def cosine_table(length):
    rows = np.arange(length, dtype=np.float64)[:, None]
    cols = np.arange(length, dtype=np.float64)[None, :]
    table = np.cos(np.pi * (cols + 0.5) * rows / length) * np.sqrt(2.0 / length)
    return np.where(rows == 0, table * np.sqrt(0.5), table).astype(np.float32)


def split_bf16(values):
    high = values.astype(jnp.bfloat16)
    low = (values - high.astype(jnp.float32)).astype(jnp.bfloat16)
    return high, low


def full_vmem():
    return pl.BlockSpec(memory_space=pltpu.VMEM)


def full_smem():
    return pl.BlockSpec(memory_space=pltpu.SMEM)


def params(vmem=VMEM_BYTES):
    return pltpu.CompilerParams(vmem_limit_bytes=vmem)


def forward(both, values):
    block = values.shape[0]
    parts = lax.dot_general(
        values, both, (((0,), (0,)), ((), ())), preferred_element_type=jnp.float32
    )
    return parts[:, :block] + parts[:, block:]


def backward(both, coefficients):
    doubled = jnp.concatenate([coefficients, coefficients], axis=1)
    return lax.dot_general(
        both, doubled, (((1,), (1,)), ((), ())), preferred_element_type=jnp.float32
    )


def landed(ids, offsets):
    lag = ids - offsets
    return (lag >= 0) & (lag < SHOT_BLK)


def head(records, offsets, me, owners, capacity, both):
    windows, block, rcv = records.shape
    shots = offsets.shape[0]
    shot_dev = shots // owners
    chunk = 8
    chunks = windows // chunk
    f32, bf16 = jnp.float32, jnp.bfloat16

    def body(
        me_ref, off_hbm, rec_hbm, both_hbm, out_ref, energy_hbm,
        off_ref, rec_ref, both_ref, sent_ref, energy_ref, table_ref, table_smem,
        small_sem, rec_sem, out_sem,
    ):
        get_off = pltpu.make_async_copy(off_hbm, off_ref, small_sem.at[0])
        get_both = pltpu.make_async_copy(both_hbm, both_ref, small_sem.at[1])
        get_rec = [
            pltpu.make_async_copy(
                rec_hbm.at[pl.ds(c * chunk, chunk)],
                rec_ref.at[pl.ds(c * chunk, chunk)],
                rec_sem.at[c],
            )
            for c in range(chunks)
        ]
        get_off.start()
        get_both.start()
        for copy in get_rec:
            copy.start()
        get_off.wait()

        ids = lax.broadcasted_iota(jnp.int32, (windows, shots), 0) * owners + me_ref[0]
        hits = jnp.where(landed(ids, off_ref[...]), 1.0, 0.0)
        cover = jnp.sum(hits, axis=1, keepdims=True)
        scale = 1.0 / jnp.maximum(cover, 1.0)

        shot = lax.broadcasted_iota(jnp.int32, (shots, owners), 0)
        first = lax.broadcasted_iota(jnp.int32, (shots, owners), 1) * shot_dev
        member = jnp.where((shot >= first) & (shot < first + shot_dev), 1.0, 0.0)
        counts = jnp.dot(hits.astype(bf16), member.astype(bf16), preferred_element_type=f32)
        present = jnp.where(counts > 0.5, 1.0, 0.0)
        after = lax.broadcasted_iota(jnp.int32, (windows, windows), 0)
        before = lax.broadcasted_iota(jnp.int32, (windows, windows), 1)
        lower = jnp.where(before < after, 1.0, 0.0)
        rank = jnp.dot(lower.astype(bf16), present.astype(bf16), preferred_element_type=f32)
        rank = rank.astype(jnp.int32)
        window = lax.broadcasted_iota(jnp.int32, (windows, owners), 0)
        for i in range(capacity):
            here = (rank == i) & (present > 0.5)
            table_ref[i : i + 1, :owners] = jnp.sum(
                jnp.where(here, window, 0), axis=0, keepdims=True
            )
        put_table = pltpu.make_async_copy(table_ref, table_smem, small_sem.at[2])
        put_table.start()

        get_both.wait()
        for c in range(chunks):
            get_rec[c].wait()
            for w in range(c * chunk, (c + 1) * chunk):
                spread = (rec_ref[w] * scale[w : w + 1, 0:1]).astype(bf16)
                coef = forward(both_ref[...], spread)
                sent_ref[w] = coef.astype(bf16)
                energy_ref[w : w + 1, :] = jnp.sum(coef * coef, axis=0, keepdims=True)

        put_energy = pltpu.make_async_copy(energy_ref, energy_hbm, small_sem.at[3])
        put_energy.start()
        put_table.wait()

        def send(h, i):
            return pltpu.make_async_copy(
                sent_ref.at[table_smem[i, h]],
                out_ref.at[h, pl.ds(i * rcv, rcv), :],
                out_sem.at[h * capacity + i],
            )

        for h in range(owners):
            for i in range(capacity):
                send(h, i).start()
        for h in range(owners):
            for i in range(capacity):
                send(h, i).wait()
        put_energy.wait()

    hbm = pl.BlockSpec(memory_space=pltpu.HBM)
    table_shape = (8, 128)
    return pl.pallas_call(
        body,
        in_specs=[full_smem(), hbm, hbm, hbm],
        out_specs=[pl.BlockSpec(memory_space=pl.ANY)] * 2,
        out_shape=[
            jax.ShapeDtypeStruct((owners, capacity * rcv, block), bf16),
            jax.ShapeDtypeStruct((windows, block), f32),
        ],
        scratch_shapes=[
            pltpu.VMEM((1, shots), jnp.int32),
            pltpu.VMEM((windows, block, rcv), f32),
            pltpu.VMEM((block, 2 * block), bf16),
            pltpu.VMEM((windows, rcv, block), bf16),
            pltpu.VMEM((windows, block), f32),
            pltpu.VMEM(table_shape, jnp.int32),
            pltpu.SMEM(table_shape, jnp.int32),
            pltpu.SemaphoreType.DMA((4,)),
            pltpu.SemaphoreType.DMA((chunks,)),
            pltpu.SemaphoreType.DMA((owners * capacity,)),
        ],
        compiler_params=params(HEAD_VMEM_BYTES),
        name="pack_coefficients",
    )(me[None], offsets[None, :], records, both)


def cutoffs(energies, hits, thresholds, receivers):
    rows = hits.shape[0]
    block = thresholds.shape[1]

    def body(*refs):
        hit_ref, thr_ref = refs[:2]
        out_ref, cuts_ref = refs[-2:]
        high, low = split_bf16(jnp.concatenate([ref[...] for ref in refs[2:-2]], axis=0))
        sums = jnp.dot(hit_ref[...], high, preferred_element_type=jnp.float32) + jnp.dot(
            hit_ref[...], low, preferred_element_type=jnp.float32
        )
        cuts_ref[...] = thr_ref[...] * jnp.sqrt(sums / (SHOT_BLK * receivers) + epsilon)

        def widen(i, _):
            at = pl.multiple_of(i * 8, 8)
            out_ref[pl.ds(at, 8)] = jnp.broadcast_to(
                cuts_ref[pl.ds(at, 8), :][:, None, :], (8, 8, block)
            )
            return 0

        lax.fori_loop(0, rows // 8, widen, 0, unroll=2)
        out_ref[rows] = jnp.zeros((8, block), jnp.float32)

    return pl.pallas_call(
        body,
        in_specs=[full_vmem()] * (2 + len(energies)),
        out_specs=full_vmem(),
        out_shape=jax.ShapeDtypeStruct((rows + 1, 8, block), jnp.float32),
        scratch_shapes=[pltpu.VMEM((rows, block), jnp.float32)],
        compiler_params=params(),
        name="first_cutoffs",
    )(hits, thresholds, *energies)


def clipped_sum(coef, cut_ref, low, high, none):
    size = jnp.abs(coef)
    unroll = 2

    def add(j, total):
        for u in range(unroll):
            row = low + j * unroll + u
            if u:
                row = jnp.where(row < high, row, none)
            total = total + jnp.minimum(size, cut_ref[row][None])
        return total

    trips = lax.div(high - low + unroll - 1, unroll)
    total = lax.fori_loop(0, trips, add, jnp.zeros_like(coef))
    return jnp.where(coef < 0, -total, total)


def second(arrived, cuts, lows, highs, scales, slots, capacity):
    owners, rows, block = arrived.shape
    rcv = rows // capacity
    tiles = rcv // 8
    shot_dev = slots.shape[0] // SHOT_BLK
    count = owners * capacity
    none = cuts.shape[0] - 1
    shots = none - shot_dev

    def body(
        low_ref, high_ref, scale_ref, slot_ref, in_ref, wide_ref, out_ref, energy_ref, diff_ref
    ):
        def block_of(slot):
            owner = slot // capacity
            start = pl.multiple_of((slot - owner * capacity) * rcv, rcv)
            values = in_ref[owner, pl.ds(start, rcv), :].astype(jnp.float32)
            return values.reshape(tiles, 8, block)

        def difference(slot, _):
            low, high = low_ref[slot], high_ref[slot]

            @pl.when(high > low)
            def _():
                coef = block_of(slot)
                clipped = clipped_sum(coef, wide_ref, low, high, none)
                scale = scale_ref[slot]
                kept = 1.0 - scale * (high - low).astype(jnp.float32)
                diff_ref[slot] = kept * coef + scale * clipped

            return 0

        lax.fori_loop(0, count, difference, 0)

        def one_shot(shot, _):
            cut = wide_ref[shots + shot][None]
            energy = jnp.zeros((8, block), jnp.float32)
            for q in range(SHOT_BLK):
                slot = slot_ref[shot * SHOT_BLK + q]
                coef = block_of(slot)
                shrunk = coef - jnp.minimum(jnp.maximum(coef, -cut), cut)
                value = step_size * shrunk + diff_ref[slot]
                out_ref[shot, q] = value.reshape(rcv, block)
                energy = energy + jnp.sum(value * value, axis=0)
            energy_ref[pl.ds(shot, 1), :] = jnp.sum(energy, axis=0, keepdims=True)
            return 0

        lax.fori_loop(0, shot_dev, one_shot, 0)

    return pl.pallas_call(
        body,
        in_specs=[full_smem()] * 4 + [full_vmem()] * 2,
        out_specs=[full_vmem()] * 2,
        out_shape=[
            jax.ShapeDtypeStruct((shot_dev, SHOT_BLK, rcv, block), jnp.float32),
            jax.ShapeDtypeStruct((shot_dev, block), jnp.float32),
        ],
        scratch_shapes=[pltpu.VMEM((count, tiles, 8, block), jnp.float32)],
        compiler_params=params(),
        cost_estimate=pl.CostEstimate(flops=1, bytes_accessed=12 << 20, transcendentals=0),
        name="second_coefficients",
    )(lows, highs, scales, slots, arrived, cuts)


def again(records, lows, highs, both):
    windows, block, rcv = records.shape

    def body(low_ref, high_ref, rec_ref, both_ref, out_ref):
        for w in range(windows):
            many = jnp.full((1, rcv), (high_ref[w] - low_ref[w]).astype(jnp.float32))
            spread = (rec_ref[w] * (1.0 / jnp.maximum(many, 1.0))).astype(jnp.bfloat16)
            out_ref[w] = forward(both_ref[...], spread)

    return pl.pallas_call(
        body,
        in_specs=[full_smem()] * 2 + [full_vmem()] * 2,
        out_specs=full_vmem(),
        out_shape=jax.ShapeDtypeStruct((windows, rcv, block), jnp.float32),
        compiler_params=params(),
        cost_estimate=pl.CostEstimate(flops=1, bytes_accessed=6 << 20, transcendentals=0),
        name="owned_again",
    )(lows, highs, records, both)


def remainder(records, coefs, cuts, lows, highs, both):
    windows, block, rcv = records.shape
    tiles = rcv // 8
    none = cuts.shape[0] - 1
    group = 4

    def body(
        low_ref, high_ref, rec_ref, coef_ref, cut_ref, both_ref, out_hbm, sum_ref, out_ref, sem
    ):
        copies = []
        for at in range(0, windows, group):
            for w in range(at, at + group):
                low, high = low_ref[w], high_ref[w]
                coef = coef_ref[w].reshape(tiles, 8, block)
                clipped = clipped_sum(coef, cut_ref, low, high, none)
                shrunk = (high - low).astype(jnp.float32) * coef - clipped
                sum_ref[pl.ds((w - at) * rcv, rcv), :] = shrunk.reshape(rcv, block).astype(
                    jnp.bfloat16
                )
            blended = backward(both_ref[...], sum_ref[...])
            for w in range(at, at + group):
                part = blended[:, (w - at) * rcv : (w - at + 1) * rcv]
                out_ref[w] = rec_ref[w] - step_size * part
            copy = pltpu.make_async_copy(
                out_ref.at[pl.ds(at, group)], out_hbm.at[pl.ds(at, group)], sem.at[at // group]
            )
            copy.start()
            copies.append(copy)
        for copy in copies:
            copy.wait()

    return pl.pallas_call(
        body,
        in_specs=[full_smem()] * 2 + [full_vmem()] * 4,
        out_specs=pl.BlockSpec(memory_space=pl.ANY),
        out_shape=jax.ShapeDtypeStruct((windows, block, rcv), jnp.float32),
        scratch_shapes=[
            pltpu.VMEM((group * rcv, block), jnp.bfloat16),
            pltpu.VMEM((windows, block, rcv), jnp.float32),
            pltpu.SemaphoreType.DMA((windows // group,)),
        ],
        compiler_params=params(),
        cost_estimate=pl.CostEstimate(flops=1, bytes_accessed=6 << 20, transcendentals=0),
        name="residual_of_records",
    )(lows, highs, records, coefs, cuts, both)


def finish(values, energies, thresholds, both, receivers):
    shot_dev, _, rcv, block = values.shape
    step = min(2, shot_dev)

    def body(in_ref, thr_ref, both_ref, *refs):
        out_hbm, out_ref, sem = refs[-3:]
        energy = refs[0][...]
        for ref in refs[1:-3]:
            energy = energy + ref[...]
        cuts = thr_ref[...] * jnp.sqrt(energy / (SHOT_BLK * receivers) + epsilon)
        copies = []
        for at in range(0, shot_dev, step):
            for i in range(at, at + step):
                cut = cuts[i : i + 1, :]
                value = in_ref[i].reshape(SHOT_BLK * rcv, block)
                shrunk = value - jnp.minimum(jnp.maximum(value, -cut), cut)
                model = lax.dot_general(
                    both_ref[:, :block], shrunk.astype(jnp.bfloat16), (((1,), (1,)), ((), ())),
                    preferred_element_type=jnp.float32,
                )
                for q in range(SHOT_BLK):
                    out_ref[i, q] = model[:, q * rcv : (q + 1) * rcv].astype(jnp.bfloat16)
            copy = pltpu.make_async_copy(
                out_ref.at[pl.ds(at, step)], out_hbm.at[pl.ds(at, step)], sem.at[at // step]
            )
            copy.start()
            copies.append(copy)
        for copy in copies:
            copy.wait()

    return pl.pallas_call(
        body,
        in_specs=[full_vmem()] * (3 + len(energies)),
        out_specs=pl.BlockSpec(memory_space=pl.ANY),
        out_shape=jax.ShapeDtypeStruct((shot_dev, SHOT_BLK, block, rcv), jnp.bfloat16),
        scratch_shapes=[
            pltpu.VMEM((shot_dev, SHOT_BLK, block, rcv), jnp.bfloat16),
            pltpu.SemaphoreType.DMA((shot_dev // step,)),
        ],
        compiler_params=params(),
        name="model_of_shots",
    )(values, thresholds, both, *energies)


def over_receivers(values):
    if lax.axis_size("rcv") == 2:
        return [values, lax.ppermute(values, "rcv", [(0, 1), (1, 0)])]
    return [lax.psum(values, "rcv")]


def rotate(values, stride, by, size):
    n = lax.axis_size("shot")
    pairs = []
    for i in range(n):
        place = (i // stride) % size
        pairs.append((i, i + ((place + by) % size - place) * stride))
    return lax.ppermute(values, "shot", pairs)


def local(record_data, offsets, thresholds):
    owners = lax.axis_size("shot")
    me = lax.axis_index("shot")
    windows, _, block, rcv = record_data.shape
    shots = offsets.shape[0]
    shot_dev = shots // owners
    pairs = shot_dev // 2
    pair_slots = min(pairs, owners // (SHOT_BLK + 1))
    capacity = (pairs + pair_slots - 1) // pair_slots
    receivers = rcv * lax.axis_size("rcv")

    high, low = split_bf16(jnp.asarray(cosine_table(block).T))
    both = jnp.concatenate([high, low], axis=1)
    records = record_data.reshape(windows, block, rcv)
    thr = thresholds[None, :]
    window_ids = jnp.arange(windows, dtype=jnp.int32)

    packed, energy = head(records, offsets, me, owners, capacity, both)
    packed, records, offsets, thr = lax.optimization_barrier((packed, records, offsets, thr))
    arrived = lax.all_to_all(packed, "shot", split_axis=0, concat_axis=0, tiled=True)

    near = min(4, owners)
    far = owners // near
    energy = sum(over_receivers(energy))
    energy = jnp.concatenate([energy] + [rotate(energy, 1, j, near) for j in range(1, near)])
    energies = [energy] + [rotate(energy, near, j, far) for j in range(1, far)]
    back = jnp.arange(far, dtype=jnp.int32)[:, None]
    side = jnp.arange(near, dtype=jnp.int32)[None, :]
    origin = (me // near - back + far) % far * near + (me % near - side + near) % near
    energy_ids = (window_ids * owners + origin[:, :, None]).reshape(-1)

    index = jnp.arange(shots, dtype=jnp.int32)
    ahead = (offsets[None, :] < offsets[:, None]) | (
        (offsets[None, :] == offsets[:, None]) & (index[None, :] < index[:, None])
    )
    place = jnp.sum(ahead.astype(jnp.int32), axis=1)
    ordered = jnp.sum(jnp.where(place[None, :] == index[:, None], offsets[None, :], 0), axis=1)
    mine = lax.dynamic_slice(offsets, (me * shot_dev,), (shot_dev,))
    all_offsets = jnp.concatenate([ordered, mine])
    grid_ids = window_ids[None, :] * owners + jnp.arange(owners, dtype=jnp.int32)[:, None]
    hits = landed(energy_ids[None, :], all_offsets[:, None]).astype(jnp.bfloat16)

    def bounds(ids):
        below = jnp.sum((offsets < ids[..., None] - (SHOT_BLK - 1)).astype(jnp.int32), axis=-1)
        upto = jnp.sum((offsets <= ids[..., None]).astype(jnp.int32), axis=-1)
        return below, upto

    own_lows, own_highs = bounds(window_ids * owners + me)
    coefs = again(records, own_lows, own_highs, both)

    slot_ids = jnp.arange(capacity, dtype=jnp.int32)
    held = jnp.max(landed(grid_ids[:, :, None], mine).astype(jnp.int32), axis=2)
    before = (window_ids[:, None] < window_ids[None, :]).astype(jnp.int32)
    held_rank = jnp.sum(held[:, :, None] * before, axis=1)
    taken = (held_rank[:, None, :] == slot_ids[None, :, None]) & (held[:, None, :] > 0)
    held_ids = jnp.sum(jnp.where(taken, grid_ids[:, None, :], 0), axis=2)
    valid = jnp.sum(taken.astype(jnp.int32), axis=2)
    lows, highs = bounds(held_ids)
    lows, highs = lows * valid, highs * valid
    scales = step_size / jnp.maximum((highs - lows).astype(jnp.float32), 1.0)
    targets = mine[:, None] + jnp.arange(SHOT_BLK, dtype=jnp.int32)[None, :]
    slot_of = jnp.arange(owners, dtype=jnp.int32)[:, None] * capacity + held_rank
    slots = jnp.sum(
        jnp.where(targets[:, :, None, None] == grid_ids[None, None], slot_of[None, None], 0),
        axis=(2, 3),
    )

    hits, coefs = lax.optimization_barrier((hits, coefs))
    cuts = cutoffs(energies, hits, thr, receivers)
    values, energy2 = second(
        arrived, cuts, lows.reshape(-1), highs.reshape(-1), scales.reshape(-1),
        slots.reshape(-1), capacity,
    )
    energies = over_receivers(energy2)
    residual = remainder(records, coefs, cuts, own_lows, own_highs, both)
    model = finish(values, energies, thr, both, receivers)
    return (model, residual.reshape(windows, 1, block, rcv))


def solution(mesh):
    return jax.shard_map(
        local,
        mesh=mesh,
        in_specs=(P(None, "shot", None, "rcv"), P(), P()),
        out_specs=(P("shot", None, None, "rcv"), P(None, "shot", None, "rcv")),
        check_vma=False,
    )
```

```python
import jax
import jax.numpy as jnp
import numpy as np
from jax import lax
from jax.experimental import pallas as pl
from jax.experimental.pallas import tpu as pltpu
from jax.sharding import PartitionSpec as P

SHOT_BLK = 4
momentum = 0.5
epsilon = 1e-06
step_size = 1.0 + momentum
VMEM_BYTES = 16 * 1024 * 1024
HEAD_VMEM_BYTES = 60 * 1024 * 1024


def cosine_table(length):
    rows = np.arange(length, dtype=np.float64)[:, None]
    cols = np.arange(length, dtype=np.float64)[None, :]
    table = np.cos(np.pi * (cols + 0.5) * rows / length) * np.sqrt(2.0 / length)
    return np.where(rows == 0, table * np.sqrt(0.5), table).astype(np.float32)


def split_bf16(values):
    high = values.astype(jnp.bfloat16)
    low = (values - high.astype(jnp.float32)).astype(jnp.bfloat16)
    return high, low


def full_vmem():
    return pl.BlockSpec(memory_space=pltpu.VMEM)


def full_smem():
    return pl.BlockSpec(memory_space=pltpu.SMEM)


def params(vmem=VMEM_BYTES):
    return pltpu.CompilerParams(vmem_limit_bytes=vmem)


def forward(both, values):
    block = values.shape[0]
    parts = lax.dot_general(
        values, both, (((0,), (0,)), ((), ())), preferred_element_type=jnp.float32
    )
    return parts[:, :block] + parts[:, block:]


def backward(both, coefficients):
    doubled = jnp.concatenate([coefficients, coefficients], axis=1)
    return lax.dot_general(
        both, doubled, (((1,), (1,)), ((), ())), preferred_element_type=jnp.float32
    )


def landed(ids, offsets):
    lag = ids - offsets
    return (lag >= 0) & (lag < SHOT_BLK)


def head(records, offsets, me, owners, capacity, both):
    windows, block, rcv = records.shape
    shots = offsets.shape[0]
    shot_dev = shots // owners
    chunk = 8
    chunks = windows // chunk
    f32, bf16 = jnp.float32, jnp.bfloat16

    def body(
        me_ref, off_hbm, rec_hbm, both_hbm, out_ref, energy_hbm,
        off_ref, rec_ref, both_ref, sent_ref, energy_ref, table_ref, table_smem,
        small_sem, rec_sem, out_sem,
    ):
        get_off = pltpu.make_async_copy(off_hbm, off_ref, small_sem.at[0])
        get_both = pltpu.make_async_copy(both_hbm, both_ref, small_sem.at[1])
        get_rec = [
            pltpu.make_async_copy(
                rec_hbm.at[pl.ds(c * chunk, chunk)],
                rec_ref.at[pl.ds(c * chunk, chunk)],
                rec_sem.at[c],
            )
            for c in range(chunks)
        ]
        get_off.start()
        get_both.start()
        for copy in get_rec:
            copy.start()
        get_off.wait()

        ids = lax.broadcasted_iota(jnp.int32, (windows, shots), 0) * owners + me_ref[0]
        hits = jnp.where(landed(ids, off_ref[...]), 1.0, 0.0)
        cover = jnp.sum(hits, axis=1, keepdims=True)
        scale = 1.0 / jnp.maximum(cover, 1.0)

        shot = lax.broadcasted_iota(jnp.int32, (shots, owners), 0)
        first = lax.broadcasted_iota(jnp.int32, (shots, owners), 1) * shot_dev
        member = jnp.where((shot >= first) & (shot < first + shot_dev), 1.0, 0.0)
        counts = jnp.dot(hits.astype(bf16), member.astype(bf16), preferred_element_type=f32)
        present = jnp.where(counts > 0.5, 1.0, 0.0)
        after = lax.broadcasted_iota(jnp.int32, (windows, windows), 0)
        before = lax.broadcasted_iota(jnp.int32, (windows, windows), 1)
        lower = jnp.where(before < after, 1.0, 0.0)
        rank = jnp.dot(lower.astype(bf16), present.astype(bf16), preferred_element_type=f32)
        rank = rank.astype(jnp.int32)
        window = lax.broadcasted_iota(jnp.int32, (windows, owners), 0)
        for i in range(capacity):
            here = (rank == i) & (present > 0.5)
            table_ref[i : i + 1, :owners] = jnp.sum(
                jnp.where(here, window, 0), axis=0, keepdims=True
            )
        put_table = pltpu.make_async_copy(table_ref, table_smem, small_sem.at[2])
        put_table.start()

        get_both.wait()
        for c in range(chunks):
            get_rec[c].wait()
            for w in range(c * chunk, (c + 1) * chunk):
                spread = (rec_ref[w] * scale[w : w + 1, 0:1]).astype(bf16)
                coef = forward(both_ref[...], spread)
                sent_ref[w] = coef.astype(bf16)
                energy_ref[w : w + 1, :] = jnp.sum(coef * coef, axis=0, keepdims=True)

        put_energy = pltpu.make_async_copy(energy_ref, energy_hbm, small_sem.at[3])
        put_energy.start()
        put_table.wait()

        def send(h, i):
            return pltpu.make_async_copy(
                sent_ref.at[table_smem[i, h]],
                out_ref.at[h, pl.ds(i * rcv, rcv), :],
                out_sem.at[h * capacity + i],
            )

        for h in range(owners):
            for i in range(capacity):
                send(h, i).start()
        for h in range(owners):
            for i in range(capacity):
                send(h, i).wait()
        put_energy.wait()

    hbm = pl.BlockSpec(memory_space=pltpu.HBM)
    table_shape = (8, 128)
    return pl.pallas_call(
        body,
        in_specs=[full_smem(), hbm, hbm, hbm],
        out_specs=[pl.BlockSpec(memory_space=pl.ANY)] * 2,
        out_shape=[
            jax.ShapeDtypeStruct((owners, capacity * rcv, block), bf16),
            jax.ShapeDtypeStruct((windows, block), f32),
        ],
        scratch_shapes=[
            pltpu.VMEM((1, shots), jnp.int32),
            pltpu.VMEM((windows, block, rcv), f32),
            pltpu.VMEM((block, 2 * block), bf16),
            pltpu.VMEM((windows, rcv, block), bf16),
            pltpu.VMEM((windows, block), f32),
            pltpu.VMEM(table_shape, jnp.int32),
            pltpu.SMEM(table_shape, jnp.int32),
            pltpu.SemaphoreType.DMA((4,)),
            pltpu.SemaphoreType.DMA((chunks,)),
            pltpu.SemaphoreType.DMA((owners * capacity,)),
        ],
        compiler_params=params(HEAD_VMEM_BYTES),
        name="pack_coefficients",
    )(me[None], offsets[None, :], records, both)


def cutoffs(energies, hits, thresholds, receivers):
    rows = hits.shape[0]
    block = thresholds.shape[1]

    def body(*refs):
        hit_ref, thr_ref = refs[:2]
        out_ref, cuts_ref = refs[-2:]
        energy = jnp.concatenate([ref[...] for ref in refs[2:-2]], axis=0)
        sums = jnp.dot(hit_ref[...], energy, preferred_element_type=jnp.float32)
        cuts_ref[...] = thr_ref[...] * jnp.sqrt(sums / (SHOT_BLK * receivers) + epsilon)

        def widen(i, _):
            at = pl.multiple_of(i * 8, 8)
            out_ref[pl.ds(at, 8)] = jnp.broadcast_to(
                cuts_ref[pl.ds(at, 8), :][:, None, :], (8, 8, block)
            )
            return 0

        lax.fori_loop(0, rows // 8, widen, 0, unroll=2)
        out_ref[rows] = jnp.zeros((8, block), jnp.float32)

    return pl.pallas_call(
        body,
        in_specs=[full_vmem()] * (2 + len(energies)),
        out_specs=full_vmem(),
        out_shape=jax.ShapeDtypeStruct((rows + 1, 8, block), jnp.float32),
        scratch_shapes=[pltpu.VMEM((rows, block), jnp.float32)],
        compiler_params=params(),
        name="first_cutoffs",
    )(hits, thresholds, *energies)


def clipped_sum(coef, cut_ref, low, high, none):
    size = jnp.abs(coef)
    peel, unroll = 6, 2

    def term(row):
        return jnp.minimum(size, cut_ref[jnp.where(row < high, row, none)][None])

    total = term(low)
    for u in range(1, peel):
        total = total + term(low + u)

    def add(j, total):
        for u in range(unroll):
            total = total + term(low + peel + j * unroll + u)
        return total

    left = jnp.maximum(high - low - peel, 0)
    total = lax.fori_loop(0, lax.div(left + unroll - 1, unroll), add, total)
    return jnp.where(coef < 0, -total, total)


def second(arrived, cuts, numbers, capacity):
    owners, rows, block = arrived.shape
    rcv = rows // capacity
    tiles = rcv // 8
    count = owners * capacity
    shot_dev = (numbers.shape[0] - 2 * count) // SHOT_BLK
    none = cuts.shape[0] - 1
    shots = none - shot_dev

    def body(number_ref, in_ref, wide_ref, out_ref, energy_ref, diff_ref, coef_ref):
        def block_of(slot):
            owner = slot // capacity
            start = pl.multiple_of((slot - owner * capacity) * rcv, rcv)
            values = in_ref[owner, pl.ds(start, rcv), :].astype(jnp.float32)
            return values.reshape(tiles, 8, block)

        def difference(slot, _):
            low, high = number_ref[slot], number_ref[count + slot]

            @pl.when(high > low)
            def _():
                coef = block_of(slot)
                clipped = clipped_sum(coef, wide_ref, low, high, none)
                many = jnp.full((1, 8, block), (high - low).astype(jnp.float32))
                scale = step_size / many
                kept = 1.0 + step_size - scale * many
                diff_ref[slot] = kept * coef + scale * clipped
                coef_ref[slot] = step_size * coef

            return 0

        lax.fori_loop(0, count, difference, 0)

        def one_shot(shot, _):
            cut = step_size * wide_ref[shots + shot][None]
            energy = jnp.zeros((8, block), jnp.float32)
            for q in range(SHOT_BLK):
                slot = number_ref[2 * count + shot * SHOT_BLK + q]
                value = diff_ref[slot] - jnp.minimum(jnp.maximum(coef_ref[slot], -cut), cut)
                out_ref[shot, q] = value.reshape(rcv, block)
                energy = energy + jnp.sum(value * value, axis=0)
            energy_ref[pl.ds(shot, 1), :] = jnp.sum(energy, axis=0, keepdims=True)
            return 0

        lax.fori_loop(0, shot_dev, one_shot, 0)

    return pl.pallas_call(
        body,
        in_specs=[full_smem()] + [full_vmem()] * 2,
        out_specs=[full_vmem()] * 2,
        out_shape=[
            jax.ShapeDtypeStruct((shot_dev, SHOT_BLK, rcv, block), jnp.float32),
            jax.ShapeDtypeStruct((shot_dev, block), jnp.float32),
        ],
        scratch_shapes=[pltpu.VMEM((count, tiles, 8, block), jnp.float32)] * 2,
        compiler_params=params(),
        cost_estimate=pl.CostEstimate(flops=1, bytes_accessed=12 << 20, transcendentals=0),
        name="second_coefficients",
    )(numbers, arrived, cuts)


def remainder(records, cuts, lows, highs, both):
    windows, block, rcv = records.shape
    tiles = rcv // 8
    none = cuts.shape[0] - 1
    group = 4

    def body(
        low_ref, high_ref, rec_ref, cut_ref, both_ref, out_hbm, coef_ref, sum_ref, out_ref, sem
    ):
        for w in range(windows):
            many = jnp.full((1, rcv), (high_ref[w] - low_ref[w]).astype(jnp.float32))
            spread = (rec_ref[w] * (1.0 / jnp.maximum(many, 1.0))).astype(jnp.bfloat16)
            coef_ref[w] = forward(both_ref[...], spread)
        copies = []
        for at in range(0, windows, group):
            for w in range(at, at + group):
                low, high = low_ref[w], high_ref[w]
                coef = coef_ref[w].reshape(tiles, 8, block)
                clipped = clipped_sum(coef, cut_ref, low, high, none)
                shrunk = (high - low).astype(jnp.float32) * coef - clipped
                sum_ref[pl.ds((w - at) * rcv, rcv), :] = shrunk.reshape(rcv, block).astype(
                    jnp.bfloat16
                )
            blended = backward(both_ref[...], sum_ref[...])
            for w in range(at, at + group):
                part = blended[:, (w - at) * rcv : (w - at + 1) * rcv]
                out_ref[w] = rec_ref[w] - step_size * part
            copy = pltpu.make_async_copy(
                out_ref.at[pl.ds(at, group)], out_hbm.at[pl.ds(at, group)], sem.at[at // group]
            )
            copy.start()
            copies.append(copy)
        for copy in copies:
            copy.wait()

    return pl.pallas_call(
        body,
        in_specs=[full_smem()] * 2 + [full_vmem()] * 3,
        out_specs=pl.BlockSpec(memory_space=pl.ANY),
        out_shape=jax.ShapeDtypeStruct((windows, block, rcv), jnp.float32),
        scratch_shapes=[
            pltpu.VMEM((windows, rcv, block), jnp.float32),
            pltpu.VMEM((group * rcv, block), jnp.bfloat16),
            pltpu.VMEM((windows, block, rcv), jnp.float32),
            pltpu.SemaphoreType.DMA((windows // group,)),
        ],
        compiler_params=params(),
        cost_estimate=pl.CostEstimate(flops=1, bytes_accessed=6 << 20, transcendentals=0),
        name="residual_of_records",
    )(lows, highs, records, cuts, both)


def finish(values, energies, thresholds, both, receivers):
    shot_dev, _, rcv, block = values.shape
    step = min(2, shot_dev)

    def body(in_ref, thr_ref, both_ref, *refs):
        out_hbm, out_ref, sem = refs[-3:]
        energy = refs[0][...]
        for ref in refs[1:-3]:
            energy = energy + ref[...]
        cuts = thr_ref[...] * jnp.sqrt(energy / (SHOT_BLK * receivers) + epsilon)
        copies = []
        for at in range(0, shot_dev, step):
            for i in range(at, at + step):
                cut = cuts[i : i + 1, :]
                value = in_ref[i].reshape(SHOT_BLK * rcv, block)
                shrunk = value - jnp.minimum(jnp.maximum(value, -cut), cut)
                model = lax.dot_general(
                    both_ref[:, :block], shrunk.astype(jnp.bfloat16), (((1,), (1,)), ((), ())),
                    preferred_element_type=jnp.float32,
                )
                for q in range(SHOT_BLK):
                    out_ref[i, q] = model[:, q * rcv : (q + 1) * rcv].astype(jnp.bfloat16)
            copy = pltpu.make_async_copy(
                out_ref.at[pl.ds(at, step)], out_hbm.at[pl.ds(at, step)], sem.at[at // step]
            )
            copy.start()
            copies.append(copy)
        for copy in copies:
            copy.wait()

    return pl.pallas_call(
        body,
        in_specs=[full_vmem()] * (3 + len(energies)),
        out_specs=pl.BlockSpec(memory_space=pl.ANY),
        out_shape=jax.ShapeDtypeStruct((shot_dev, SHOT_BLK, block, rcv), jnp.bfloat16),
        scratch_shapes=[
            pltpu.VMEM((shot_dev, SHOT_BLK, block, rcv), jnp.bfloat16),
            pltpu.SemaphoreType.DMA((shot_dev // step,)),
        ],
        compiler_params=params(),
        name="model_of_shots",
    )(values, thresholds, both, *energies)


def over_receivers(values):
    if lax.axis_size("rcv") == 2:
        return [values, lax.ppermute(values, "rcv", [(0, 1), (1, 0)])]
    return [lax.psum(values, "rcv")]


def rotate(values, stride, by, size):
    n = lax.axis_size("shot")
    pairs = []
    for i in range(n):
        place = (i // stride) % size
        pairs.append((i, i + ((place + by) % size - place) * stride))
    return lax.ppermute(values, "shot", pairs)


def local(record_data, offsets, thresholds):
    owners = lax.axis_size("shot")
    me = lax.axis_index("shot")
    windows, _, block, rcv = record_data.shape
    shots = offsets.shape[0]
    shot_dev = shots // owners
    pairs = shot_dev // 2
    pair_slots = min(pairs, owners // (SHOT_BLK + 1))
    capacity = (pairs + pair_slots - 1) // pair_slots
    receivers = rcv * lax.axis_size("rcv")

    high, low = split_bf16(jnp.asarray(cosine_table(block).T))
    both = jnp.concatenate([high, low], axis=1)
    records = record_data.reshape(windows, block, rcv)
    thr = thresholds[None, :]
    window_ids = jnp.arange(windows, dtype=jnp.int32)

    packed, energy = head(records, offsets, me, owners, capacity, both)
    packed, records, offsets, thr = lax.optimization_barrier((packed, records, offsets, thr))
    arrived = lax.all_to_all(packed, "shot", split_axis=0, concat_axis=0, tiled=True)

    near = min(4, owners)
    far = owners // near
    energy = energy.astype(jnp.bfloat16)
    energy = sum(part.astype(jnp.float32) for part in over_receivers(energy)).astype(jnp.bfloat16)
    energy = jnp.concatenate([energy] + [rotate(energy, 1, j, near) for j in range(1, near)])
    energies = [energy] + [rotate(energy, near, j, far) for j in range(1, far)]
    back = jnp.arange(far, dtype=jnp.int32)[:, None]
    side = jnp.arange(near, dtype=jnp.int32)[None, :]
    origin = (me // near - back + far) % far * near + (me % near - side + near) % near
    energy_ids = (window_ids * owners + origin[:, :, None]).reshape(-1)

    index = jnp.arange(shots, dtype=jnp.int32)
    ahead = (offsets[None, :] < offsets[:, None]) | (
        (offsets[None, :] == offsets[:, None]) & (index[None, :] < index[:, None])
    )
    place = jnp.sum(ahead.astype(jnp.int32), axis=1)
    ordered = jnp.sum(jnp.where(place[None, :] == index[:, None], offsets[None, :], 0), axis=1)
    mine = lax.dynamic_slice(offsets, (me * shot_dev,), (shot_dev,))
    all_offsets = jnp.concatenate([ordered, mine])
    grid_ids = window_ids[None, :] * owners + jnp.arange(owners, dtype=jnp.int32)[:, None]
    hits = landed(energy_ids[None, :], all_offsets[:, None]).astype(jnp.bfloat16)

    def bounds(ids):
        below = jnp.sum((offsets < ids[..., None] - (SHOT_BLK - 1)).astype(jnp.int32), axis=-1)
        upto = jnp.sum((offsets <= ids[..., None]).astype(jnp.int32), axis=-1)
        return below, upto

    own_lows, own_highs = bounds(window_ids * owners + me)

    slot_ids = jnp.arange(capacity, dtype=jnp.int32)
    held = jnp.max(landed(grid_ids[:, :, None], mine).astype(jnp.int32), axis=2)
    before = (window_ids[:, None] < window_ids[None, :]).astype(jnp.int32)
    held_rank = jnp.sum(held[:, :, None] * before, axis=1)
    taken = (held_rank[:, None, :] == slot_ids[None, :, None]) & (held[:, None, :] > 0)
    held_ids = jnp.sum(jnp.where(taken, grid_ids[:, None, :], 0), axis=2)
    valid = jnp.sum(taken.astype(jnp.int32), axis=2)
    lows, highs = bounds(held_ids)
    lows, highs = lows * valid, highs * valid
    targets = mine[:, None] + jnp.arange(SHOT_BLK, dtype=jnp.int32)[None, :]
    slot_of = jnp.arange(owners, dtype=jnp.int32)[:, None] * capacity + held_rank
    slots = jnp.sum(
        jnp.where(targets[:, :, None, None] == grid_ids[None, None], slot_of[None, None], 0),
        axis=(2, 3),
    )

    numbers = jnp.concatenate([lows.reshape(-1), highs.reshape(-1), slots.reshape(-1)])
    cuts = cutoffs(energies, hits, thr, receivers)
    values, energy2 = second(arrived, cuts, numbers, capacity)
    energies = over_receivers(energy2)
    residual = remainder(records, cuts, own_lows, own_highs, both)
    model = finish(values, energies, thr, both, receivers)
    return (model, residual.reshape(windows, 1, block, rcv))


def solution(mesh):
    return jax.shard_map(
        local,
        mesh=mesh,
        in_specs=(P(None, "shot", None, "rcv"), P(), P()),
        out_specs=(P("shot", None, None, "rcv"), P(None, "shot", None, "rcv")),
        check_vma=False,
    )
```

```python
import jax
import jax.numpy as jnp
import numpy as np
from jax import lax
from jax.experimental import pallas as pl
from jax.experimental.pallas import tpu as pltpu
from jax.sharding import PartitionSpec as P

SHOT_BLK = 4
momentum = 0.5
epsilon = 1e-06
step_size = 1.0 + momentum
VMEM_BYTES = 16 * 1024 * 1024
HEAD_VMEM_BYTES = 60 * 1024 * 1024


def cosine_table(length):
    rows = np.arange(length, dtype=np.float64)[:, None]
    cols = np.arange(length, dtype=np.float64)[None, :]
    table = np.cos(np.pi * (cols + 0.5) * rows / length) * np.sqrt(2.0 / length)
    return np.where(rows == 0, table * np.sqrt(0.5), table).astype(np.float32)


def split_bf16(values):
    high = values.astype(jnp.bfloat16)
    low = (values - high.astype(jnp.float32)).astype(jnp.bfloat16)
    return high, low


def full_vmem():
    return pl.BlockSpec(memory_space=pltpu.VMEM)


def full_smem():
    return pl.BlockSpec(memory_space=pltpu.SMEM)


def params(vmem=VMEM_BYTES):
    return pltpu.CompilerParams(vmem_limit_bytes=vmem)


def forward(both, values):
    block = values.shape[0]
    parts = lax.dot_general(
        values, both, (((0,), (0,)), ((), ())), preferred_element_type=jnp.float32
    )
    return parts[:, :block] + parts[:, block:]


def backward(both, coefficients):
    doubled = jnp.concatenate([coefficients, coefficients], axis=1)
    return lax.dot_general(
        both, doubled, (((1,), (1,)), ((), ())), preferred_element_type=jnp.float32
    )


def landed(ids, offsets):
    lag = ids - offsets
    return (lag >= 0) & (lag < SHOT_BLK)


def head(records, offsets, me, owners, capacity, both):
    windows, block, rcv = records.shape
    shots = offsets.shape[0]
    shot_dev = shots // owners
    chunk = 8
    chunks = windows // chunk
    f32, bf16 = jnp.float32, jnp.bfloat16

    def body(
        me_ref, off_hbm, rec_hbm, both_hbm, out_ref, energy_hbm,
        off_ref, rec_ref, both_ref, sent_ref, energy_ref, table_ref, table_smem,
        small_sem, rec_sem, out_sem,
    ):
        get_off = pltpu.make_async_copy(off_hbm, off_ref, small_sem.at[0])
        get_both = pltpu.make_async_copy(both_hbm, both_ref, small_sem.at[1])
        get_rec = [
            pltpu.make_async_copy(
                rec_hbm.at[pl.ds(c * chunk, chunk)],
                rec_ref.at[pl.ds(c * chunk, chunk)],
                rec_sem.at[c],
            )
            for c in range(chunks)
        ]
        get_off.start()
        get_both.start()
        for copy in get_rec:
            copy.start()
        get_off.wait()

        ids = lax.broadcasted_iota(jnp.int32, (windows, shots), 0) * owners + me_ref[0]
        hits = jnp.where(landed(ids, off_ref[...]), 1.0, 0.0)
        cover = jnp.sum(hits, axis=1, keepdims=True)
        scale = 1.0 / jnp.maximum(cover, 1.0)

        shot = lax.broadcasted_iota(jnp.int32, (shots, owners), 0)
        first = lax.broadcasted_iota(jnp.int32, (shots, owners), 1) * shot_dev
        member = jnp.where((shot >= first) & (shot < first + shot_dev), 1.0, 0.0)
        counts = jnp.dot(hits.astype(bf16), member.astype(bf16), preferred_element_type=f32)
        present = jnp.where(counts > 0.5, 1.0, 0.0)
        after = lax.broadcasted_iota(jnp.int32, (windows, windows), 0)
        before = lax.broadcasted_iota(jnp.int32, (windows, windows), 1)
        lower = jnp.where(before < after, 1.0, 0.0)
        rank = jnp.dot(lower.astype(bf16), present.astype(bf16), preferred_element_type=f32)
        rank = rank.astype(jnp.int32)
        window = lax.broadcasted_iota(jnp.int32, (windows, owners), 0)
        for i in range(capacity):
            here = (rank == i) & (present > 0.5)
            table_ref[i : i + 1, :owners] = jnp.sum(
                jnp.where(here, window, 0), axis=0, keepdims=True
            )
        put_table = pltpu.make_async_copy(table_ref, table_smem, small_sem.at[2])
        put_table.start()

        get_both.wait()
        rows = []
        for c in range(chunks):
            get_rec[c].wait()
            for w in range(c * chunk, (c + 1) * chunk):
                spread = (rec_ref[w] * scale[w : w + 1, 0:1]).astype(bf16)
                coef = forward(both_ref[...], spread)
                sent_ref[w] = coef.astype(bf16)
                rows.append(jnp.sum(coef * coef, axis=0, keepdims=True))

        energy_ref[...] = jnp.concatenate(rows, axis=0).astype(bf16)
        put_energy = pltpu.make_async_copy(energy_ref, energy_hbm, small_sem.at[3])
        put_energy.start()
        put_table.wait()

        def send(h, i):
            return pltpu.make_async_copy(
                sent_ref.at[table_smem[i, h]],
                out_ref.at[h, pl.ds(i * rcv, rcv), :],
                out_sem.at[h * capacity + i],
            )

        for h in range(owners):
            for i in range(capacity):
                send(h, i).start()
        for h in range(owners):
            for i in range(capacity):
                send(h, i).wait()
        put_energy.wait()

    hbm = pl.BlockSpec(memory_space=pltpu.HBM)
    table_shape = (8, 128)
    return pl.pallas_call(
        body,
        in_specs=[full_smem(), hbm, hbm, hbm],
        out_specs=[pl.BlockSpec(memory_space=pl.ANY)] * 2,
        out_shape=[
            jax.ShapeDtypeStruct((owners, capacity * rcv, block), bf16),
            jax.ShapeDtypeStruct((windows, block), bf16),
        ],
        scratch_shapes=[
            pltpu.VMEM((1, shots), jnp.int32),
            pltpu.VMEM((windows, block, rcv), f32),
            pltpu.VMEM((block, 2 * block), bf16),
            pltpu.VMEM((windows, rcv, block), bf16),
            pltpu.VMEM((windows, block), bf16),
            pltpu.VMEM(table_shape, jnp.int32),
            pltpu.SMEM(table_shape, jnp.int32),
            pltpu.SemaphoreType.DMA((4,)),
            pltpu.SemaphoreType.DMA((chunks,)),
            pltpu.SemaphoreType.DMA((owners * capacity,)),
        ],
        compiler_params=params(HEAD_VMEM_BYTES),
        name="pack_coefficients",
    )(me[None], offsets[None, :], records, both)


def cutoffs(energies, hits, thresholds, receivers):
    rows = hits.shape[0]
    block = thresholds.shape[1]

    def body(*refs):
        hit_ref, thr_ref = refs[:2]
        out_ref, cuts_ref = refs[-2:]
        sums = jnp.dot(hit_ref[...], refs[2][...], preferred_element_type=jnp.float32)
        for ref in refs[3:-2]:
            sums = sums + jnp.dot(hit_ref[...], ref[...], preferred_element_type=jnp.float32)
        cuts_ref[...] = thr_ref[...] * jnp.sqrt(sums / (SHOT_BLK * receivers) + epsilon)

        def widen(i, _):
            at = pl.multiple_of(i * 8, 8)
            out_ref[pl.ds(at, 8)] = jnp.broadcast_to(
                cuts_ref[pl.ds(at, 8), :][:, None, :], (8, 8, block)
            )
            return 0

        lax.fori_loop(0, rows // 8, widen, 0, unroll=2)
        out_ref[rows] = jnp.zeros((8, block), jnp.float32)

    return pl.pallas_call(
        body,
        in_specs=[full_vmem()] * (2 + len(energies)),
        out_specs=full_vmem(),
        out_shape=jax.ShapeDtypeStruct((rows + 1, 8, block), jnp.float32),
        scratch_shapes=[pltpu.VMEM((rows, block), jnp.float32)],
        compiler_params=params(),
        name="first_cutoffs",
    )(hits, thresholds, *energies)


def clipped_sum(coef, cut_ref, low, high, none):
    size = jnp.abs(coef)
    peel, unroll = 6, 2

    def term(row):
        return jnp.minimum(size, cut_ref[jnp.where(row < high, row, none)][None])

    total = term(low)
    for u in range(1, peel):
        total = total + term(low + u)

    def add(j, total):
        for u in range(unroll):
            total = total + term(low + peel + j * unroll + u)
        return total

    left = jnp.maximum(high - low - peel, 0)
    total = lax.fori_loop(0, lax.div(left + unroll - 1, unroll), add, total)
    return jnp.where(coef < 0, -total, total)


def shot_terms(coef, cut_ref, low, high, none):
    clipped = clipped_sum(coef, cut_ref, low, high, none)
    many = jnp.full((1, 8, coef.shape[2]), (high - low).astype(jnp.float32))
    scale = step_size / jnp.maximum(many, 1.0)
    diff = (1.0 + step_size - scale * many) * coef + scale * clipped
    return diff, step_size * coef, many * coef - clipped


def landed_energies(records, cuts, numbers, both, groups):
    windows, block, rcv = records.shape
    tiles = rcv // 8
    none = cuts.shape[0] - 1
    shots = numbers.shape[0] - 2 * windows
    size = shots // groups
    chunk = 4
    chunks = windows // chunk

    def body(number_ref, rec_ref, cut_ref, both_ref, *refs):
        energy_refs, out_hbm = refs[:groups], refs[groups]
        diff_ref, base_ref, shrunk_ref, out_ref, sum_ref, sem = refs[groups + 1 :]
        sum_ref[...] = jnp.zeros_like(sum_ref)
        for w in range(windows):
            cover = (number_ref[windows + w] - number_ref[w]).astype(jnp.float32)
            scale = 1.0 / jnp.maximum(jnp.full((1, rcv), cover), 1.0)
            spread = (rec_ref[w] * scale).astype(jnp.bfloat16)
            base_ref[w] = forward(both_ref[...], spread).reshape(tiles, 8, block)

        def one_window(w, _):
            low, high = number_ref[w], number_ref[windows + w]
            diff_ref[w], base_ref[w], shrunk = shot_terms(base_ref[w], cut_ref, low, high, none)
            shrunk_ref[w] = shrunk.reshape(rcv, block).astype(jnp.bfloat16)
            return 0

        lax.fori_loop(0, windows, one_window, 0)
        copies = []
        for c in range(chunks):
            part = pl.ds(c * chunk, chunk)
            blended = backward(both_ref[...], shrunk_ref[part].reshape(chunk * rcv, block))
            for w in range(chunk):
                at = c * chunk + w
                out_ref[at] = rec_ref[at] - step_size * blended[:, w * rcv : (w + 1) * rcv]
            copy = pltpu.make_async_copy(out_ref.at[part], out_hbm.at[part], sem.at[c])
            copy.start()
            copies.append(copy)

        def energies_of_window(w, _):
            diff, base = diff_ref[w], base_ref[w]

            def one_shot(row, _):
                cut = step_size * cut_ref[row][None]
                value = diff - jnp.minimum(jnp.maximum(base, -cut), cut)
                sum_ref[number_ref[2 * windows + row]] = jnp.sum(value * value, axis=0)
                return 0

            lax.fori_loop(number_ref[w], number_ref[windows + w], one_shot, 0)
            return 0

        lax.fori_loop(0, windows, energies_of_window, 0)
        for g in range(groups):
            energy_refs[g][...] = jnp.sum(sum_ref[g * size : (g + 1) * size], axis=1)
        for copy in copies:
            copy.wait()

    terms = pltpu.VMEM((windows, tiles, 8, block), jnp.float32)
    return pl.pallas_call(
        body,
        in_specs=[full_smem()] + [full_vmem()] * 3,
        out_specs=[full_vmem()] * groups + [pl.BlockSpec(memory_space=pl.ANY)],
        out_shape=[jax.ShapeDtypeStruct((size, block), jnp.float32)] * groups
        + [jax.ShapeDtypeStruct((windows, block, rcv), jnp.float32)],
        scratch_shapes=[
            terms,
            terms,
            pltpu.VMEM((windows, rcv, block), jnp.bfloat16),
            pltpu.VMEM((windows, block, rcv), jnp.float32),
            pltpu.VMEM((shots, 8, block), jnp.float32),
            pltpu.SemaphoreType.DMA((chunks,)),
        ],
        compiler_params=params(),
        cost_estimate=pl.CostEstimate(flops=1, bytes_accessed=6 << 20, transcendentals=0),
        name="residual_and_energies",
    )(numbers, records, cuts, both)


def differences(arrived, cuts, numbers, capacity):
    owners, rows, block = arrived.shape
    rcv = rows // capacity
    tiles = rcv // 8
    count = owners * capacity
    none = cuts.shape[0] - 1

    def body(number_ref, in_ref, cut_ref, diff_ref, base_ref):
        def one_block(slot, _):
            low, high = number_ref[slot], number_ref[count + slot]

            @pl.when(high > low)
            def _():
                owner = slot // capacity
                start = pl.multiple_of((slot - owner * capacity) * rcv, rcv)
                coef = in_ref[owner, pl.ds(start, rcv), :].astype(jnp.float32)
                diff_ref[slot], base_ref[slot], _ = shot_terms(
                    coef.reshape(tiles, 8, block), cut_ref, low, high, none
                )

            return 0

        lax.fori_loop(0, count, one_block, 0)

    shape = jax.ShapeDtypeStruct((count, tiles, 8, block), jnp.float32)
    return pl.pallas_call(
        body,
        in_specs=[full_smem()] + [full_vmem()] * 2,
        out_specs=[full_vmem()] * 2,
        out_shape=[shape] * 2,
        compiler_params=params(),
        cost_estimate=pl.CostEstimate(flops=1, bytes_accessed=8 << 20, transcendentals=0),
        name="shot_differences",
    )(numbers, arrived, cuts)


def finish(diffs, bases, cuts, energies, thresholds, numbers, both, receivers):
    count, tiles, _, block = diffs.shape
    rcv = tiles * 8
    shot_dev = (numbers.shape[0] - 2 * count) // SHOT_BLK
    shots = cuts.shape[0] - 1 - shot_dev
    step = min(2, shot_dev)

    def body(number_ref, diff_ref, base_ref, cut_ref, thr_ref, both_ref, *refs):
        out_hbm, out_ref, sem = refs[-3:]
        energy = refs[0][...]
        for ref in refs[1:-3]:
            energy = energy + ref[...]
        seconds = thr_ref[...] * jnp.sqrt(energy / (SHOT_BLK * receivers) + epsilon)
        copies = []
        for at in range(0, shot_dev, step):
            for i in range(at, at + step):
                first = step_size * cut_ref[shots + i][None]
                cut = seconds[i : i + 1, :]
                parts = []
                for q in range(SHOT_BLK):
                    slot = number_ref[2 * count + i * SHOT_BLK + q]
                    value = diff_ref[slot] - jnp.minimum(jnp.maximum(base_ref[slot], -first), first)
                    value = value.reshape(rcv, block)
                    shrunk = value - jnp.minimum(jnp.maximum(value, -cut), cut)
                    parts.append(shrunk.astype(jnp.bfloat16))
                model = lax.dot_general(
                    both_ref[:, :block], jnp.concatenate(parts, axis=0), (((1,), (1,)), ((), ())),
                    preferred_element_type=jnp.float32,
                )
                for q in range(SHOT_BLK):
                    out_ref[i, q] = model[:, q * rcv : (q + 1) * rcv].astype(jnp.bfloat16)
            copy = pltpu.make_async_copy(
                out_ref.at[pl.ds(at, step)], out_hbm.at[pl.ds(at, step)], sem.at[at // step]
            )
            copy.start()
            copies.append(copy)
        for copy in copies:
            copy.wait()

    return pl.pallas_call(
        body,
        in_specs=[full_smem()] + [full_vmem()] * (5 + len(energies)),
        out_specs=pl.BlockSpec(memory_space=pl.ANY),
        out_shape=jax.ShapeDtypeStruct((shot_dev, SHOT_BLK, block, rcv), jnp.bfloat16),
        scratch_shapes=[
            pltpu.VMEM((shot_dev, SHOT_BLK, block, rcv), jnp.bfloat16),
            pltpu.SemaphoreType.DMA((shot_dev // step,)),
        ],
        compiler_params=params(),
        name="model_of_shots",
    )(numbers, diffs, bases, cuts, thresholds, both, *energies)


def over_receivers(values):
    if lax.axis_size("rcv") == 2:
        return [values, lax.ppermute(values, "rcv", [(0, 1), (1, 0)])]
    return [lax.psum(values.astype(jnp.float32), "rcv").astype(values.dtype)]


def rotate(values, stride, by, size):
    n = lax.axis_size("shot")
    pairs = []
    for i in range(n):
        place = (i // stride) % size
        pairs.append((i, i + ((place + by) % size - place) * stride))
    return lax.ppermute(values, "shot", pairs)


def local(record_data, offsets, thresholds):
    owners = lax.axis_size("shot")
    me = lax.axis_index("shot")
    windows, _, block, rcv = record_data.shape
    shots = offsets.shape[0]
    shot_dev = shots // owners
    pairs = shot_dev // 2
    pair_slots = min(pairs, owners // (SHOT_BLK + 1))
    capacity = (pairs + pair_slots - 1) // pair_slots
    receivers = rcv * lax.axis_size("rcv")

    high, low = split_bf16(jnp.asarray(cosine_table(block).T))
    both = jnp.concatenate([high, low], axis=1)
    records = record_data.reshape(windows, block, rcv)
    thr = thresholds[None, :]
    window_ids = jnp.arange(windows, dtype=jnp.int32)

    packed, energy = head(records, offsets, me, owners, capacity, both)
    packed, records, offsets, thr = lax.optimization_barrier((packed, records, offsets, thr))
    arrived = lax.all_to_all(packed, "shot", split_axis=0, concat_axis=0, tiled=True)

    near = min(4, owners)
    far = owners // near
    energy = jnp.concatenate([energy] + [rotate(energy, near, j, far) for j in range(1, far)])
    energy = jnp.concatenate([energy] + [rotate(energy, 1, j, near) for j in range(1, near)])
    energies = over_receivers(energy)
    back = jnp.arange(far, dtype=jnp.int32)[None, :]
    side = jnp.arange(near, dtype=jnp.int32)[:, None]
    origin = (me // near - back + far) % far * near + (me % near - side + near) % near
    energy_ids = (window_ids * owners + origin[:, :, None]).reshape(-1)

    index = jnp.arange(shots, dtype=jnp.int32)
    ahead = (offsets[None, :] < offsets[:, None]) | (
        (offsets[None, :] == offsets[:, None]) & (index[None, :] < index[:, None])
    )
    place = jnp.sum(ahead.astype(jnp.int32), axis=1)
    ordered = jnp.sum(jnp.where(place[None, :] == index[:, None], offsets[None, :], 0), axis=1)
    mine = lax.dynamic_slice(offsets, (me * shot_dev,), (shot_dev,))
    all_offsets = jnp.concatenate([ordered, mine])
    grid_ids = window_ids[None, :] * owners + jnp.arange(owners, dtype=jnp.int32)[:, None]
    hits = landed(energy_ids[None, :], all_offsets[:, None]).astype(jnp.bfloat16)

    def bounds(ids):
        below = jnp.sum((offsets < ids[..., None] - (SHOT_BLK - 1)).astype(jnp.int32), axis=-1)
        upto = jnp.sum((offsets <= ids[..., None]).astype(jnp.int32), axis=-1)
        return below, upto

    own_lows, own_highs = bounds(window_ids * owners + me)

    slot_ids = jnp.arange(capacity, dtype=jnp.int32)
    held = jnp.max(landed(grid_ids[:, :, None], mine).astype(jnp.int32), axis=2)
    before = (window_ids[:, None] < window_ids[None, :]).astype(jnp.int32)
    held_rank = jnp.sum(held[:, :, None] * before, axis=1)
    taken = (held_rank[:, None, :] == slot_ids[None, :, None]) & (held[:, None, :] > 0)
    held_ids = jnp.sum(jnp.where(taken, grid_ids[:, None, :], 0), axis=2)
    valid = jnp.sum(taken.astype(jnp.int32), axis=2)
    lows, highs = bounds(held_ids)
    lows, highs = lows * valid, highs * valid
    targets = mine[:, None] + jnp.arange(SHOT_BLK, dtype=jnp.int32)[None, :]
    slot_of = jnp.arange(owners, dtype=jnp.int32)[:, None] * capacity + held_rank
    slots = jnp.sum(
        jnp.where(targets[:, :, None, None] == grid_ids[None, None], slot_of[None, None], 0),
        axis=(2, 3),
    )

    numbers = jnp.concatenate([lows.reshape(-1), highs.reshape(-1), slots.reshape(-1)])
    group = index // shot_dev
    away = (group % near - me % near + near) % near * far
    away = (away + (group // near - me // near + far) % far) * shot_dev + index % shot_dev
    order = jnp.sum(jnp.where(place[None, :] == index[:, None], away[None, :], 0), axis=1)
    own_numbers = jnp.concatenate([own_lows, own_highs, order])

    cuts = cutoffs(energies, hits, thr, receivers)
    *landed_parts, residual = landed_energies(records, cuts, own_numbers, both, near)
    plane = [landed_parts[0]] + [rotate(landed_parts[j], 1, j, near) for j in range(1, near)]
    plane = sum(plane)
    plane = sum(over_receivers(plane))
    energies = [plane[:shot_dev]] + [
        rotate(plane[j * shot_dev : (j + 1) * shot_dev], near, j, far) for j in range(1, far)
    ]
    diffs, bases = differences(arrived, cuts, numbers, capacity)
    model = finish(diffs, bases, cuts, energies, thr, numbers, both, receivers)
    return (model, residual.reshape(windows, 1, block, rcv))


def solution(mesh):
    return jax.shard_map(
        local,
        mesh=mesh,
        in_specs=(P(None, "shot", None, "rcv"), P(), P()),
        out_specs=(P("shot", None, None, "rcv"), P(None, "shot", None, "rcv")),
        check_vma=False,
    )
```

```python
import jax
import jax.numpy as jnp
import numpy as np
from jax import lax
from jax.experimental import pallas as pl
from jax.experimental.pallas import tpu as pltpu
from jax.sharding import PartitionSpec as P

SHOT_BLK = 4
momentum = 0.5
epsilon = 1e-06
step_size = 1.0 + momentum
VMEM_BYTES = 16 * 1024 * 1024
HEAD_VMEM_BYTES = 60 * 1024 * 1024


def cosine_table(length):
    rows = np.arange(length, dtype=np.float64)[:, None]
    cols = np.arange(length, dtype=np.float64)[None, :]
    table = np.cos(np.pi * (cols + 0.5) * rows / length) * np.sqrt(2.0 / length)
    return np.where(rows == 0, table * np.sqrt(0.5), table).astype(np.float32)


def split_bf16(values):
    high = values.astype(jnp.bfloat16)
    low = (values - high.astype(jnp.float32)).astype(jnp.bfloat16)
    return high, low


def full_vmem():
    return pl.BlockSpec(memory_space=pltpu.VMEM)


def full_smem():
    return pl.BlockSpec(memory_space=pltpu.SMEM)


def params(vmem=VMEM_BYTES):
    return pltpu.CompilerParams(vmem_limit_bytes=vmem)


def forward(both, values):
    block = values.shape[0]
    parts = lax.dot_general(
        values, both, (((0,), (0,)), ((), ())), preferred_element_type=jnp.float32
    )
    return parts[:, :block] + parts[:, block:]


def backward(both, coefficients):
    doubled = jnp.concatenate([coefficients, coefficients], axis=1)
    return lax.dot_general(
        both, doubled, (((1,), (1,)), ((), ())), preferred_element_type=jnp.float32
    )


def landed(ids, offsets):
    lag = ids - offsets
    return (lag >= 0) & (lag < SHOT_BLK)


def head(records, offsets, me, owners, capacity, both):
    windows, block, rcv = records.shape
    shots = offsets.shape[0]
    shot_dev = shots // owners
    chunk = 8
    chunks = windows // chunk
    f32, bf16 = jnp.float32, jnp.bfloat16

    def body(
        me_ref, off_hbm, rec_hbm, both_hbm, out_ref, energy_hbm,
        off_ref, rec_ref, both_ref, sent_ref, energy_ref, table_ref, table_smem,
        small_sem, rec_sem, out_sem,
    ):
        get_off = pltpu.make_async_copy(off_hbm, off_ref, small_sem.at[0])
        get_both = pltpu.make_async_copy(both_hbm, both_ref, small_sem.at[1])
        get_rec = [
            pltpu.make_async_copy(
                rec_hbm.at[pl.ds(c * chunk, chunk)],
                rec_ref.at[pl.ds(c * chunk, chunk)],
                rec_sem.at[c],
            )
            for c in range(chunks)
        ]
        get_off.start()
        get_both.start()
        for copy in get_rec:
            copy.start()
        get_off.wait()

        ids = lax.broadcasted_iota(jnp.int32, (windows, shots), 0) * owners + me_ref[0]
        hits = jnp.where(landed(ids, off_ref[...]), 1.0, 0.0)
        cover = jnp.sum(hits, axis=1, keepdims=True)
        scale = 1.0 / jnp.maximum(cover, 1.0)

        shot = lax.broadcasted_iota(jnp.int32, (shots, owners), 0)
        first = lax.broadcasted_iota(jnp.int32, (shots, owners), 1) * shot_dev
        member = jnp.where((shot >= first) & (shot < first + shot_dev), 1.0, 0.0)
        counts = jnp.dot(hits.astype(bf16), member.astype(bf16), preferred_element_type=f32)
        present = jnp.where(counts > 0.5, 1.0, 0.0)
        after = lax.broadcasted_iota(jnp.int32, (windows, windows), 0)
        before = lax.broadcasted_iota(jnp.int32, (windows, windows), 1)
        lower = jnp.where(before < after, 1.0, 0.0)
        rank = jnp.dot(lower.astype(bf16), present.astype(bf16), preferred_element_type=f32)
        rank = rank.astype(jnp.int32)
        window = lax.broadcasted_iota(jnp.int32, (windows, owners), 0)
        for i in range(capacity):
            here = (rank == i) & (present > 0.5)
            table_ref[i : i + 1, :owners] = jnp.sum(
                jnp.where(here, window, 0), axis=0, keepdims=True
            )
        put_table = pltpu.make_async_copy(table_ref, table_smem, small_sem.at[2])
        put_table.start()

        get_both.wait()
        rows = []
        for c in range(chunks):
            get_rec[c].wait()
            for w in range(c * chunk, (c + 1) * chunk):
                spread = (rec_ref[w] * scale[w : w + 1, 0:1]).astype(bf16)
                coef = forward(both_ref[...], spread)
                sent_ref[w] = coef.astype(bf16)
                rows.append(jnp.sum(coef * coef, axis=0, keepdims=True))

        energy_ref[...] = jnp.concatenate(rows, axis=0).astype(bf16)
        put_energy = pltpu.make_async_copy(energy_ref, energy_hbm, small_sem.at[3])
        put_energy.start()
        put_table.wait()

        def send(h, i):
            return pltpu.make_async_copy(
                sent_ref.at[table_smem[i, h]],
                out_ref.at[h, pl.ds(i * rcv, rcv), :],
                out_sem.at[h * capacity + i],
            )

        for h in range(owners):
            for i in range(capacity):
                send(h, i).start()
        for h in range(owners):
            for i in range(capacity):
                send(h, i).wait()
        put_energy.wait()

    hbm = pl.BlockSpec(memory_space=pltpu.HBM)
    table_shape = (8, 128)
    return pl.pallas_call(
        body,
        in_specs=[full_smem(), hbm, hbm, hbm],
        out_specs=[pl.BlockSpec(memory_space=pl.ANY)] * 2,
        out_shape=[
            jax.ShapeDtypeStruct((owners, capacity * rcv, block), bf16),
            jax.ShapeDtypeStruct((windows, block), bf16),
        ],
        scratch_shapes=[
            pltpu.VMEM((1, shots), jnp.int32),
            pltpu.VMEM((windows, block, rcv), f32),
            pltpu.VMEM((block, 2 * block), bf16),
            pltpu.VMEM((windows, rcv, block), bf16),
            pltpu.VMEM((windows, block), bf16),
            pltpu.VMEM(table_shape, jnp.int32),
            pltpu.SMEM(table_shape, jnp.int32),
            pltpu.SemaphoreType.DMA((4,)),
            pltpu.SemaphoreType.DMA((chunks,)),
            pltpu.SemaphoreType.DMA((owners * capacity,)),
        ],
        compiler_params=params(HEAD_VMEM_BYTES),
        name="pack_coefficients",
    )(me[None], offsets[None, :], records, both)


def clipped_sum(coef, cut_ref, low, high, none):
    size = jnp.abs(coef)
    peel, unroll = 6, 2

    def term(row):
        return jnp.minimum(size, cut_ref[jnp.where(row < high, row, none)][None])

    total = term(low)
    for u in range(1, peel):
        total = total + term(low + u)

    def add(j, total):
        for u in range(unroll):
            total = total + term(low + peel + j * unroll + u)
        return total

    left = jnp.maximum(high - low - peel, 0)
    total = lax.fori_loop(0, lax.div(left + unroll - 1, unroll), add, total)
    return jnp.where(coef < 0, -total, total)


def shot_terms(coef, cut_ref, low, high, none):
    clipped = clipped_sum(coef, cut_ref, low, high, none)
    many = jnp.full((1, 8, coef.shape[2]), (high - low).astype(jnp.float32))
    scale = step_size / jnp.maximum(many, 1.0)
    diff = (1.0 + step_size - scale * many) * coef + scale * clipped
    return diff, step_size * coef, many * coef - clipped


def landed_energies(records, energies, hits, thresholds, numbers, both, groups, receivers):
    windows, block, rcv = records.shape
    tiles = rcv // 8
    none = hits.shape[0]
    shots = numbers.shape[0] - 2 * windows
    size = shots // groups

    def body(number_ref, rec_hbm, hit_ref, thr_ref, both_ref, *refs):
        refs, scratch = refs[:-6], refs[-6:]
        cuts_ref, rec_ref, diff_ref, base_ref, sum_ref, sem = scratch
        part_refs, (cut_ref, *energy_refs, shrunk_ref) = (
            refs[: len(energies)],
            refs[len(energies) :],
        )
        get_rec = pltpu.make_async_copy(rec_hbm, rec_ref, sem)
        get_rec.start()
        energy = jnp.concatenate([ref[...] for ref in part_refs], axis=0)
        sums = jnp.dot(hit_ref[...], energy, preferred_element_type=jnp.float32)
        cuts_ref[...] = thr_ref[...] * jnp.sqrt(sums / (SHOT_BLK * receivers) + epsilon)

        def widen(i, _):
            at = pl.multiple_of(i * 8, 8)
            cut_ref[pl.ds(at, 8)] = jnp.broadcast_to(
                cuts_ref[pl.ds(at, 8), :][:, None, :], (8, 8, block)
            )
            return 0

        lax.fori_loop(0, none // 8, widen, 0, unroll=2)
        cut_ref[none] = jnp.zeros((8, block), jnp.float32)
        sum_ref[...] = jnp.zeros_like(sum_ref)
        get_rec.wait()
        for w in range(windows):
            cover = (number_ref[windows + w] - number_ref[w]).astype(jnp.float32)
            scale = 1.0 / jnp.maximum(jnp.full((1, rcv), cover), 1.0)
            spread = (rec_ref[w] * scale).astype(jnp.bfloat16)
            base_ref[w] = forward(both_ref[...], spread).reshape(tiles, 8, block)

        def one_window(w, _):
            low, high = number_ref[w], number_ref[windows + w]
            diff_ref[w], base_ref[w], shrunk = shot_terms(base_ref[w], cut_ref, low, high, none)
            shrunk_ref[w] = shrunk.reshape(rcv, block).astype(jnp.bfloat16)
            return 0

        lax.fori_loop(0, windows, one_window, 0)
        def energies_of_window(w, _):
            diff, base = diff_ref[w], base_ref[w]

            def one_shot(row, _):
                cut = step_size * cut_ref[row][None]
                value = diff - jnp.minimum(jnp.maximum(base, -cut), cut)
                sum_ref[number_ref[2 * windows + row]] = jnp.sum(value * value, axis=0)
                return 0

            lax.fori_loop(number_ref[w], number_ref[windows + w], one_shot, 0)
            return 0

        lax.fori_loop(0, windows, energies_of_window, 0)
        for g in range(groups):
            energy_refs[g][...] = jnp.sum(sum_ref[g * size : (g + 1) * size], axis=1)

    terms = pltpu.VMEM((windows, tiles, 8, block), jnp.float32)
    return pl.pallas_call(
        body,
        in_specs=[full_smem(), pl.BlockSpec(memory_space=pltpu.HBM)]
        + [full_vmem()] * (3 + len(energies)),
        out_specs=[full_vmem()] * (groups + 2),
        out_shape=[jax.ShapeDtypeStruct((none + 1, 8, block), jnp.float32)]
        + [jax.ShapeDtypeStruct((size, block), jnp.float32)] * groups
        + [jax.ShapeDtypeStruct((windows, rcv, block), jnp.bfloat16)],
        scratch_shapes=[
            pltpu.VMEM((none, block), jnp.float32),
            pltpu.VMEM((windows, block, rcv), jnp.float32),
            terms,
            terms,
            pltpu.VMEM((shots, 8, block), jnp.float32),
            pltpu.SemaphoreType.DMA,
        ],
        compiler_params=params(),
        cost_estimate=pl.CostEstimate(flops=1, bytes_accessed=6 << 20, transcendentals=0),
        name="second_energies",
    )(numbers, records, hits, thresholds, both, *energies)


def remainder(records, sums, both):
    windows, block, rcv = records.shape
    chunk = 4
    chunks = windows // chunk

    def body(rec_hbm, sum_ref, both_ref, out_hbm, rec_ref, out_ref, sem):
        def copy(c, source, target, k):
            part = pl.ds(c * chunk, chunk)
            return pltpu.make_async_copy(source.at[part], target.at[part], sem.at[k])

        for c in range(chunks):
            copy(c, rec_hbm, rec_ref, c).start()
        for c in range(chunks):
            sums = sum_ref[c * chunk : (c + 1) * chunk].reshape(chunk * rcv, block)
            blended = backward(both_ref[...], sums)
            copy(c, rec_hbm, rec_ref, c).wait()
            for w in range(chunk):
                at = c * chunk + w
                out_ref[at] = rec_ref[at] - step_size * blended[:, w * rcv : (w + 1) * rcv]
            copy(c, out_ref, out_hbm, chunks + c).start()
        for c in range(chunks):
            copy(c, out_ref, out_hbm, chunks + c).wait()

    own = pltpu.VMEM((windows, block, rcv), jnp.float32)
    return pl.pallas_call(
        body,
        in_specs=[pl.BlockSpec(memory_space=pltpu.HBM), full_vmem(), full_vmem()],
        out_specs=pl.BlockSpec(memory_space=pl.ANY),
        out_shape=jax.ShapeDtypeStruct((windows, block, rcv), jnp.float32),
        scratch_shapes=[own, own, pltpu.SemaphoreType.DMA((2 * chunks,))],
        compiler_params=params(),
        cost_estimate=pl.CostEstimate(flops=1, bytes_accessed=4 << 20, transcendentals=0),
        name="residual_of_records",
    )(records, sums, both)


def differences(arrived, cuts, numbers, capacity):
    owners, rows, block = arrived.shape
    rcv = rows // capacity
    tiles = rcv // 8
    count = owners * capacity
    none = cuts.shape[0] - 1

    def body(number_ref, in_ref, cut_ref, diff_ref, base_ref):
        def one_block(place):
            slot = number_ref[place]
            owner = slot // capacity
            start = pl.multiple_of((slot - owner * capacity) * rcv, rcv)
            coef = in_ref[owner, pl.ds(start, rcv), :].astype(jnp.float32)
            diff_ref[slot], base_ref[slot], _ = shot_terms(
                coef.reshape(tiles, 8, block), cut_ref,
                number_ref[count + slot], number_ref[2 * count + slot], none,
            )

        def two_blocks(i, _):
            one_block(2 * i)
            one_block(2 * i + 1)
            return 0

        lax.fori_loop(0, number_ref[number_ref.shape[0] - 1], two_blocks, 0)

    shape = jax.ShapeDtypeStruct((count, tiles, 8, block), jnp.float32)
    return pl.pallas_call(
        body,
        in_specs=[full_smem()] + [full_vmem()] * 2,
        out_specs=[full_vmem()] * 2,
        out_shape=[shape] * 2,
        compiler_params=params(),
        cost_estimate=pl.CostEstimate(flops=1, bytes_accessed=8 << 20, transcendentals=0),
        name="shot_differences",
    )(numbers, arrived, cuts)


def finish(diffs, bases, cuts, energies, thresholds, numbers, both, receivers):
    count, tiles, _, block = diffs.shape
    rcv = tiles * 8
    shot_dev = (numbers.shape[0] - 1 - 3 * count) // SHOT_BLK
    shots = cuts.shape[0] - 1 - shot_dev
    step = min(2, shot_dev)

    def body(number_ref, diff_ref, base_ref, cut_ref, thr_ref, both_ref, *refs):
        out_hbm, out_ref, sem = refs[-3:]
        energy = refs[0][...]
        for ref in refs[1:-3]:
            energy = energy + ref[...]
        seconds = thr_ref[...] * jnp.sqrt(energy / (SHOT_BLK * receivers) + epsilon)
        copies = []
        for at in range(0, shot_dev, step):
            for i in range(at, at + step):
                first = step_size * cut_ref[shots + i][None]
                cut = seconds[i : i + 1, :]
                parts = []
                for q in range(SHOT_BLK):
                    slot = number_ref[3 * count + i * SHOT_BLK + q]
                    value = diff_ref[slot] - jnp.minimum(jnp.maximum(base_ref[slot], -first), first)
                    value = value.reshape(rcv, block)
                    shrunk = value - jnp.minimum(jnp.maximum(value, -cut), cut)
                    parts.append(shrunk.astype(jnp.bfloat16))
                model = lax.dot_general(
                    both_ref[:, :block], jnp.concatenate(parts, axis=0), (((1,), (1,)), ((), ())),
                    preferred_element_type=jnp.float32,
                )
                for q in range(SHOT_BLK):
                    out_ref[i, q] = model[:, q * rcv : (q + 1) * rcv].astype(jnp.bfloat16)
            copy = pltpu.make_async_copy(
                out_ref.at[pl.ds(at, step)], out_hbm.at[pl.ds(at, step)], sem.at[at // step]
            )
            copy.start()
            copies.append(copy)
        for copy in copies:
            copy.wait()

    return pl.pallas_call(
        body,
        in_specs=[full_smem()] + [full_vmem()] * (5 + len(energies)),
        out_specs=pl.BlockSpec(memory_space=pl.ANY),
        out_shape=jax.ShapeDtypeStruct((shot_dev, SHOT_BLK, block, rcv), jnp.bfloat16),
        scratch_shapes=[
            pltpu.VMEM((shot_dev, SHOT_BLK, block, rcv), jnp.bfloat16),
            pltpu.SemaphoreType.DMA((shot_dev // step,)),
        ],
        compiler_params=params(),
        name="model_of_shots",
    )(numbers, diffs, bases, cuts, thresholds, both, *energies)


def over_receivers(values):
    if lax.axis_size("rcv") == 2:
        return [values, lax.ppermute(values, "rcv", [(0, 1), (1, 0)])]
    return [lax.psum(values.astype(jnp.float32), "rcv").astype(values.dtype)]


def rotate(values, stride, by, size):
    n = lax.axis_size("shot")
    pairs = []
    for i in range(n):
        place = (i // stride) % size
        pairs.append((i, i + ((place + by) % size - place) * stride))
    return lax.ppermute(values, "shot", pairs)


def local(record_data, offsets, thresholds):
    owners = lax.axis_size("shot")
    me = lax.axis_index("shot")
    windows, _, block, rcv = record_data.shape
    shots = offsets.shape[0]
    shot_dev = shots // owners
    pairs = shot_dev // 2
    pair_slots = min(pairs, owners // (SHOT_BLK + 1))
    capacity = (pairs + pair_slots - 1) // pair_slots
    receivers = rcv * lax.axis_size("rcv")

    high, low = split_bf16(jnp.asarray(cosine_table(block).T))
    both = jnp.concatenate([high, low], axis=1)
    records = record_data.reshape(windows, block, rcv)
    thr = thresholds[None, :]
    window_ids = jnp.arange(windows, dtype=jnp.int32)

    packed, energy = head(records, offsets, me, owners, capacity, both)
    packed, records, offsets, thr = lax.optimization_barrier((packed, records, offsets, thr))
    arrived = lax.all_to_all(packed, "shot", split_axis=0, concat_axis=0, tiled=True)

    near = min(4, owners)
    far = owners // near
    energy = jnp.concatenate([energy] + [rotate(energy, near, j, far) for j in range(1, far)])
    energy, offsets = lax.optimization_barrier((energy, offsets))
    energy = sum(part.astype(jnp.float32) for part in over_receivers(energy)).astype(jnp.bfloat16)
    energies = [energy] + [rotate(energy, 1, j, near) for j in range(1, near)]
    back = jnp.arange(far, dtype=jnp.int32)[None, :]
    side = jnp.arange(near, dtype=jnp.int32)[:, None]
    origin = (me // near - back + far) % far * near + (me % near - side + near) % near
    energy_ids = (window_ids * owners + origin[:, :, None]).reshape(-1)

    index = jnp.arange(shots, dtype=jnp.int32)
    ahead = (offsets[None, :] < offsets[:, None]) | (
        (offsets[None, :] == offsets[:, None]) & (index[None, :] < index[:, None])
    )
    place = jnp.sum(ahead.astype(jnp.int32), axis=1)
    ordered = jnp.sum(jnp.where(place[None, :] == index[:, None], offsets[None, :], 0), axis=1)
    mine = lax.dynamic_slice(offsets, (me * shot_dev,), (shot_dev,))
    all_offsets = jnp.concatenate([ordered, mine])
    grid_ids = window_ids[None, :] * owners + jnp.arange(owners, dtype=jnp.int32)[:, None]
    hits = landed(energy_ids[None, :], all_offsets[:, None]).astype(jnp.bfloat16)

    def bounds(ids):
        below = jnp.sum((offsets < ids[..., None] - (SHOT_BLK - 1)).astype(jnp.int32), axis=-1)
        upto = jnp.sum((offsets <= ids[..., None]).astype(jnp.int32), axis=-1)
        return below, upto

    own_lows, own_highs = bounds(window_ids * owners + me)

    slot_ids = jnp.arange(capacity, dtype=jnp.int32)
    held = jnp.max(landed(grid_ids[:, :, None], mine).astype(jnp.int32), axis=2)
    before = (window_ids[:, None] < window_ids[None, :]).astype(jnp.int32)
    held_rank = jnp.sum(held[:, :, None] * before, axis=1)
    taken = (held_rank[:, None, :] == slot_ids[None, :, None]) & (held[:, None, :] > 0)
    held_ids = jnp.sum(jnp.where(taken, grid_ids[:, None, :], 0), axis=2)
    valid = jnp.sum(taken.astype(jnp.int32), axis=2)
    lows, highs = bounds(held_ids)
    lows, highs = lows * valid, highs * valid
    targets = mine[:, None] + jnp.arange(SHOT_BLK, dtype=jnp.int32)[None, :]
    slot_of = jnp.arange(owners, dtype=jnp.int32)[:, None] * capacity + held_rank
    slots = jnp.sum(
        jnp.where(targets[:, :, None, None] == grid_ids[None, None], slot_of[None, None], 0),
        axis=(2, 3),
    )

    filled = valid.reshape(-1)
    count = jnp.arange(filled.shape[0], dtype=jnp.int32)
    nth = jnp.sum(jnp.where(count[None, :] < count[:, None], filled[None, :], 0), axis=1)
    chosen = (nth[None, :] == count[:, None]) & (filled[None, :] > 0)
    chosen = jnp.sum(jnp.where(chosen, count[None, :], 0), axis=1)
    half = (jnp.sum(filled) + 1) // 2
    numbers = jnp.concatenate(
        [chosen, lows.reshape(-1), highs.reshape(-1), slots.reshape(-1), half[None]]
    )
    group = index // shot_dev
    away = (group % near - me % near + near) % near * far
    away = (away + (group // near - me // near + far) % far) * shot_dev + index % shot_dev
    order = jnp.sum(jnp.where(place[None, :] == index[:, None], away[None, :], 0), axis=1)
    own_numbers = jnp.concatenate([own_lows, own_highs, order])

    records = pltpu.with_memory_space_constraint(records, pltpu.HBM)
    hits, own_numbers, numbers = lax.optimization_barrier((hits, own_numbers, numbers))
    cuts, *landed_parts, sums = landed_energies(
        records, energies, hits, thr, own_numbers, both, near, receivers
    )
    residual = remainder(records, sums, both)
    plane = [landed_parts[0]] + [rotate(landed_parts[j], 1, j, near) for j in range(1, near)]
    *plane, residual = lax.optimization_barrier((*plane, residual))
    plane = sum(plane)
    plane = sum(over_receivers(plane))
    energies = [plane[:shot_dev]] + [
        rotate(plane[j * shot_dev : (j + 1) * shot_dev], near, j, far) for j in range(1, far)
    ]
    diffs, bases = differences(arrived, cuts, numbers, capacity)
    model = finish(diffs, bases, cuts, energies, thr, numbers, both, receivers)
    return (model, residual.reshape(windows, 1, block, rcv))


def solution(mesh):
    return jax.shard_map(
        local,
        mesh=mesh,
        in_specs=(P(None, "shot", None, "rcv"), P(), P()),
        out_specs=(P("shot", None, None, "rcv"), P(None, "shot", None, "rcv")),
        check_vma=False,
    )
```

```python
import jax
import jax.numpy as jnp
import numpy as np
from jax import lax
from jax.experimental import pallas as pl
from jax.experimental.pallas import tpu as pltpu
from jax.sharding import PartitionSpec as P

SHOT_BLK = 4
momentum = 0.5
epsilon = 1e-06
step_size = 1.0 + momentum
VMEM_BYTES = 16 * 1024 * 1024
HEAD_VMEM_BYTES = 60 * 1024 * 1024


def cosine_table(length):
    rows = np.arange(length, dtype=np.float64)[:, None]
    cols = np.arange(length, dtype=np.float64)[None, :]
    table = np.cos(np.pi * (cols + 0.5) * rows / length) * np.sqrt(2.0 / length)
    return np.where(rows == 0, table * np.sqrt(0.5), table).astype(np.float32)


def split_bf16(values):
    high = values.astype(jnp.bfloat16)
    low = (values - high.astype(jnp.float32)).astype(jnp.bfloat16)
    return high, low


def full_vmem():
    return pl.BlockSpec(memory_space=pltpu.VMEM)


def full_smem():
    return pl.BlockSpec(memory_space=pltpu.SMEM)


def params(vmem=VMEM_BYTES):
    return pltpu.CompilerParams(vmem_limit_bytes=vmem)


def forward(both, values):
    block = values.shape[0]
    parts = lax.dot_general(
        values, both, (((0,), (0,)), ((), ())), preferred_element_type=jnp.float32
    )
    return parts[:, :block] + parts[:, block:]


def backward(both, coefficients):
    doubled = jnp.concatenate([coefficients, coefficients], axis=1)
    return lax.dot_general(
        both, doubled, (((1,), (1,)), ((), ())), preferred_element_type=jnp.float32
    )


def landed(ids, offsets):
    lag = ids - offsets
    return (lag >= 0) & (lag < SHOT_BLK)


def head(records, offsets, me, owners, capacity, both):
    windows, block, rcv = records.shape
    shots = offsets.shape[0]
    shot_dev = shots // owners
    chunk = 8
    chunks = windows // chunk
    f32, bf16 = jnp.float32, jnp.bfloat16

    def body(
        me_ref, off_hbm, rec_hbm, both_hbm, out_ref, energy_hbm,
        off_ref, rec_ref, both_ref, sent_ref, energy_ref, table_ref, table_smem,
        small_sem, rec_sem, out_sem,
    ):
        get_off = pltpu.make_async_copy(off_hbm, off_ref, small_sem.at[0])
        get_both = pltpu.make_async_copy(both_hbm, both_ref, small_sem.at[1])
        get_rec = [
            pltpu.make_async_copy(
                rec_hbm.at[pl.ds(c * chunk, chunk)],
                rec_ref.at[pl.ds(c * chunk, chunk)],
                rec_sem.at[c],
            )
            for c in range(chunks)
        ]
        get_off.start()
        get_both.start()
        for copy in get_rec:
            copy.start()
        get_off.wait()

        ids = lax.broadcasted_iota(jnp.int32, (windows, shots), 0) * owners + me_ref[0]
        hits = jnp.where(landed(ids, off_ref[...]), 1.0, 0.0)
        cover = jnp.sum(hits, axis=1, keepdims=True)
        scale = 1.0 / jnp.maximum(cover, 1.0)

        shot = lax.broadcasted_iota(jnp.int32, (shots, owners), 0)
        first = lax.broadcasted_iota(jnp.int32, (shots, owners), 1) * shot_dev
        member = jnp.where((shot >= first) & (shot < first + shot_dev), 1.0, 0.0)
        counts = jnp.dot(hits.astype(bf16), member.astype(bf16), preferred_element_type=f32)
        present = jnp.where(counts > 0.5, 1.0, 0.0)
        after = lax.broadcasted_iota(jnp.int32, (windows, windows), 0)
        before = lax.broadcasted_iota(jnp.int32, (windows, windows), 1)
        lower = jnp.where(before < after, 1.0, 0.0)
        rank = jnp.dot(lower.astype(bf16), present.astype(bf16), preferred_element_type=f32)
        rank = rank.astype(jnp.int32)
        window = lax.broadcasted_iota(jnp.int32, (windows, owners), 0)
        for i in range(capacity):
            here = (rank == i) & (present > 0.5)
            table_ref[i : i + 1, :owners] = jnp.sum(
                jnp.where(here, window, 0), axis=0, keepdims=True
            )
        put_table = pltpu.make_async_copy(table_ref, table_smem, small_sem.at[2])
        put_table.start()

        get_both.wait()
        rows = []
        for c in range(chunks):
            get_rec[c].wait()
            for w in range(c * chunk, (c + 1) * chunk):
                spread = (rec_ref[w] * scale[w : w + 1, 0:1]).astype(bf16)
                coef = forward(both_ref[...], spread)
                sent_ref[w] = coef.astype(bf16)
                rows.append(jnp.sum(coef * coef, axis=0, keepdims=True))

        energy_ref[...] = jnp.concatenate(rows, axis=0).astype(bf16)
        put_energy = pltpu.make_async_copy(energy_ref, energy_hbm, small_sem.at[3])
        put_energy.start()
        put_table.wait()

        def send(h, i):
            return pltpu.make_async_copy(
                sent_ref.at[table_smem[i, h]],
                out_ref.at[h, pl.ds(i * rcv, rcv), :],
                out_sem.at[h * capacity + i],
            )

        for h in range(owners):
            for i in range(capacity):
                send(h, i).start()
        for h in range(owners):
            for i in range(capacity):
                send(h, i).wait()
        put_energy.wait()

    hbm = pl.BlockSpec(memory_space=pltpu.HBM)
    table_shape = (8, 128)
    return pl.pallas_call(
        body,
        in_specs=[full_smem(), hbm, hbm, hbm],
        out_specs=[pl.BlockSpec(memory_space=pl.ANY)] * 2,
        out_shape=[
            jax.ShapeDtypeStruct((owners, capacity * rcv, block), bf16),
            jax.ShapeDtypeStruct((windows, block), bf16),
        ],
        scratch_shapes=[
            pltpu.VMEM((1, shots), jnp.int32),
            pltpu.VMEM((windows, block, rcv), f32),
            pltpu.VMEM((block, 2 * block), bf16),
            pltpu.VMEM((windows, rcv, block), bf16),
            pltpu.VMEM((windows, block), bf16),
            pltpu.VMEM(table_shape, jnp.int32),
            pltpu.SMEM(table_shape, jnp.int32),
            pltpu.SemaphoreType.DMA((4,)),
            pltpu.SemaphoreType.DMA((chunks,)),
            pltpu.SemaphoreType.DMA((owners * capacity,)),
        ],
        compiler_params=params(HEAD_VMEM_BYTES),
        name="pack_coefficients",
    )(me[None], offsets[None, :], records, both)


def clipped_sum(coef, cut_ref, low, high, none):
    size = jnp.abs(coef)
    peel, unroll = 6, 2

    def term(row):
        return jnp.minimum(size, cut_ref[jnp.where(row < high, row, none)][None])

    total = term(low)
    for u in range(1, peel):
        total = total + term(low + u)

    def add(j, total):
        for u in range(unroll):
            total = total + term(low + peel + j * unroll + u)
        return total

    left = jnp.maximum(high - low - peel, 0)
    total = lax.fori_loop(0, lax.div(left + unroll - 1, unroll), add, total)
    return jnp.where(coef < 0, -total, total)


def shot_terms(coef, cut_ref, low, high, none):
    clipped = clipped_sum(coef, cut_ref, low, high, none)
    many = jnp.full((1, 8, coef.shape[2]), (high - low).astype(jnp.float32))
    scale = step_size / jnp.maximum(many, 1.0)
    diff = (1.0 + step_size - scale * many) * coef + scale * clipped
    return diff, step_size * coef, many * coef - clipped


def landed_energies(records, energies, hits, thresholds, numbers, both, groups, receivers):
    windows, block, rcv = records.shape
    tiles = rcv // 8
    none = hits.shape[0]
    shots = numbers.shape[0] - 2 * windows
    size = shots // groups

    def body(number_ref, rec_hbm, hit_ref, thr_ref, both_ref, *refs):
        refs, scratch = refs[:-6], refs[-6:]
        cuts_ref, rec_ref, diff_ref, base_ref, sum_ref, sem = scratch
        part_refs, (cut_ref, *energy_refs, shrunk_ref) = (
            refs[: len(energies)],
            refs[len(energies) :],
        )
        get_rec = pltpu.make_async_copy(rec_hbm, rec_ref, sem)
        get_rec.start()
        energy = jnp.concatenate([ref[...] for ref in part_refs], axis=0)
        sums = jnp.dot(hit_ref[...], energy, preferred_element_type=jnp.float32)
        cuts_ref[...] = thr_ref[...] * jnp.sqrt(sums / (SHOT_BLK * receivers) + epsilon)

        def widen(i, _):
            at = pl.multiple_of(i * 8, 8)
            cut_ref[pl.ds(at, 8)] = jnp.broadcast_to(
                cuts_ref[pl.ds(at, 8), :][:, None, :], (8, 8, block)
            )
            return 0

        lax.fori_loop(0, none // 8, widen, 0, unroll=2)
        cut_ref[none] = jnp.zeros((8, block), jnp.float32)
        sum_ref[...] = jnp.zeros_like(sum_ref)
        get_rec.wait()
        for w in range(windows):
            cover = (number_ref[windows + w] - number_ref[w]).astype(jnp.float32)
            scale = 1.0 / jnp.maximum(jnp.full((1, rcv), cover), 1.0)
            spread = (rec_ref[w] * scale).astype(jnp.bfloat16)
            base_ref[w] = forward(both_ref[...], spread).reshape(tiles, 8, block)

        def one_window(w, _):
            low, high = number_ref[w], number_ref[windows + w]
            diff_ref[w], base_ref[w], shrunk = shot_terms(base_ref[w], cut_ref, low, high, none)
            shrunk_ref[w] = shrunk.reshape(rcv, block).astype(jnp.bfloat16)
            return 0

        lax.fori_loop(0, windows, one_window, 0)
        def energies_of_window(w, _):
            diff, base = diff_ref[w], base_ref[w]

            def one_shot(row, _):
                cut = step_size * cut_ref[row][None]
                value = diff - jnp.minimum(jnp.maximum(base, -cut), cut)
                sum_ref[number_ref[2 * windows + row]] = jnp.sum(value * value, axis=0)
                return 0

            lax.fori_loop(number_ref[w], number_ref[windows + w], one_shot, 0)
            return 0

        lax.fori_loop(0, windows, energies_of_window, 0)
        for g in range(groups):
            energy_refs[g][...] = jnp.sum(sum_ref[g * size : (g + 1) * size], axis=1)

    terms = pltpu.VMEM((windows, tiles, 8, block), jnp.float32)
    return pl.pallas_call(
        body,
        in_specs=[full_smem(), pl.BlockSpec(memory_space=pltpu.HBM)]
        + [full_vmem()] * (3 + len(energies)),
        out_specs=[full_vmem()] * (groups + 2),
        out_shape=[jax.ShapeDtypeStruct((none + 1, 8, block), jnp.float32)]
        + [jax.ShapeDtypeStruct((size, block), jnp.float32)] * groups
        + [jax.ShapeDtypeStruct((windows, rcv, block), jnp.bfloat16)],
        scratch_shapes=[
            pltpu.VMEM((none, block), jnp.float32),
            pltpu.VMEM((windows, block, rcv), jnp.float32),
            terms,
            terms,
            pltpu.VMEM((shots, 8, block), jnp.float32),
            pltpu.SemaphoreType.DMA,
        ],
        compiler_params=params(),
        cost_estimate=pl.CostEstimate(flops=1, bytes_accessed=6 << 20, transcendentals=0),
        name="second_energies",
    )(numbers, records, hits, thresholds, both, *energies)


def remainder(records, sums, both):
    windows, block, rcv = records.shape
    chunk = 4
    chunks = windows // chunk

    def body(rec_hbm, sum_ref, both_ref, out_hbm, rec_ref, out_ref, sem):
        def copy(c, source, target, k):
            part = pl.ds(c * chunk, chunk)
            return pltpu.make_async_copy(source.at[part], target.at[part], sem.at[k])

        for c in range(chunks):
            copy(c, rec_hbm, rec_ref, c).start()
        for c in range(chunks):
            sums = sum_ref[c * chunk : (c + 1) * chunk].reshape(chunk * rcv, block)
            blended = backward(both_ref[...], sums)
            copy(c, rec_hbm, rec_ref, c).wait()
            for w in range(chunk):
                at = c * chunk + w
                out_ref[at] = rec_ref[at] - step_size * blended[:, w * rcv : (w + 1) * rcv]
            copy(c, out_ref, out_hbm, chunks + c).start()
        for c in range(chunks):
            copy(c, out_ref, out_hbm, chunks + c).wait()

    own = pltpu.VMEM((windows, block, rcv), jnp.float32)
    return pl.pallas_call(
        body,
        in_specs=[pl.BlockSpec(memory_space=pltpu.HBM), full_vmem(), full_vmem()],
        out_specs=pl.BlockSpec(memory_space=pl.ANY),
        out_shape=jax.ShapeDtypeStruct((windows, block, rcv), jnp.float32),
        scratch_shapes=[own, own, pltpu.SemaphoreType.DMA((2 * chunks,))],
        compiler_params=params(),
        cost_estimate=pl.CostEstimate(flops=1, bytes_accessed=4 << 20, transcendentals=0),
        name="residual_of_records",
    )(records, sums, both)


def differences(arrived, cuts, numbers, capacity):
    owners, rows, block = arrived.shape
    rcv = rows // capacity
    tiles = rcv // 8
    count = owners * capacity
    none = cuts.shape[0] - 1

    def body(number_ref, in_ref, cut_ref, diff_ref, base_ref):
        def one_block(place):
            slot = number_ref[place]
            owner = slot // capacity
            start = pl.multiple_of((slot - owner * capacity) * rcv, rcv)
            coef = in_ref[owner, pl.ds(start, rcv), :].astype(jnp.float32)
            diff_ref[slot], base_ref[slot], _ = shot_terms(
                coef.reshape(tiles, 8, block), cut_ref,
                number_ref[count + slot], number_ref[2 * count + slot], none,
            )

        def two_blocks(i, _):
            one_block(2 * i)
            one_block(2 * i + 1)
            return 0

        lax.fori_loop(0, number_ref[number_ref.shape[0] - 1], two_blocks, 0)

    shape = jax.ShapeDtypeStruct((count, tiles, 8, block), jnp.float32)
    return pl.pallas_call(
        body,
        in_specs=[full_smem()] + [full_vmem()] * 2,
        out_specs=[full_vmem()] * 2,
        out_shape=[shape] * 2,
        compiler_params=params(),
        cost_estimate=pl.CostEstimate(flops=1, bytes_accessed=8 << 20, transcendentals=0),
        name="shot_differences",
    )(numbers, arrived, cuts)


def finish(diffs, bases, cuts, energies, thresholds, numbers, both, receivers):
    count, tiles, _, block = diffs.shape
    rcv = tiles * 8
    shot_dev = (numbers.shape[0] - 1 - 3 * count) // SHOT_BLK
    shots = cuts.shape[0] - 1 - shot_dev
    step = min(2, shot_dev)

    def body(number_ref, diff_ref, base_ref, cut_ref, thr_ref, both_ref, *refs):
        out_hbm, out_ref, sem = refs[-3:]
        energy = refs[0][...]
        for ref in refs[1:-3]:
            energy = energy + ref[...]
        seconds = thr_ref[...] * jnp.sqrt(energy / (SHOT_BLK * receivers) + epsilon)
        copies = []
        for at in range(0, shot_dev, step):
            for i in range(at, at + step):
                first = step_size * cut_ref[shots + i][None]
                cut = seconds[i : i + 1, :]
                parts = []
                for q in range(SHOT_BLK):
                    slot = number_ref[3 * count + i * SHOT_BLK + q]
                    value = diff_ref[slot] - jnp.minimum(jnp.maximum(base_ref[slot], -first), first)
                    value = value.reshape(rcv, block)
                    shrunk = value - jnp.minimum(jnp.maximum(value, -cut), cut)
                    parts.append(shrunk.astype(jnp.bfloat16))
                model = lax.dot_general(
                    both_ref[:, :block], jnp.concatenate(parts, axis=0), (((1,), (1,)), ((), ())),
                    preferred_element_type=jnp.float32,
                )
                for q in range(SHOT_BLK):
                    out_ref[i, q] = model[:, q * rcv : (q + 1) * rcv].astype(jnp.bfloat16)
            copy = pltpu.make_async_copy(
                out_ref.at[pl.ds(at, step)], out_hbm.at[pl.ds(at, step)], sem.at[at // step]
            )
            copy.start()
            copies.append(copy)
        for copy in copies:
            copy.wait()

    return pl.pallas_call(
        body,
        in_specs=[full_smem()] + [full_vmem()] * (5 + len(energies)),
        out_specs=pl.BlockSpec(memory_space=pl.ANY),
        out_shape=jax.ShapeDtypeStruct((shot_dev, SHOT_BLK, block, rcv), jnp.bfloat16),
        scratch_shapes=[
            pltpu.VMEM((shot_dev, SHOT_BLK, block, rcv), jnp.bfloat16),
            pltpu.SemaphoreType.DMA((shot_dev // step,)),
        ],
        compiler_params=params(),
        name="model_of_shots",
    )(numbers, diffs, bases, cuts, thresholds, both, *energies)


def over_receivers(values):
    if lax.axis_size("rcv") == 2:
        return [values, lax.ppermute(values, "rcv", [(0, 1), (1, 0)])]
    return [lax.psum(values.astype(jnp.float32), "rcv").astype(values.dtype)]


def rotate(values, stride, by, size):
    n = lax.axis_size("shot")
    pairs = []
    for i in range(n):
        place = (i // stride) % size
        pairs.append((i, i + ((place + by) % size - place) * stride))
    return lax.ppermute(values, "shot", pairs)


def zorder(far):
    return list((2, 3, 1)) if far == 4 else list(range(1, far))


def local(record_data, offsets, thresholds):
    owners = lax.axis_size("shot")
    me = lax.axis_index("shot")
    windows, _, block, rcv = record_data.shape
    shots = offsets.shape[0]
    shot_dev = shots // owners
    pairs = shot_dev // 2
    pair_slots = min(pairs, owners // (SHOT_BLK + 1))
    capacity = (pairs + pair_slots - 1) // pair_slots
    receivers = rcv * lax.axis_size("rcv")

    high, low = split_bf16(jnp.asarray(cosine_table(block).T))
    both = jnp.concatenate([high, low], axis=1)
    records = record_data.reshape(windows, block, rcv)
    thr = thresholds[None, :]
    window_ids = jnp.arange(windows, dtype=jnp.int32)

    packed, energy = head(records, offsets, me, owners, capacity, both)
    packed, records, offsets, thr = lax.optimization_barrier((packed, records, offsets, thr))
    arrived = lax.all_to_all(packed, "shot", split_axis=0, concat_axis=0, tiled=True)

    near = min(4, owners)
    far = owners // near
    energy = jnp.concatenate([energy] + [rotate(energy, near, j, far) for j in zorder(far)])
    energy, offsets = lax.optimization_barrier((energy, offsets))
    energy = sum(part.astype(jnp.float32) for part in over_receivers(energy)).astype(jnp.bfloat16)
    energies = [energy] + [rotate(energy, 1, j, near) for j in range(1, near)]
    back = jnp.asarray([0] + zorder(far), jnp.int32)[None, :]
    side = jnp.arange(near, dtype=jnp.int32)[:, None]
    origin = (me // near - back + far) % far * near + (me % near - side + near) % near
    energy_ids = (window_ids * owners + origin[:, :, None]).reshape(-1)

    index = jnp.arange(shots, dtype=jnp.int32)
    ahead = (offsets[None, :] < offsets[:, None]) | (
        (offsets[None, :] == offsets[:, None]) & (index[None, :] < index[:, None])
    )
    place = jnp.sum(ahead.astype(jnp.int32), axis=1)
    ordered = jnp.sum(jnp.where(place[None, :] == index[:, None], offsets[None, :], 0), axis=1)
    mine = lax.dynamic_slice(offsets, (me * shot_dev,), (shot_dev,))
    all_offsets = jnp.concatenate([ordered, mine])
    grid_ids = window_ids[None, :] * owners + jnp.arange(owners, dtype=jnp.int32)[:, None]
    hits = landed(energy_ids[None, :], all_offsets[:, None]).astype(jnp.bfloat16)

    def bounds(ids):
        below = jnp.sum((offsets < ids[..., None] - (SHOT_BLK - 1)).astype(jnp.int32), axis=-1)
        upto = jnp.sum((offsets <= ids[..., None]).astype(jnp.int32), axis=-1)
        return below, upto

    own_lows, own_highs = bounds(window_ids * owners + me)

    slot_ids = jnp.arange(capacity, dtype=jnp.int32)
    held = jnp.max(landed(grid_ids[:, :, None], mine).astype(jnp.int32), axis=2)
    before = (window_ids[:, None] < window_ids[None, :]).astype(jnp.int32)
    held_rank = jnp.sum(held[:, :, None] * before, axis=1)
    taken = (held_rank[:, None, :] == slot_ids[None, :, None]) & (held[:, None, :] > 0)
    held_ids = jnp.sum(jnp.where(taken, grid_ids[:, None, :], 0), axis=2)
    valid = jnp.sum(taken.astype(jnp.int32), axis=2)
    lows, highs = bounds(held_ids)
    lows, highs = lows * valid, highs * valid
    targets = mine[:, None] + jnp.arange(SHOT_BLK, dtype=jnp.int32)[None, :]
    slot_of = jnp.arange(owners, dtype=jnp.int32)[:, None] * capacity + held_rank
    slots = jnp.sum(
        jnp.where(targets[:, :, None, None] == grid_ids[None, None], slot_of[None, None], 0),
        axis=(2, 3),
    )

    filled = valid.reshape(-1)
    count = jnp.arange(filled.shape[0], dtype=jnp.int32)
    nth = jnp.sum(jnp.where(count[None, :] < count[:, None], filled[None, :], 0), axis=1)
    chosen = (nth[None, :] == count[:, None]) & (filled[None, :] > 0)
    chosen = jnp.sum(jnp.where(chosen, count[None, :], 0), axis=1)
    half = (jnp.sum(filled) + 1) // 2
    numbers = jnp.concatenate(
        [chosen, lows.reshape(-1), highs.reshape(-1), slots.reshape(-1), half[None]]
    )
    group = index // shot_dev
    away = (group % near - me % near + near) % near * far
    away = (away + (group // near - me // near + far) % far) * shot_dev + index % shot_dev
    order = jnp.sum(jnp.where(place[None, :] == index[:, None], away[None, :], 0), axis=1)
    own_numbers = jnp.concatenate([own_lows, own_highs, order])

    records = pltpu.with_memory_space_constraint(records, pltpu.HBM)
    hits, own_numbers, numbers = lax.optimization_barrier((hits, own_numbers, numbers))
    cuts, *landed_parts, sums = landed_energies(
        records, energies, hits, thr, own_numbers, both, near, receivers
    )
    residual = remainder(records, sums, both)
    plane = [landed_parts[0]] + [rotate(landed_parts[j], 1, j, near) for j in range(1, near)]
    *plane, residual = lax.optimization_barrier((*plane, residual))
    plane = sum(plane)
    plane = sum(over_receivers(plane))
    energies = [plane[:shot_dev]] + [
        rotate(plane[j * shot_dev : (j + 1) * shot_dev], near, j, far) for j in range(1, far)
    ]
    diffs, bases = differences(arrived, cuts, numbers, capacity)
    model = finish(diffs, bases, cuts, energies, thr, numbers, both, receivers)
    return (model, residual.reshape(windows, 1, block, rcv))


def solution(mesh):
    return jax.shard_map(
        local,
        mesh=mesh,
        in_specs=(P(None, "shot", None, "rcv"), P(), P()),
        out_specs=(P("shot", None, None, "rcv"), P(None, "shot", None, "rcv")),
        check_vma=False,
    )
```

```python
import jax
import jax.numpy as jnp
import numpy as np
from jax import lax
from jax.experimental import pallas as pl
from jax.experimental.pallas import tpu as pltpu
from jax.sharding import PartitionSpec as P

SHOT_BLK = 4
momentum = 0.5
epsilon = 1e-06
step_size = 1.0 + momentum
VMEM_BYTES = 16 * 1024 * 1024
BLOCKS_STEP = 4
HEAD_VMEM_BYTES = 60 * 1024 * 1024


def cosine_table(length):
    rows = np.arange(length, dtype=np.float64)[:, None]
    cols = np.arange(length, dtype=np.float64)[None, :]
    table = np.cos(np.pi * (cols + 0.5) * rows / length) * np.sqrt(2.0 / length)
    return np.where(rows == 0, table * np.sqrt(0.5), table).astype(np.float32)


def split_bf16(values):
    high = values.astype(jnp.bfloat16)
    low = (values - high.astype(jnp.float32)).astype(jnp.bfloat16)
    return high, low


def full_vmem():
    return pl.BlockSpec(memory_space=pltpu.VMEM)


def full_smem():
    return pl.BlockSpec(memory_space=pltpu.SMEM)


def params(vmem=VMEM_BYTES):
    return pltpu.CompilerParams(vmem_limit_bytes=vmem)


def forward(both, values):
    block = values.shape[0]
    parts = lax.dot_general(
        values, both, (((0,), (0,)), ((), ())), preferred_element_type=jnp.float32
    )
    return parts[:, :block] + parts[:, block:]


def backward(both, coefficients):
    doubled = jnp.concatenate([coefficients, coefficients], axis=1)
    return lax.dot_general(
        both, doubled, (((1,), (1,)), ((), ())), preferred_element_type=jnp.float32
    )


def landed(ids, offsets):
    lag = ids - offsets
    return (lag >= 0) & (lag < SHOT_BLK)


def head(records, offsets, me, owners, capacity, both):
    windows, block, rcv = records.shape
    shots = offsets.shape[0]
    shot_dev = shots // owners
    chunk = 8
    chunks = windows // chunk
    f32, bf16 = jnp.float32, jnp.bfloat16

    def body(
        me_ref, off_hbm, rec_hbm, both_hbm, out_ref, energy_hbm,
        off_ref, rec_ref, both_ref, sent_ref, energy_ref, table_ref, table_smem,
        small_sem, rec_sem, out_sem,
    ):
        get_off = pltpu.make_async_copy(off_hbm, off_ref, small_sem.at[0])
        get_both = pltpu.make_async_copy(both_hbm, both_ref, small_sem.at[1])
        get_rec = [
            pltpu.make_async_copy(
                rec_hbm.at[pl.ds(c * chunk, chunk)],
                rec_ref.at[pl.ds(c * chunk, chunk)],
                rec_sem.at[c],
            )
            for c in range(chunks)
        ]
        get_off.start()
        get_both.start()
        for copy in get_rec:
            copy.start()
        get_off.wait()

        ids = lax.broadcasted_iota(jnp.int32, (windows, shots), 0) * owners + me_ref[0]
        hits = jnp.where(landed(ids, off_ref[...]), 1.0, 0.0)
        cover = jnp.sum(hits, axis=1, keepdims=True)
        scale = 1.0 / jnp.maximum(cover, 1.0)

        shot = lax.broadcasted_iota(jnp.int32, (shots, owners), 0)
        first = lax.broadcasted_iota(jnp.int32, (shots, owners), 1) * shot_dev
        member = jnp.where((shot >= first) & (shot < first + shot_dev), 1.0, 0.0)
        counts = jnp.dot(hits.astype(bf16), member.astype(bf16), preferred_element_type=f32)
        present = jnp.where(counts > 0.5, 1.0, 0.0)
        after = lax.broadcasted_iota(jnp.int32, (windows, windows), 0)
        before = lax.broadcasted_iota(jnp.int32, (windows, windows), 1)
        lower = jnp.where(before < after, 1.0, 0.0)
        rank = jnp.dot(lower.astype(bf16), present.astype(bf16), preferred_element_type=f32)
        rank = rank.astype(jnp.int32)
        window = lax.broadcasted_iota(jnp.int32, (windows, owners), 0)
        for i in range(capacity):
            here = (rank == i) & (present > 0.5)
            table_ref[i : i + 1, :owners] = jnp.sum(
                jnp.where(here, window, 0), axis=0, keepdims=True
            )
        put_table = pltpu.make_async_copy(table_ref, table_smem, small_sem.at[2])
        put_table.start()

        get_both.wait()
        rows = []
        for c in range(chunks):
            get_rec[c].wait()
            for w in range(c * chunk, (c + 1) * chunk):
                spread = (rec_ref[w] * scale[w : w + 1, 0:1]).astype(bf16)
                coef = forward(both_ref[...], spread)
                sent_ref[w] = coef.astype(bf16)
                rows.append(jnp.sum(coef * coef, axis=0, keepdims=True))

        energy_ref[...] = jnp.concatenate(rows, axis=0).astype(bf16)
        put_energy = pltpu.make_async_copy(energy_ref, energy_hbm, small_sem.at[3])
        put_energy.start()
        put_table.wait()

        def send(h, i):
            return pltpu.make_async_copy(
                sent_ref.at[table_smem[i, h]],
                out_ref.at[h, pl.ds(i * rcv, rcv), :],
                out_sem.at[h * capacity + i],
            )

        for h in range(owners):
            for i in range(capacity):
                send(h, i).start()
        for h in range(owners):
            for i in range(capacity):
                send(h, i).wait()
        put_energy.wait()

    hbm = pl.BlockSpec(memory_space=pltpu.HBM)
    table_shape = (8, 128)
    return pl.pallas_call(
        body,
        in_specs=[full_smem(), hbm, hbm, hbm],
        out_specs=[pl.BlockSpec(memory_space=pl.ANY)] * 2,
        out_shape=[
            jax.ShapeDtypeStruct((owners, capacity * rcv, block), bf16),
            jax.ShapeDtypeStruct((windows, block), bf16),
        ],
        scratch_shapes=[
            pltpu.VMEM((1, shots), jnp.int32),
            pltpu.VMEM((windows, block, rcv), f32),
            pltpu.VMEM((block, 2 * block), bf16),
            pltpu.VMEM((windows, rcv, block), bf16),
            pltpu.VMEM((windows, block), bf16),
            pltpu.VMEM(table_shape, jnp.int32),
            pltpu.SMEM(table_shape, jnp.int32),
            pltpu.SemaphoreType.DMA((4,)),
            pltpu.SemaphoreType.DMA((chunks,)),
            pltpu.SemaphoreType.DMA((owners * capacity,)),
        ],
        compiler_params=params(HEAD_VMEM_BYTES),
        name="pack_coefficients",
    )(me[None], offsets[None, :], records, both)


def clipped_sum(coef, cut_ref, low, high, none):
    size = jnp.abs(coef)
    peel, unroll = 6, 2

    def term(row):
        return jnp.minimum(size, cut_ref[jnp.where(row < high, row, none)][None])

    total = term(low)
    for u in range(1, peel):
        total = total + term(low + u)

    def add(j, total):
        for u in range(unroll):
            total = total + term(low + peel + j * unroll + u)
        return total

    left = jnp.maximum(high - low - peel, 0)
    total = lax.fori_loop(0, lax.div(left + unroll - 1, unroll), add, total)
    return jnp.where(coef < 0, -total, total)


def shot_terms(coef, cut_ref, low, high, none):
    clipped = clipped_sum(coef, cut_ref, low, high, none)
    many = jnp.full((1, 8, coef.shape[2]), (high - low).astype(jnp.float32))
    scale = step_size / jnp.maximum(many, 1.0)
    diff = (1.0 + step_size - scale * many) * coef + scale * clipped
    return diff, step_size * coef, many * coef - clipped


def landed_energies(records, energies, hits, thresholds, numbers, both, groups, receivers):
    windows, block, rcv = records.shape
    tiles = rcv // 8
    none = hits.shape[0]
    shots = numbers.shape[0] - 2 * windows
    size = shots // groups

    def body(number_ref, rec_hbm, hit_ref, thr_ref, both_ref, *refs):
        refs, scratch = refs[:-6], refs[-6:]
        cuts_ref, rec_ref, diff_ref, base_ref, sum_ref, sem = scratch
        part_refs, (cut_ref, *energy_refs, shrunk_ref) = (
            refs[: len(energies)],
            refs[len(energies) :],
        )
        get_rec = pltpu.make_async_copy(rec_hbm, rec_ref, sem)
        get_rec.start()
        energy = jnp.concatenate([ref[...] for ref in part_refs], axis=0)
        sums = jnp.dot(hit_ref[...], energy, preferred_element_type=jnp.float32)
        cuts_ref[...] = thr_ref[...] * jnp.sqrt(sums / (SHOT_BLK * receivers) + epsilon)

        def widen(i, _):
            at = pl.multiple_of(i * 8, 8)
            cut_ref[pl.ds(at, 8)] = jnp.broadcast_to(
                cuts_ref[pl.ds(at, 8), :][:, None, :], (8, 8, block)
            )
            return 0

        lax.fori_loop(0, none // 8, widen, 0, unroll=2)
        cut_ref[none] = jnp.zeros((8, block), jnp.float32)
        sum_ref[...] = jnp.zeros_like(sum_ref)
        get_rec.wait()
        for w in range(windows):
            cover = (number_ref[windows + w] - number_ref[w]).astype(jnp.float32)
            scale = 1.0 / jnp.maximum(jnp.full((1, rcv), cover), 1.0)
            spread = (rec_ref[w] * scale).astype(jnp.bfloat16)
            base_ref[w] = forward(both_ref[...], spread).reshape(tiles, 8, block)

        def one_window(w, _):
            low, high = number_ref[w], number_ref[windows + w]
            diff_ref[w], base_ref[w], shrunk = shot_terms(base_ref[w], cut_ref, low, high, none)
            shrunk_ref[w] = shrunk.reshape(rcv, block).astype(jnp.bfloat16)
            return 0

        lax.fori_loop(0, windows, one_window, 0)
        def energies_of_window(w, _):
            diff, base = diff_ref[w], base_ref[w]

            def one_shot(row, _):
                cut = step_size * cut_ref[row][None]
                value = diff - jnp.minimum(jnp.maximum(base, -cut), cut)
                sum_ref[number_ref[2 * windows + row]] = jnp.sum(value * value, axis=0)
                return 0

            lax.fori_loop(number_ref[w], number_ref[windows + w], one_shot, 0)
            return 0

        lax.fori_loop(0, windows, energies_of_window, 0)
        for g in range(groups):
            energy_refs[g][...] = jnp.sum(sum_ref[g * size : (g + 1) * size], axis=1)

    terms = pltpu.VMEM((windows, tiles, 8, block), jnp.float32)
    return pl.pallas_call(
        body,
        in_specs=[full_smem(), pl.BlockSpec(memory_space=pltpu.HBM)]
        + [full_vmem()] * (3 + len(energies)),
        out_specs=[full_vmem()] * (groups + 2),
        out_shape=[jax.ShapeDtypeStruct((none + 1, 8, block), jnp.float32)]
        + [jax.ShapeDtypeStruct((size, block), jnp.float32)] * groups
        + [jax.ShapeDtypeStruct((windows, rcv, block), jnp.bfloat16)],
        scratch_shapes=[
            pltpu.VMEM((none, block), jnp.float32),
            pltpu.VMEM((windows, block, rcv), jnp.float32),
            terms,
            terms,
            pltpu.VMEM((shots, 8, block), jnp.float32),
            pltpu.SemaphoreType.DMA,
        ],
        compiler_params=params(),
        cost_estimate=pl.CostEstimate(flops=1, bytes_accessed=6 << 20, transcendentals=0),
        name="second_energies",
    )(numbers, records, hits, thresholds, both, *energies)


def remainder(records, sums, both):
    windows, block, rcv = records.shape
    chunk = 4
    chunks = windows // chunk

    def body(rec_hbm, sum_ref, both_ref, out_hbm, rec_ref, out_ref, sem):
        def copy(c, source, target, k):
            part = pl.ds(c * chunk, chunk)
            return pltpu.make_async_copy(source.at[part], target.at[part], sem.at[k])

        for c in range(chunks):
            copy(c, rec_hbm, rec_ref, c).start()
        for c in range(chunks):
            sums = sum_ref[c * chunk : (c + 1) * chunk].reshape(chunk * rcv, block)
            blended = backward(both_ref[...], sums)
            copy(c, rec_hbm, rec_ref, c).wait()
            for w in range(chunk):
                at = c * chunk + w
                out_ref[at] = rec_ref[at] - step_size * blended[:, w * rcv : (w + 1) * rcv]
            copy(c, out_ref, out_hbm, chunks + c).start()
        for c in range(chunks):
            copy(c, out_ref, out_hbm, chunks + c).wait()

    own = pltpu.VMEM((windows, block, rcv), jnp.float32)
    return pl.pallas_call(
        body,
        in_specs=[pl.BlockSpec(memory_space=pltpu.HBM), full_vmem(), full_vmem()],
        out_specs=pl.BlockSpec(memory_space=pl.ANY),
        out_shape=jax.ShapeDtypeStruct((windows, block, rcv), jnp.float32),
        scratch_shapes=[own, own, pltpu.SemaphoreType.DMA((2 * chunks,))],
        compiler_params=params(),
        cost_estimate=pl.CostEstimate(flops=1, bytes_accessed=4 << 20, transcendentals=0),
        name="residual_of_records",
    )(records, sums, both)


def differences(arrived, cuts, numbers, capacity):
    owners, rows, block = arrived.shape
    rcv = rows // capacity
    tiles = rcv // 8
    count = owners * capacity
    none = cuts.shape[0] - 1

    def body(number_ref, in_ref, cut_ref, diff_ref, base_ref):
        def one_block(place):
            slot = number_ref[place]
            owner = slot // capacity
            start = pl.multiple_of((slot - owner * capacity) * rcv, rcv)
            coef = in_ref[owner, pl.ds(start, rcv), :].astype(jnp.float32)
            diff_ref[slot], base_ref[slot], _ = shot_terms(
                coef.reshape(tiles, 8, block), cut_ref,
                number_ref[count + slot], number_ref[2 * count + slot], none,
            )

        def some_blocks(i, _):
            for u in range(BLOCKS_STEP):
                one_block(BLOCKS_STEP * i + u)
            return 0

        lax.fori_loop(0, number_ref[number_ref.shape[0] - 1], some_blocks, 0)

    shape = jax.ShapeDtypeStruct((count, tiles, 8, block), jnp.float32)
    return pl.pallas_call(
        body,
        in_specs=[full_smem()] + [full_vmem()] * 2,
        out_specs=[full_vmem()] * 2,
        out_shape=[shape] * 2,
        compiler_params=params(),
        cost_estimate=pl.CostEstimate(flops=1, bytes_accessed=8 << 20, transcendentals=0),
        name="shot_differences",
    )(numbers, arrived, cuts)


def finish(diffs, bases, cuts, energies, thresholds, numbers, both, receivers):
    count, tiles, _, block = diffs.shape
    rcv = tiles * 8
    shot_dev = (numbers.shape[0] - 1 - 3 * count) // SHOT_BLK
    shots = cuts.shape[0] - 1 - shot_dev
    step = min(2, shot_dev)

    def body(number_ref, diff_ref, base_ref, cut_ref, thr_ref, both_ref, *refs):
        out_hbm, out_ref, sem = refs[-3:]
        energy = refs[0][...]
        for ref in refs[1:-3]:
            energy = energy + ref[...]
        seconds = thr_ref[...] * jnp.sqrt(energy / (SHOT_BLK * receivers) + epsilon)
        copies = []
        for at in range(0, shot_dev, step):
            for i in range(at, at + step):
                first = step_size * cut_ref[shots + i][None]
                cut = seconds[i : i + 1, :]
                parts = []
                for q in range(SHOT_BLK):
                    slot = number_ref[3 * count + i * SHOT_BLK + q]
                    value = diff_ref[slot] - jnp.minimum(jnp.maximum(base_ref[slot], -first), first)
                    value = value.reshape(rcv, block)
                    shrunk = value - jnp.minimum(jnp.maximum(value, -cut), cut)
                    parts.append(shrunk.astype(jnp.bfloat16))
                model = lax.dot_general(
                    both_ref[:, :block], jnp.concatenate(parts, axis=0), (((1,), (1,)), ((), ())),
                    preferred_element_type=jnp.float32,
                )
                for q in range(SHOT_BLK):
                    out_ref[i, q] = model[:, q * rcv : (q + 1) * rcv].astype(jnp.bfloat16)
            copy = pltpu.make_async_copy(
                out_ref.at[pl.ds(at, step)], out_hbm.at[pl.ds(at, step)], sem.at[at // step]
            )
            copy.start()
            copies.append(copy)
        for copy in copies:
            copy.wait()

    return pl.pallas_call(
        body,
        in_specs=[full_smem()] + [full_vmem()] * (5 + len(energies)),
        out_specs=pl.BlockSpec(memory_space=pl.ANY),
        out_shape=jax.ShapeDtypeStruct((shot_dev, SHOT_BLK, block, rcv), jnp.bfloat16),
        scratch_shapes=[
            pltpu.VMEM((shot_dev, SHOT_BLK, block, rcv), jnp.bfloat16),
            pltpu.SemaphoreType.DMA((shot_dev // step,)),
        ],
        compiler_params=params(),
        name="model_of_shots",
    )(numbers, diffs, bases, cuts, thresholds, both, *energies)


def over_receivers(values):
    if lax.axis_size("rcv") == 2:
        return [values, lax.ppermute(values, "rcv", [(0, 1), (1, 0)])]
    return [lax.psum(values.astype(jnp.float32), "rcv").astype(values.dtype)]


def rotate(values, stride, by, size):
    n = lax.axis_size("shot")
    pairs = []
    for i in range(n):
        place = (i // stride) % size
        pairs.append((i, i + ((place + by) % size - place) * stride))
    return lax.ppermute(values, "shot", pairs)


def zorder(far):
    return list((2, 3, 1)) if far == 4 else list(range(1, far))


def local(record_data, offsets, thresholds):
    owners = lax.axis_size("shot")
    me = lax.axis_index("shot")
    windows, _, block, rcv = record_data.shape
    shots = offsets.shape[0]
    shot_dev = shots // owners
    pairs = shot_dev // 2
    pair_slots = min(pairs, owners // (SHOT_BLK + 1))
    capacity = (pairs + pair_slots - 1) // pair_slots
    receivers = rcv * lax.axis_size("rcv")

    high, low = split_bf16(jnp.asarray(cosine_table(block).T))
    both = jnp.concatenate([high, low], axis=1)
    records = record_data.reshape(windows, block, rcv)
    thr = thresholds[None, :]
    window_ids = jnp.arange(windows, dtype=jnp.int32)

    packed, energy = head(records, offsets, me, owners, capacity, both)
    packed, records, offsets, thr = lax.optimization_barrier((packed, records, offsets, thr))
    arrived = lax.all_to_all(packed, "shot", split_axis=0, concat_axis=0, tiled=True)

    near = min(4, owners)
    far = owners // near
    energy = jnp.concatenate([energy] + [rotate(energy, near, j, far) for j in zorder(far)])
    energy, offsets = lax.optimization_barrier((energy, offsets))
    energy = sum(part.astype(jnp.float32) for part in over_receivers(energy)).astype(jnp.bfloat16)
    energies = [energy] + [rotate(energy, 1, j, near) for j in range(1, near)]
    back = jnp.asarray([0] + zorder(far), jnp.int32)[None, :]
    side = jnp.arange(near, dtype=jnp.int32)[:, None]
    origin = (me // near - back + far) % far * near + (me % near - side + near) % near
    energy_ids = (window_ids * owners + origin[:, :, None]).reshape(-1)

    index = jnp.arange(shots, dtype=jnp.int32)
    ahead = (offsets[None, :] < offsets[:, None]) | (
        (offsets[None, :] == offsets[:, None]) & (index[None, :] < index[:, None])
    )
    place = jnp.sum(ahead.astype(jnp.int32), axis=1)
    ordered = jnp.sum(jnp.where(place[None, :] == index[:, None], offsets[None, :], 0), axis=1)
    mine = lax.dynamic_slice(offsets, (me * shot_dev,), (shot_dev,))
    all_offsets = jnp.concatenate([ordered, mine])
    grid_ids = window_ids[None, :] * owners + jnp.arange(owners, dtype=jnp.int32)[:, None]
    hits = landed(energy_ids[None, :], all_offsets[:, None]).astype(jnp.bfloat16)

    def bounds(ids):
        below = jnp.sum((offsets < ids[..., None] - (SHOT_BLK - 1)).astype(jnp.int32), axis=-1)
        upto = jnp.sum((offsets <= ids[..., None]).astype(jnp.int32), axis=-1)
        return below, upto

    own_lows, own_highs = bounds(window_ids * owners + me)

    slot_ids = jnp.arange(capacity, dtype=jnp.int32)
    held = jnp.max(landed(grid_ids[:, :, None], mine).astype(jnp.int32), axis=2)
    before = (window_ids[:, None] < window_ids[None, :]).astype(jnp.int32)
    held_rank = jnp.sum(held[:, :, None] * before, axis=1)
    taken = (held_rank[:, None, :] == slot_ids[None, :, None]) & (held[:, None, :] > 0)
    held_ids = jnp.sum(jnp.where(taken, grid_ids[:, None, :], 0), axis=2)
    valid = jnp.sum(taken.astype(jnp.int32), axis=2)
    lows, highs = bounds(held_ids)
    lows, highs = lows * valid, highs * valid
    targets = mine[:, None] + jnp.arange(SHOT_BLK, dtype=jnp.int32)[None, :]
    slot_of = jnp.arange(owners, dtype=jnp.int32)[:, None] * capacity + held_rank
    slots = jnp.sum(
        jnp.where(targets[:, :, None, None] == grid_ids[None, None], slot_of[None, None], 0),
        axis=(2, 3),
    )

    filled = valid.reshape(-1)
    count = jnp.arange(filled.shape[0], dtype=jnp.int32)
    nth = jnp.sum(jnp.where(count[None, :] < count[:, None], filled[None, :], 0), axis=1)
    chosen = (nth[None, :] == count[:, None]) & (filled[None, :] > 0)
    chosen = jnp.sum(jnp.where(chosen, count[None, :], 0), axis=1)
    steps = (jnp.sum(filled) + BLOCKS_STEP - 1) // BLOCKS_STEP
    numbers = jnp.concatenate(
        [chosen, lows.reshape(-1), highs.reshape(-1), slots.reshape(-1), steps[None]]
    )
    group = index // shot_dev
    away = (group % near - me % near + near) % near * far
    away = (away + (group // near - me // near + far) % far) * shot_dev + index % shot_dev
    order = jnp.sum(jnp.where(place[None, :] == index[:, None], away[None, :], 0), axis=1)
    own_numbers = jnp.concatenate([own_lows, own_highs, order])

    records = pltpu.with_memory_space_constraint(records, pltpu.HBM)
    hits, own_numbers, numbers = lax.optimization_barrier((hits, own_numbers, numbers))
    cuts, *landed_parts, sums = landed_energies(
        records, energies, hits, thr, own_numbers, both, near, receivers
    )
    residual = remainder(records, sums, both)
    plane = [landed_parts[0]] + [rotate(landed_parts[j], 1, j, near) for j in range(1, near)]
    *plane, residual = lax.optimization_barrier((*plane, residual))
    plane = sum(plane)
    plane = sum(over_receivers(plane))
    energies = [plane[:shot_dev]] + [
        rotate(plane[j * shot_dev : (j + 1) * shot_dev], near, j, far) for j in range(1, far)
    ]
    diffs, bases = differences(arrived, cuts, numbers, capacity)
    model = finish(diffs, bases, cuts, energies, thr, numbers, both, receivers)
    return (model, residual.reshape(windows, 1, block, rcv))


def solution(mesh):
    return jax.shard_map(
        local,
        mesh=mesh,
        in_specs=(P(None, "shot", None, "rcv"), P(), P()),
        out_specs=(P("shot", None, None, "rcv"), P(None, "shot", None, "rcv")),
        check_vma=False,
    )
```

```python
import jax
import jax.numpy as jnp
import numpy as np
from jax import lax
from jax.experimental import pallas as pl
from jax.experimental.pallas import tpu as pltpu
from jax.sharding import PartitionSpec as P

SHOT_BLK = 4
momentum = 0.5
epsilon = 1e-06
step_size = 1.0 + momentum
VMEM_BYTES = 16 * 1024 * 1024
BLOCKS_STEP = 4
HEAD_VMEM_BYTES = 60 * 1024 * 1024


def cosine_table(length):
    rows = np.arange(length, dtype=np.float64)[:, None]
    cols = np.arange(length, dtype=np.float64)[None, :]
    table = np.cos(np.pi * (cols + 0.5) * rows / length) * np.sqrt(2.0 / length)
    return np.where(rows == 0, table * np.sqrt(0.5), table).astype(np.float32)


def split_bf16(values):
    high = values.astype(jnp.bfloat16)
    low = (values - high.astype(jnp.float32)).astype(jnp.bfloat16)
    return high, low


def full_vmem():
    return pl.BlockSpec(memory_space=pltpu.VMEM)


def full_smem():
    return pl.BlockSpec(memory_space=pltpu.SMEM)


def params(vmem=VMEM_BYTES):
    return pltpu.CompilerParams(vmem_limit_bytes=vmem)


def forward(both, values):
    block = values.shape[0]
    parts = lax.dot_general(
        values, both, (((0,), (0,)), ((), ())), preferred_element_type=jnp.float32
    )
    return parts[:, :block] + parts[:, block:]


def backward(both, coefficients):
    doubled = jnp.concatenate([coefficients, coefficients], axis=1)
    return lax.dot_general(
        both, doubled, (((1,), (1,)), ((), ())), preferred_element_type=jnp.float32
    )


def landed(ids, offsets):
    lag = ids - offsets
    return (lag >= 0) & (lag < SHOT_BLK)


def head(records, offsets, me, owners, capacity, both):
    windows, block, rcv = records.shape
    shots = offsets.shape[0]
    shot_dev = shots // owners
    chunk = 8
    chunks = windows // chunk
    f32, bf16 = jnp.float32, jnp.bfloat16

    def body(
        me_ref, off_hbm, rec_hbm, both_hbm, out_ref, energy_hbm,
        off_ref, rec_ref, both_ref, sent_ref, energy_ref, table_ref, table_smem,
        small_sem, rec_sem, out_sem,
    ):
        get_off = pltpu.make_async_copy(off_hbm, off_ref, small_sem.at[0])
        get_both = pltpu.make_async_copy(both_hbm, both_ref, small_sem.at[1])
        get_rec = [
            pltpu.make_async_copy(
                rec_hbm.at[pl.ds(c * chunk, chunk)],
                rec_ref.at[pl.ds(c * chunk, chunk)],
                rec_sem.at[c],
            )
            for c in range(chunks)
        ]
        get_off.start()
        get_both.start()
        for copy in get_rec:
            copy.start()
        get_off.wait()

        ids = lax.broadcasted_iota(jnp.int32, (windows, shots), 0) * owners + me_ref[0]
        hits = jnp.where(landed(ids, off_ref[...]), 1.0, 0.0)
        cover = jnp.sum(hits, axis=1, keepdims=True)
        scale = 1.0 / jnp.maximum(cover, 1.0)

        shot = lax.broadcasted_iota(jnp.int32, (shots, owners), 0)
        first = lax.broadcasted_iota(jnp.int32, (shots, owners), 1) * shot_dev
        member = jnp.where((shot >= first) & (shot < first + shot_dev), 1.0, 0.0)
        counts = jnp.dot(hits.astype(bf16), member.astype(bf16), preferred_element_type=f32)
        present = jnp.where(counts > 0.5, 1.0, 0.0)
        after = lax.broadcasted_iota(jnp.int32, (windows, windows), 0)
        before = lax.broadcasted_iota(jnp.int32, (windows, windows), 1)
        lower = jnp.where(before < after, 1.0, 0.0)
        rank = jnp.dot(lower.astype(bf16), present.astype(bf16), preferred_element_type=f32)
        rank = rank.astype(jnp.int32)
        window = lax.broadcasted_iota(jnp.int32, (windows, owners), 0)
        for i in range(capacity):
            here = (rank == i) & (present > 0.5)
            table_ref[i : i + 1, :owners] = jnp.sum(
                jnp.where(here, window, 0), axis=0, keepdims=True
            )
        put_table = pltpu.make_async_copy(table_ref, table_smem, small_sem.at[2])
        put_table.start()

        get_both.wait()
        rows = []
        for c in range(chunks):
            get_rec[c].wait()
            for w in range(c * chunk, (c + 1) * chunk):
                spread = (rec_ref[w] * scale[w : w + 1, 0:1]).astype(bf16)
                coef = forward(both_ref[...], spread)
                sent_ref[w] = coef.astype(bf16)
                rows.append(jnp.sum(coef * coef, axis=0, keepdims=True))

        energy_ref[...] = jnp.concatenate(rows, axis=0).astype(bf16)
        put_energy = pltpu.make_async_copy(energy_ref, energy_hbm, small_sem.at[3])
        put_energy.start()
        put_table.wait()

        def send(h, i):
            return pltpu.make_async_copy(
                sent_ref.at[table_smem[i, h]],
                out_ref.at[h, pl.ds(i * rcv, rcv), :],
                out_sem.at[h * capacity + i],
            )

        for h in range(owners):
            for i in range(capacity):
                send(h, i).start()
        for h in range(owners):
            for i in range(capacity):
                send(h, i).wait()
        put_energy.wait()

    hbm = pl.BlockSpec(memory_space=pltpu.HBM)
    table_shape = (8, 128)
    return pl.pallas_call(
        body,
        in_specs=[full_smem(), hbm, hbm, hbm],
        out_specs=[pl.BlockSpec(memory_space=pl.ANY)] * 2,
        out_shape=[
            jax.ShapeDtypeStruct((owners, capacity * rcv, block), bf16),
            jax.ShapeDtypeStruct((windows, block), bf16),
        ],
        scratch_shapes=[
            pltpu.VMEM((1, shots), jnp.int32),
            pltpu.VMEM((windows, block, rcv), f32),
            pltpu.VMEM((block, 2 * block), bf16),
            pltpu.VMEM((windows, rcv, block), bf16),
            pltpu.VMEM((windows, block), bf16),
            pltpu.VMEM(table_shape, jnp.int32),
            pltpu.SMEM(table_shape, jnp.int32),
            pltpu.SemaphoreType.DMA((4,)),
            pltpu.SemaphoreType.DMA((chunks,)),
            pltpu.SemaphoreType.DMA((owners * capacity,)),
        ],
        compiler_params=params(HEAD_VMEM_BYTES),
        name="pack_coefficients",
    )(me[None], offsets[None, :], records, both)


def clipped_sum(coef, cut_ref, low, high, none):
    size = jnp.abs(coef)
    peel, unroll = 6, 2

    def term(row):
        return jnp.minimum(size, cut_ref[jnp.where(row < high, row, none)][None])

    total = term(low)
    for u in range(1, peel):
        total = total + term(low + u)

    def add(j, total):
        for u in range(unroll):
            total = total + term(low + peel + j * unroll + u)
        return total

    left = jnp.maximum(high - low - peel, 0)
    total = lax.fori_loop(0, lax.div(left + unroll - 1, unroll), add, total)
    return jnp.where(coef < 0, -total, total)


def shot_terms(coef, cut_ref, low, high, none):
    clipped = clipped_sum(coef, cut_ref, low, high, none)
    many = jnp.full((1, 8, coef.shape[2]), (high - low).astype(jnp.float32))
    scale = step_size / jnp.maximum(many, 1.0)
    diff = (1.0 + step_size - scale * many) * coef + scale * clipped
    return diff, step_size * coef, many * coef - clipped


def landed_energies(records, energies, hits, thresholds, numbers, both, groups, receivers):
    windows, block, rcv = records.shape
    tiles = rcv // 8
    none = hits.shape[0]
    shots = numbers.shape[0] - 2 * windows
    size = shots // groups

    def body(number_ref, rec_hbm, hit_ref, thr_ref, both_ref, *refs):
        refs, scratch = refs[:-6], refs[-6:]
        cuts_ref, rec_ref, diff_ref, base_ref, sum_ref, sem = scratch
        part_refs, (cut_ref, *energy_refs, shrunk_ref) = (
            refs[: len(energies)],
            refs[len(energies) :],
        )
        get_rec = pltpu.make_async_copy(rec_hbm, rec_ref, sem)
        get_rec.start()
        energy = jnp.concatenate([ref[...] for ref in part_refs], axis=0)
        sums = jnp.dot(hit_ref[...], energy, preferred_element_type=jnp.float32)
        cuts_ref[...] = thr_ref[...] * jnp.sqrt(sums / (SHOT_BLK * receivers) + epsilon)

        def widen(i, _):
            at = pl.multiple_of(i * 8, 8)
            cut_ref[pl.ds(at, 8)] = jnp.broadcast_to(
                cuts_ref[pl.ds(at, 8), :][:, None, :], (8, 8, block)
            )
            return 0

        lax.fori_loop(0, none // 8, widen, 0, unroll=2)
        cut_ref[none] = jnp.zeros((8, block), jnp.float32)
        sum_ref[...] = jnp.zeros_like(sum_ref)
        get_rec.wait()
        for w in range(windows):
            cover = (number_ref[windows + w] - number_ref[w]).astype(jnp.float32)
            scale = 1.0 / jnp.maximum(jnp.full((1, rcv), cover), 1.0)
            spread = (rec_ref[w] * scale).astype(jnp.bfloat16)
            base_ref[w] = forward(both_ref[...], spread).reshape(tiles, 8, block)

        def one_window(w, _):
            low, high = number_ref[w], number_ref[windows + w]
            diff_ref[w], base_ref[w], shrunk = shot_terms(base_ref[w], cut_ref, low, high, none)
            shrunk_ref[w] = shrunk.reshape(rcv, block).astype(jnp.bfloat16)
            return 0

        lax.fori_loop(0, windows, one_window, 0)
        def energies_of_window(w, _):
            diff, base = diff_ref[w], base_ref[w]

            def one_shot(row, _):
                cut = step_size * cut_ref[row][None]
                value = diff - jnp.minimum(jnp.maximum(base, -cut), cut)
                sum_ref[number_ref[2 * windows + row]] = jnp.sum(value * value, axis=0)
                return 0

            lax.fori_loop(number_ref[w], number_ref[windows + w], one_shot, 0)
            return 0

        lax.fori_loop(0, windows, energies_of_window, 0)
        for g in range(groups):
            energy_refs[g][...] = jnp.sum(sum_ref[g * size : (g + 1) * size], axis=1)

    terms = pltpu.VMEM((windows, tiles, 8, block), jnp.float32)
    return pl.pallas_call(
        body,
        in_specs=[full_smem(), pl.BlockSpec(memory_space=pltpu.HBM)]
        + [full_vmem()] * (3 + len(energies)),
        out_specs=[full_vmem()] * (groups + 2),
        out_shape=[jax.ShapeDtypeStruct((none + 1, 8, block), jnp.float32)]
        + [jax.ShapeDtypeStruct((size, block), jnp.float32)] * groups
        + [jax.ShapeDtypeStruct((windows, rcv, block), jnp.bfloat16)],
        scratch_shapes=[
            pltpu.VMEM((none, block), jnp.float32),
            pltpu.VMEM((windows, block, rcv), jnp.float32),
            terms,
            terms,
            pltpu.VMEM((shots, 8, block), jnp.float32),
            pltpu.SemaphoreType.DMA,
        ],
        compiler_params=params(),
        cost_estimate=pl.CostEstimate(flops=1, bytes_accessed=6 << 20, transcendentals=0),
        name="second_energies",
    )(numbers, records, hits, thresholds, both, *energies)


def remainder(records, sums, both):
    windows, block, rcv = records.shape
    chunk = 4
    chunks = windows // chunk

    def body(rec_hbm, sum_ref, both_ref, out_hbm, rec_ref, out_ref, sem):
        def copy(c, source, target, k):
            part = pl.ds(c * chunk, chunk)
            return pltpu.make_async_copy(source.at[part], target.at[part], sem.at[k])

        for c in range(chunks):
            copy(c, rec_hbm, rec_ref, c).start()
        for c in range(chunks):
            sums = sum_ref[c * chunk : (c + 1) * chunk].reshape(chunk * rcv, block)
            blended = backward(both_ref[...], sums)
            copy(c, rec_hbm, rec_ref, c).wait()
            for w in range(chunk):
                at = c * chunk + w
                out_ref[at] = rec_ref[at] - step_size * blended[:, w * rcv : (w + 1) * rcv]
            copy(c, out_ref, out_hbm, chunks + c).start()
        for c in range(chunks):
            copy(c, out_ref, out_hbm, chunks + c).wait()

    own = pltpu.VMEM((windows, block, rcv), jnp.float32)
    return pl.pallas_call(
        body,
        in_specs=[pl.BlockSpec(memory_space=pltpu.HBM), full_vmem(), full_vmem()],
        out_specs=pl.BlockSpec(memory_space=pl.ANY),
        out_shape=jax.ShapeDtypeStruct((windows, block, rcv), jnp.float32),
        scratch_shapes=[own, own, pltpu.SemaphoreType.DMA((2 * chunks,))],
        compiler_params=params(),
        cost_estimate=pl.CostEstimate(flops=1, bytes_accessed=4 << 20, transcendentals=0),
        name="residual_of_records",
    )(records, sums, both)


def second(arrived, cuts, numbers, capacity, shot_dev):
    owners, rows, block = arrived.shape
    rcv = rows // capacity
    tiles = rcv // 8
    count = owners * capacity
    none = cuts.shape[0] - 1
    shots = none - shot_dev

    def body(number_ref, in_ref, cut_ref, out_ref, diff_ref, base_ref):
        def one_block(place):
            slot = number_ref[place]
            owner = slot // capacity
            start = pl.multiple_of((slot - owner * capacity) * rcv, rcv)
            coef = in_ref[owner, pl.ds(start, rcv), :].astype(jnp.float32)
            diff_ref[slot], base_ref[slot], _ = shot_terms(
                coef.reshape(tiles, 8, block), cut_ref,
                number_ref[count + slot], number_ref[2 * count + slot], none,
            )

        def some_blocks(i, _):
            for u in range(BLOCKS_STEP):
                one_block(BLOCKS_STEP * i + u)
            return 0

        lax.fori_loop(0, number_ref[number_ref.shape[0] - 1], some_blocks, 0)

        def one_shot(shot, _):
            cut = step_size * cut_ref[shots + shot][None]
            for q in range(SHOT_BLK):
                entry = shot * SHOT_BLK + q
                slot = number_ref[3 * count + entry]
                value = diff_ref[slot] - jnp.minimum(jnp.maximum(base_ref[slot], -cut), cut)
                out_ref[entry] = value.reshape(rcv, block)
            return 0

        lax.fori_loop(0, shot_dev, one_shot, 0, unroll=2)

    terms = pltpu.VMEM((count, tiles, 8, block), jnp.float32)
    return pl.pallas_call(
        body,
        in_specs=[full_smem()] + [full_vmem()] * 2,
        out_specs=full_vmem(),
        out_shape=jax.ShapeDtypeStruct((shot_dev * SHOT_BLK, rcv, block), jnp.float32),
        scratch_shapes=[terms, terms],
        compiler_params=params(),
        cost_estimate=pl.CostEstimate(flops=1, bytes_accessed=8 << 20, transcendentals=0),
        name="second_coefficients",
    )(numbers, arrived, cuts)


def finish(values, energies, thresholds, both, receivers):
    entries, rcv, block = values.shape
    shot_dev = entries // SHOT_BLK
    step = min(2, shot_dev)

    def body(in_ref, thr_ref, both_ref, *refs):
        out_hbm, out_ref, sem = refs[-3:]
        energy = refs[0][...]
        for ref in refs[1:-3]:
            energy = energy + ref[...]
        cuts = thr_ref[...] * jnp.sqrt(energy / (SHOT_BLK * receivers) + epsilon)
        copies = []
        for at in range(0, shot_dev, step):
            for i in range(at, at + step):
                cut = cuts[i : i + 1, :]
                value = in_ref[i * SHOT_BLK : (i + 1) * SHOT_BLK].reshape(SHOT_BLK * rcv, block)
                shrunk = value - jnp.minimum(jnp.maximum(value, -cut), cut)
                model = lax.dot_general(
                    both_ref[:, :block], shrunk.astype(jnp.bfloat16), (((1,), (1,)), ((), ())),
                    preferred_element_type=jnp.float32,
                )
                for q in range(SHOT_BLK):
                    out_ref[i, q] = model[:, q * rcv : (q + 1) * rcv].astype(jnp.bfloat16)
            copy = pltpu.make_async_copy(
                out_ref.at[pl.ds(at, step)], out_hbm.at[pl.ds(at, step)], sem.at[at // step]
            )
            copy.start()
            copies.append(copy)
        for copy in copies:
            copy.wait()

    return pl.pallas_call(
        body,
        in_specs=[full_vmem()] * (3 + len(energies)),
        out_specs=pl.BlockSpec(memory_space=pl.ANY),
        out_shape=jax.ShapeDtypeStruct((shot_dev, SHOT_BLK, block, rcv), jnp.bfloat16),
        scratch_shapes=[
            pltpu.VMEM((shot_dev, SHOT_BLK, block, rcv), jnp.bfloat16),
            pltpu.SemaphoreType.DMA((shot_dev // step,)),
        ],
        compiler_params=params(),
        name="model_of_shots",
    )(values, thresholds, both, *energies)


def over_receivers(values):
    if lax.axis_size("rcv") == 2:
        return [values, lax.ppermute(values, "rcv", [(0, 1), (1, 0)])]
    return [lax.psum(values.astype(jnp.float32), "rcv").astype(values.dtype)]


def rotate(values, stride, by, size):
    n = lax.axis_size("shot")
    pairs = []
    for i in range(n):
        place = (i // stride) % size
        pairs.append((i, i + ((place + by) % size - place) * stride))
    return lax.ppermute(values, "shot", pairs)


def zorder(far):
    return list((2, 3, 1)) if far == 4 else list(range(1, far))


def local(record_data, offsets, thresholds):
    owners = lax.axis_size("shot")
    me = lax.axis_index("shot")
    windows, _, block, rcv = record_data.shape
    shots = offsets.shape[0]
    shot_dev = shots // owners
    pairs = shot_dev // 2
    pair_slots = min(pairs, owners // (SHOT_BLK + 1))
    capacity = (pairs + pair_slots - 1) // pair_slots
    receivers = rcv * lax.axis_size("rcv")

    high, low = split_bf16(jnp.asarray(cosine_table(block).T))
    both = jnp.concatenate([high, low], axis=1)
    records = record_data.reshape(windows, block, rcv)
    thr = thresholds[None, :]
    window_ids = jnp.arange(windows, dtype=jnp.int32)

    packed, energy = head(records, offsets, me, owners, capacity, both)
    packed, records, offsets, thr = lax.optimization_barrier((packed, records, offsets, thr))
    arrived = lax.all_to_all(packed, "shot", split_axis=0, concat_axis=0, tiled=True)

    near = min(4, owners)
    far = owners // near
    energy = jnp.concatenate([energy] + [rotate(energy, near, j, far) for j in zorder(far)])
    energy, offsets = lax.optimization_barrier((energy, offsets))
    energy = sum(part.astype(jnp.float32) for part in over_receivers(energy)).astype(jnp.bfloat16)
    energies = [energy] + [rotate(energy, 1, j, near) for j in range(1, near)]
    back = jnp.asarray([0] + zorder(far), jnp.int32)[None, :]
    side = jnp.arange(near, dtype=jnp.int32)[:, None]
    origin = (me // near - back + far) % far * near + (me % near - side + near) % near
    energy_ids = (window_ids * owners + origin[:, :, None]).reshape(-1)

    index = jnp.arange(shots, dtype=jnp.int32)
    ahead = (offsets[None, :] < offsets[:, None]) | (
        (offsets[None, :] == offsets[:, None]) & (index[None, :] < index[:, None])
    )
    place = jnp.sum(ahead.astype(jnp.int32), axis=1)
    ordered = jnp.sum(jnp.where(place[None, :] == index[:, None], offsets[None, :], 0), axis=1)
    mine = lax.dynamic_slice(offsets, (me * shot_dev,), (shot_dev,))
    all_offsets = jnp.concatenate([ordered, mine])
    grid_ids = window_ids[None, :] * owners + jnp.arange(owners, dtype=jnp.int32)[:, None]
    hits = landed(energy_ids[None, :], all_offsets[:, None]).astype(jnp.bfloat16)

    def bounds(ids):
        below = jnp.sum((offsets < ids[..., None] - (SHOT_BLK - 1)).astype(jnp.int32), axis=-1)
        upto = jnp.sum((offsets <= ids[..., None]).astype(jnp.int32), axis=-1)
        return below, upto

    own_lows, own_highs = bounds(window_ids * owners + me)

    slot_ids = jnp.arange(capacity, dtype=jnp.int32)
    held = jnp.max(landed(grid_ids[:, :, None], mine).astype(jnp.int32), axis=2)
    before = (window_ids[:, None] < window_ids[None, :]).astype(jnp.int32)
    held_rank = jnp.sum(held[:, :, None] * before, axis=1)
    taken = (held_rank[:, None, :] == slot_ids[None, :, None]) & (held[:, None, :] > 0)
    held_ids = jnp.sum(jnp.where(taken, grid_ids[:, None, :], 0), axis=2)
    valid = jnp.sum(taken.astype(jnp.int32), axis=2)
    lows, highs = bounds(held_ids)
    lows, highs = lows * valid, highs * valid
    targets = mine[:, None] + jnp.arange(SHOT_BLK, dtype=jnp.int32)[None, :]
    slot_of = jnp.arange(owners, dtype=jnp.int32)[:, None] * capacity + held_rank
    slots = jnp.sum(
        jnp.where(targets[:, :, None, None] == grid_ids[None, None], slot_of[None, None], 0),
        axis=(2, 3),
    )

    filled = valid.reshape(-1)
    count = jnp.arange(filled.shape[0], dtype=jnp.int32)
    nth = jnp.sum(jnp.where(count[None, :] < count[:, None], filled[None, :], 0), axis=1)
    chosen = (nth[None, :] == count[:, None]) & (filled[None, :] > 0)
    chosen = jnp.sum(jnp.where(chosen, count[None, :], 0), axis=1)
    steps = (jnp.sum(filled) + BLOCKS_STEP - 1) // BLOCKS_STEP
    numbers = jnp.concatenate(
        [chosen, lows.reshape(-1), highs.reshape(-1), slots.reshape(-1), steps[None]]
    )
    group = index // shot_dev
    away = (group % near - me % near + near) % near * far
    away = (away + (group // near - me // near + far) % far) * shot_dev + index % shot_dev
    order = jnp.sum(jnp.where(place[None, :] == index[:, None], away[None, :], 0), axis=1)
    own_numbers = jnp.concatenate([own_lows, own_highs, order])

    records = pltpu.with_memory_space_constraint(records, pltpu.HBM)
    hits, own_numbers, numbers = lax.optimization_barrier((hits, own_numbers, numbers))
    cuts, *landed_parts, sums = landed_energies(
        records, energies, hits, thr, own_numbers, both, near, receivers
    )
    residual = remainder(records, sums, both)
    plane = [landed_parts[0]] + [rotate(landed_parts[j], 1, j, near) for j in range(1, near)]
    *plane, residual = lax.optimization_barrier((*plane, residual))
    plane = sum(plane)
    plane = sum(over_receivers(plane))
    energies = [plane[:shot_dev]] + [
        rotate(plane[j * shot_dev : (j + 1) * shot_dev], near, j, far) for j in range(1, far)
    ]
    values = second(arrived, cuts, numbers, capacity, shot_dev)
    model = finish(values, energies, thr, both, receivers)
    return (model, residual.reshape(windows, 1, block, rcv))


def solution(mesh):
    return jax.shard_map(
        local,
        mesh=mesh,
        in_specs=(P(None, "shot", None, "rcv"), P(), P()),
        out_specs=(P("shot", None, None, "rcv"), P(None, "shot", None, "rcv")),
        check_vma=False,
    )
```

```python
import jax
import jax.numpy as jnp
import numpy as np
from jax import lax
from jax.experimental import pallas as pl
from jax.experimental.pallas import tpu as pltpu
from jax.sharding import PartitionSpec as P

SHOT_BLK = 4
momentum = 0.5
epsilon = 1e-06
step_size = 1.0 + momentum
VMEM_BYTES = 16 * 1024 * 1024
BLOCKS_STEP = 4
HEAD_VMEM_BYTES = 60 * 1024 * 1024


def cosine_table(length):
    rows = np.arange(length, dtype=np.float64)[:, None]
    cols = np.arange(length, dtype=np.float64)[None, :]
    table = np.cos(np.pi * (cols + 0.5) * rows / length) * np.sqrt(2.0 / length)
    return np.where(rows == 0, table * np.sqrt(0.5), table).astype(np.float32)


def split_bf16(values):
    high = values.astype(jnp.bfloat16)
    low = (values - high.astype(jnp.float32)).astype(jnp.bfloat16)
    return high, low


def full_vmem():
    return pl.BlockSpec(memory_space=pltpu.VMEM)


def full_smem():
    return pl.BlockSpec(memory_space=pltpu.SMEM)


def params(vmem=VMEM_BYTES):
    return pltpu.CompilerParams(vmem_limit_bytes=vmem)


def forward(both, values):
    block = values.shape[0]
    parts = lax.dot_general(
        values, both, (((0,), (0,)), ((), ())), preferred_element_type=jnp.float32
    )
    return parts[:, :block] + parts[:, block:]


def backward(both, coefficients):
    doubled = jnp.concatenate([coefficients, coefficients], axis=1)
    return lax.dot_general(
        both, doubled, (((1,), (1,)), ((), ())), preferred_element_type=jnp.float32
    )


def landed(ids, offsets):
    lag = ids - offsets
    return (lag >= 0) & (lag < SHOT_BLK)


def head(records, offsets, me, owners, capacity, both):
    windows, block, rcv = records.shape
    shots = offsets.shape[0]
    shot_dev = shots // owners
    chunk = 8
    chunks = windows // chunk
    f32, bf16 = jnp.float32, jnp.bfloat16

    def body(
        me_ref, off_hbm, rec_hbm, both_hbm, out_ref, energy_hbm,
        off_ref, rec_ref, both_ref, sent_ref, energy_ref, table_ref, table_smem,
        small_sem, rec_sem, out_sem,
    ):
        get_off = pltpu.make_async_copy(off_hbm, off_ref, small_sem.at[0])
        get_both = pltpu.make_async_copy(both_hbm, both_ref, small_sem.at[1])
        get_rec = [
            pltpu.make_async_copy(
                rec_hbm.at[pl.ds(c * chunk, chunk)],
                rec_ref.at[pl.ds(c * chunk, chunk)],
                rec_sem.at[c],
            )
            for c in range(chunks)
        ]
        get_off.start()
        get_both.start()
        for copy in get_rec:
            copy.start()
        get_off.wait()

        ids = lax.broadcasted_iota(jnp.int32, (windows, shots), 0) * owners + me_ref[0]
        hits = jnp.where(landed(ids, off_ref[...]), 1.0, 0.0)
        cover = jnp.sum(hits, axis=1, keepdims=True)
        scale = 1.0 / jnp.maximum(cover, 1.0)

        shot = lax.broadcasted_iota(jnp.int32, (shots, owners), 0)
        first = lax.broadcasted_iota(jnp.int32, (shots, owners), 1) * shot_dev
        member = jnp.where((shot >= first) & (shot < first + shot_dev), 1.0, 0.0)
        counts = jnp.dot(hits.astype(bf16), member.astype(bf16), preferred_element_type=f32)
        present = jnp.where(counts > 0.5, 1.0, 0.0)
        after = lax.broadcasted_iota(jnp.int32, (windows, windows), 0)
        before = lax.broadcasted_iota(jnp.int32, (windows, windows), 1)
        lower = jnp.where(before < after, 1.0, 0.0)
        rank = jnp.dot(lower.astype(bf16), present.astype(bf16), preferred_element_type=f32)
        rank = rank.astype(jnp.int32)
        window = lax.broadcasted_iota(jnp.int32, (windows, owners), 0)
        for i in range(capacity):
            here = (rank == i) & (present > 0.5)
            table_ref[i : i + 1, :owners] = jnp.sum(
                jnp.where(here, window, 0), axis=0, keepdims=True
            )
        put_table = pltpu.make_async_copy(table_ref, table_smem, small_sem.at[2])
        put_table.start()

        get_both.wait()
        rows = []
        for c in range(chunks):
            get_rec[c].wait()
            for w in range(c * chunk, (c + 1) * chunk):
                spread = (rec_ref[w] * scale[w : w + 1, 0:1]).astype(bf16)
                coef = forward(both_ref[...], spread)
                sent_ref[w] = coef.astype(bf16)
                rows.append(jnp.sum(coef * coef, axis=0, keepdims=True))

        energy_ref[...] = jnp.concatenate(rows, axis=0).astype(bf16)
        put_energy = pltpu.make_async_copy(energy_ref, energy_hbm, small_sem.at[3])
        put_energy.start()
        put_table.wait()

        def send(h, i):
            return pltpu.make_async_copy(
                sent_ref.at[table_smem[i, h]],
                out_ref.at[h, pl.ds(i * rcv, rcv), :],
                out_sem.at[h * capacity + i],
            )

        for h in range(owners):
            for i in range(capacity):
                send(h, i).start()
        for h in range(owners):
            for i in range(capacity):
                send(h, i).wait()
        put_energy.wait()

    hbm = pl.BlockSpec(memory_space=pltpu.HBM)
    table_shape = (8, 128)
    return pl.pallas_call(
        body,
        in_specs=[full_smem(), hbm, hbm, hbm],
        out_specs=[pl.BlockSpec(memory_space=pl.ANY)] * 2,
        out_shape=[
            jax.ShapeDtypeStruct((owners, capacity * rcv, block), bf16),
            jax.ShapeDtypeStruct((windows, block), bf16),
        ],
        scratch_shapes=[
            pltpu.VMEM((1, shots), jnp.int32),
            pltpu.VMEM((windows, block, rcv), f32),
            pltpu.VMEM((block, 2 * block), bf16),
            pltpu.VMEM((windows, rcv, block), bf16),
            pltpu.VMEM((windows, block), bf16),
            pltpu.VMEM(table_shape, jnp.int32),
            pltpu.SMEM(table_shape, jnp.int32),
            pltpu.SemaphoreType.DMA((4,)),
            pltpu.SemaphoreType.DMA((chunks,)),
            pltpu.SemaphoreType.DMA((owners * capacity,)),
        ],
        compiler_params=params(HEAD_VMEM_BYTES),
        name="pack_coefficients",
    )(me[None], offsets[None, :], records, both)


def clipped_sum(coef, cut_ref, low, high, none):
    size = jnp.abs(coef)
    peel, unroll = 6, 2

    def term(row):
        return jnp.minimum(size, cut_ref[jnp.where(row < high, row, none)][None])

    total = term(low)
    for u in range(1, peel):
        total = total + term(low + u)

    def add(j, total):
        for u in range(unroll):
            total = total + term(low + peel + j * unroll + u)
        return total

    left = jnp.maximum(high - low - peel, 0)
    total = lax.fori_loop(0, lax.div(left + unroll - 1, unroll), add, total)
    return jnp.where(coef < 0, -total, total)


def shot_terms(coef, cut_ref, low, high, none):
    clipped = clipped_sum(coef, cut_ref, low, high, none)
    many = jnp.full((1, 8, coef.shape[2]), (high - low).astype(jnp.float32))
    scale = step_size / jnp.maximum(many, 1.0)
    diff = (1.0 + step_size - scale * many) * coef + scale * clipped
    return diff, step_size * coef, many * coef - clipped


def landed_energies(records, energies, hits, thresholds, numbers, both, groups, receivers):
    windows, block, rcv = records.shape
    tiles = rcv // 8
    none = hits.shape[0]
    shots = numbers.shape[0] - 2 * windows
    size = shots // groups

    def body(number_ref, rec_hbm, hit_ref, thr_ref, both_ref, *refs):
        refs, scratch = refs[:-6], refs[-6:]
        cuts_ref, rec_ref, diff_ref, base_ref, sum_ref, sem = scratch
        part_refs, (cut_ref, *energy_refs, shrunk_ref) = (
            refs[: len(energies)],
            refs[len(energies) :],
        )
        get_rec = pltpu.make_async_copy(rec_hbm, rec_ref, sem)
        get_rec.start()
        energy = jnp.concatenate([ref[...] for ref in part_refs], axis=0)
        sums = jnp.dot(hit_ref[...], energy, preferred_element_type=jnp.float32)
        cuts_ref[...] = thr_ref[...] * jnp.sqrt(sums / (SHOT_BLK * receivers) + epsilon)

        def widen(i, _):
            at = pl.multiple_of(i * 8, 8)
            cut_ref[pl.ds(at, 8)] = jnp.broadcast_to(
                cuts_ref[pl.ds(at, 8), :][:, None, :], (8, 8, block)
            )
            return 0

        lax.fori_loop(0, none // 8, widen, 0, unroll=2)
        cut_ref[none] = jnp.zeros((8, block), jnp.float32)
        sum_ref[...] = jnp.zeros_like(sum_ref)
        get_rec.wait()
        for w in range(windows):
            cover = (number_ref[windows + w] - number_ref[w]).astype(jnp.float32)
            scale = 1.0 / jnp.maximum(jnp.full((1, rcv), cover), 1.0)
            spread = (rec_ref[w] * scale).astype(jnp.bfloat16)
            base_ref[w] = forward(both_ref[...], spread).reshape(tiles, 8, block)

        def one_window(w, _):
            low, high = number_ref[w], number_ref[windows + w]
            diff_ref[w], base_ref[w], shrunk = shot_terms(base_ref[w], cut_ref, low, high, none)
            shrunk_ref[w] = shrunk.reshape(rcv, block).astype(jnp.bfloat16)
            return 0

        lax.fori_loop(0, windows, one_window, 0)
        def energies_of_window(w, _):
            diff, base = diff_ref[w], base_ref[w]

            def one_shot(row, _):
                cut = step_size * cut_ref[row][None]
                value = diff - jnp.minimum(jnp.maximum(base, -cut), cut)
                sum_ref[number_ref[2 * windows + row]] = jnp.sum(value * value, axis=0)
                return 0

            lax.fori_loop(number_ref[w], number_ref[windows + w], one_shot, 0)
            return 0

        lax.fori_loop(0, windows, energies_of_window, 0)
        for g in range(groups):
            energies_out = jnp.sum(sum_ref[g * size : (g + 1) * size], axis=1)
            energy_refs[g][...] = energies_out.astype(jnp.bfloat16)

    terms = pltpu.VMEM((windows, tiles, 8, block), jnp.float32)
    return pl.pallas_call(
        body,
        in_specs=[full_smem(), pl.BlockSpec(memory_space=pltpu.HBM)]
        + [full_vmem()] * (3 + len(energies)),
        out_specs=[full_vmem()] * (groups + 2),
        out_shape=[jax.ShapeDtypeStruct((none + 1, 8, block), jnp.float32)]
        + [jax.ShapeDtypeStruct((size, block), jnp.bfloat16)] * groups
        + [jax.ShapeDtypeStruct((windows, rcv, block), jnp.bfloat16)],
        scratch_shapes=[
            pltpu.VMEM((none, block), jnp.float32),
            pltpu.VMEM((windows, block, rcv), jnp.float32),
            terms,
            terms,
            pltpu.VMEM((shots, 8, block), jnp.float32),
            pltpu.SemaphoreType.DMA,
        ],
        compiler_params=params(),
        cost_estimate=pl.CostEstimate(flops=1, bytes_accessed=6 << 20, transcendentals=0),
        name="second_energies",
    )(numbers, records, hits, thresholds, both, *energies)


def remainder(records, sums, both):
    windows, block, rcv = records.shape
    chunk = 4
    chunks = windows // chunk

    def body(rec_hbm, sum_ref, both_ref, out_hbm, rec_ref, out_ref, sem):
        def copy(c, source, target, k):
            part = pl.ds(c * chunk, chunk)
            return pltpu.make_async_copy(source.at[part], target.at[part], sem.at[k])

        for c in range(chunks):
            copy(c, rec_hbm, rec_ref, c).start()
        for c in range(chunks):
            sums = sum_ref[c * chunk : (c + 1) * chunk].reshape(chunk * rcv, block)
            blended = backward(both_ref[...], sums)
            copy(c, rec_hbm, rec_ref, c).wait()
            for w in range(chunk):
                at = c * chunk + w
                out_ref[at] = rec_ref[at] - step_size * blended[:, w * rcv : (w + 1) * rcv]
            copy(c, out_ref, out_hbm, chunks + c).start()
        for c in range(chunks):
            copy(c, out_ref, out_hbm, chunks + c).wait()

    own = pltpu.VMEM((windows, block, rcv), jnp.float32)
    return pl.pallas_call(
        body,
        in_specs=[pl.BlockSpec(memory_space=pltpu.HBM), full_vmem(), full_vmem()],
        out_specs=pl.BlockSpec(memory_space=pl.ANY),
        out_shape=jax.ShapeDtypeStruct((windows, block, rcv), jnp.float32),
        scratch_shapes=[own, own, pltpu.SemaphoreType.DMA((2 * chunks,))],
        compiler_params=params(),
        cost_estimate=pl.CostEstimate(flops=1, bytes_accessed=4 << 20, transcendentals=0),
        name="residual_of_records",
    )(records, sums, both)


def second(arrived, cuts, numbers, capacity, shot_dev):
    owners, rows, block = arrived.shape
    rcv = rows // capacity
    tiles = rcv // 8
    count = owners * capacity
    none = cuts.shape[0] - 1
    shots = none - shot_dev

    def body(number_ref, in_ref, cut_ref, out_ref, diff_ref, base_ref):
        def one_block(place):
            slot = number_ref[place]
            owner = slot // capacity
            start = pl.multiple_of((slot - owner * capacity) * rcv, rcv)
            coef = in_ref[owner, pl.ds(start, rcv), :].astype(jnp.float32)
            diff_ref[slot], base_ref[slot], _ = shot_terms(
                coef.reshape(tiles, 8, block), cut_ref,
                number_ref[count + slot], number_ref[2 * count + slot], none,
            )

        def some_blocks(i, _):
            for u in range(BLOCKS_STEP):
                one_block(BLOCKS_STEP * i + u)
            return 0

        lax.fori_loop(0, number_ref[number_ref.shape[0] - 1], some_blocks, 0)

        def one_shot(shot, _):
            cut = step_size * cut_ref[shots + shot][None]
            for q in range(SHOT_BLK):
                entry = shot * SHOT_BLK + q
                slot = number_ref[3 * count + entry]
                value = diff_ref[slot] - jnp.minimum(jnp.maximum(base_ref[slot], -cut), cut)
                out_ref[entry] = value.reshape(rcv, block)
            return 0

        lax.fori_loop(0, shot_dev, one_shot, 0, unroll=4)

    terms = pltpu.VMEM((count, tiles, 8, block), jnp.float32)
    return pl.pallas_call(
        body,
        in_specs=[full_smem()] + [full_vmem()] * 2,
        out_specs=full_vmem(),
        out_shape=jax.ShapeDtypeStruct((shot_dev * SHOT_BLK, rcv, block), jnp.float32),
        scratch_shapes=[terms, terms],
        compiler_params=params(),
        cost_estimate=pl.CostEstimate(flops=1, bytes_accessed=8 << 20, transcendentals=0),
        name="second_coefficients",
    )(numbers, arrived, cuts)


def finish(values, energies, thresholds, both, receivers):
    entries, rcv, block = values.shape
    shot_dev = entries // SHOT_BLK
    step = min(2, shot_dev)

    def body(in_ref, thr_ref, both_ref, *refs):
        out_hbm, out_ref, sem = refs[-3:]
        energy = refs[0][...].astype(jnp.float32)
        for ref in refs[1:-3]:
            energy = energy + ref[...].astype(jnp.float32)
        cuts = thr_ref[...] * jnp.sqrt(energy / (SHOT_BLK * receivers) + epsilon)
        copies = []
        for at in range(0, shot_dev, step):
            for i in range(at, at + step):
                cut = cuts[i : i + 1, :]
                value = in_ref[i * SHOT_BLK : (i + 1) * SHOT_BLK].reshape(SHOT_BLK * rcv, block)
                shrunk = value - jnp.minimum(jnp.maximum(value, -cut), cut)
                model = lax.dot_general(
                    both_ref[:, :block], shrunk.astype(jnp.bfloat16), (((1,), (1,)), ((), ())),
                    preferred_element_type=jnp.float32,
                )
                for q in range(SHOT_BLK):
                    out_ref[i, q] = model[:, q * rcv : (q + 1) * rcv].astype(jnp.bfloat16)
            copy = pltpu.make_async_copy(
                out_ref.at[pl.ds(at, step)], out_hbm.at[pl.ds(at, step)], sem.at[at // step]
            )
            copy.start()
            copies.append(copy)
        for copy in copies:
            copy.wait()

    return pl.pallas_call(
        body,
        in_specs=[full_vmem()] * (3 + len(energies)),
        out_specs=pl.BlockSpec(memory_space=pl.ANY),
        out_shape=jax.ShapeDtypeStruct((shot_dev, SHOT_BLK, block, rcv), jnp.bfloat16),
        scratch_shapes=[
            pltpu.VMEM((shot_dev, SHOT_BLK, block, rcv), jnp.bfloat16),
            pltpu.SemaphoreType.DMA((shot_dev // step,)),
        ],
        compiler_params=params(),
        name="model_of_shots",
    )(values, thresholds, both, *energies)


def over_receivers(values):
    if lax.axis_size("rcv") == 2:
        return [values, lax.ppermute(values, "rcv", [(0, 1), (1, 0)])]
    return [lax.psum(values.astype(jnp.float32), "rcv").astype(values.dtype)]


def rotate(values, stride, by, size):
    n = lax.axis_size("shot")
    pairs = []
    for i in range(n):
        place = (i // stride) % size
        pairs.append((i, i + ((place + by) % size - place) * stride))
    return lax.ppermute(values, "shot", pairs)


def zorder(far):
    return list((2, 3, 1)) if far == 4 else list(range(1, far))


def local(record_data, offsets, thresholds):
    owners = lax.axis_size("shot")
    me = lax.axis_index("shot")
    windows, _, block, rcv = record_data.shape
    shots = offsets.shape[0]
    shot_dev = shots // owners
    pairs = shot_dev // 2
    pair_slots = min(pairs, owners // (SHOT_BLK + 1))
    capacity = (pairs + pair_slots - 1) // pair_slots
    receivers = rcv * lax.axis_size("rcv")

    high, low = split_bf16(jnp.asarray(cosine_table(block).T))
    both = jnp.concatenate([high, low], axis=1)
    records = record_data.reshape(windows, block, rcv)
    thr = thresholds[None, :]
    window_ids = jnp.arange(windows, dtype=jnp.int32)

    packed, energy = head(records, offsets, me, owners, capacity, both)
    packed, records, offsets, thr = lax.optimization_barrier((packed, records, offsets, thr))
    arrived = lax.all_to_all(packed, "shot", split_axis=0, concat_axis=0, tiled=True)

    near = min(4, owners)
    far = owners // near
    energy = jnp.concatenate([energy] + [rotate(energy, near, j, far) for j in zorder(far)])
    energy, offsets = lax.optimization_barrier((energy, offsets))
    energy = sum(part.astype(jnp.float32) for part in over_receivers(energy)).astype(jnp.bfloat16)
    energies = [energy] + [rotate(energy, 1, j, near) for j in range(1, near)]
    back = jnp.asarray([0] + zorder(far), jnp.int32)[None, :]
    side = jnp.arange(near, dtype=jnp.int32)[:, None]
    origin = (me // near - back + far) % far * near + (me % near - side + near) % near
    energy_ids = (window_ids * owners + origin[:, :, None]).reshape(-1)

    index = jnp.arange(shots, dtype=jnp.int32)
    ahead = (offsets[None, :] < offsets[:, None]) | (
        (offsets[None, :] == offsets[:, None]) & (index[None, :] < index[:, None])
    )
    place = jnp.sum(ahead.astype(jnp.int32), axis=1)
    ordered = jnp.sum(jnp.where(place[None, :] == index[:, None], offsets[None, :], 0), axis=1)
    mine = lax.dynamic_slice(offsets, (me * shot_dev,), (shot_dev,))
    all_offsets = jnp.concatenate([ordered, mine])
    grid_ids = window_ids[None, :] * owners + jnp.arange(owners, dtype=jnp.int32)[:, None]
    hits = landed(energy_ids[None, :], all_offsets[:, None]).astype(jnp.bfloat16)

    def bounds(ids):
        below = jnp.sum((offsets < ids[..., None] - (SHOT_BLK - 1)).astype(jnp.int32), axis=-1)
        upto = jnp.sum((offsets <= ids[..., None]).astype(jnp.int32), axis=-1)
        return below, upto

    own_lows, own_highs = bounds(window_ids * owners + me)

    slot_ids = jnp.arange(capacity, dtype=jnp.int32)
    held = jnp.max(landed(grid_ids[:, :, None], mine).astype(jnp.int32), axis=2)
    before = (window_ids[:, None] < window_ids[None, :]).astype(jnp.int32)
    held_rank = jnp.sum(held[:, :, None] * before, axis=1)
    taken = (held_rank[:, None, :] == slot_ids[None, :, None]) & (held[:, None, :] > 0)
    held_ids = jnp.sum(jnp.where(taken, grid_ids[:, None, :], 0), axis=2)
    valid = jnp.sum(taken.astype(jnp.int32), axis=2)
    lows, highs = bounds(held_ids)
    lows, highs = lows * valid, highs * valid
    targets = mine[:, None] + jnp.arange(SHOT_BLK, dtype=jnp.int32)[None, :]
    slot_of = jnp.arange(owners, dtype=jnp.int32)[:, None] * capacity + held_rank
    slots = jnp.sum(
        jnp.where(targets[:, :, None, None] == grid_ids[None, None], slot_of[None, None], 0),
        axis=(2, 3),
    )

    filled = valid.reshape(-1)
    count = jnp.arange(filled.shape[0], dtype=jnp.int32)
    nth = jnp.sum(jnp.where(count[None, :] < count[:, None], filled[None, :], 0), axis=1)
    chosen = (nth[None, :] == count[:, None]) & (filled[None, :] > 0)
    chosen = jnp.sum(jnp.where(chosen, count[None, :], 0), axis=1)
    steps = (jnp.sum(filled) + BLOCKS_STEP - 1) // BLOCKS_STEP
    numbers = jnp.concatenate(
        [chosen, lows.reshape(-1), highs.reshape(-1), slots.reshape(-1), steps[None]]
    )
    group = index // shot_dev
    away = (group % near - me % near + near) % near * far
    away = (away + (group // near - me // near + far) % far) * shot_dev + index % shot_dev
    order = jnp.sum(jnp.where(place[None, :] == index[:, None], away[None, :], 0), axis=1)
    own_numbers = jnp.concatenate([own_lows, own_highs, order])

    records = pltpu.with_memory_space_constraint(records, pltpu.HBM)
    hits, own_numbers, numbers = lax.optimization_barrier((hits, own_numbers, numbers))
    cuts, *landed_parts, sums = landed_energies(
        records, energies, hits, thr, own_numbers, both, near, receivers
    )
    residual = remainder(records, sums, both)
    plane = [landed_parts[0]] + [rotate(landed_parts[j], 1, j, near) for j in range(1, near)]
    *plane, residual = lax.optimization_barrier((*plane, residual))
    plane = sum(part.astype(jnp.float32) for part in plane).astype(jnp.bfloat16)
    plane = sum(part.astype(jnp.float32) for part in over_receivers(plane)).astype(jnp.bfloat16)
    energies = [plane[:shot_dev]] + [
        rotate(plane[j * shot_dev : (j + 1) * shot_dev], near, j, far) for j in range(1, far)
    ]
    values = second(arrived, cuts, numbers, capacity, shot_dev)
    model = finish(values, energies, thr, both, receivers)
    return (model, residual.reshape(windows, 1, block, rcv))


def solution(mesh):
    return jax.shard_map(
        local,
        mesh=mesh,
        in_specs=(P(None, "shot", None, "rcv"), P(), P()),
        out_specs=(P("shot", None, None, "rcv"), P(None, "shot", None, "rcv")),
        check_vma=False,
    )
```

```python
import jax
import jax.numpy as jnp
import numpy as np
from jax import lax
from jax.experimental import pallas as pl
from jax.experimental.pallas import tpu as pltpu
from jax.sharding import PartitionSpec as P

SHOT_BLK = 4
momentum = 0.5
epsilon = 1e-06
step_size = 1.0 + momentum
VMEM_BYTES = 16 * 1024 * 1024
BLOCKS_STEP = 4
HEAD_VMEM_BYTES = 60 * 1024 * 1024


def cosine_table(length):
    rows = np.arange(length, dtype=np.float64)[:, None]
    cols = np.arange(length, dtype=np.float64)[None, :]
    table = np.cos(np.pi * (cols + 0.5) * rows / length) * np.sqrt(2.0 / length)
    return np.where(rows == 0, table * np.sqrt(0.5), table).astype(np.float32)


def split_bf16(values):
    high = values.astype(jnp.bfloat16)
    low = (values - high.astype(jnp.float32)).astype(jnp.bfloat16)
    return high, low


def full_vmem():
    return pl.BlockSpec(memory_space=pltpu.VMEM)


def full_smem():
    return pl.BlockSpec(memory_space=pltpu.SMEM)


def params(vmem=VMEM_BYTES):
    return pltpu.CompilerParams(vmem_limit_bytes=vmem)


def forward(both, values):
    block = values.shape[0]
    parts = lax.dot_general(
        values, both, (((0,), (0,)), ((), ())), preferred_element_type=jnp.float32
    )
    return parts[:, :block] + parts[:, block:]


def backward(both, coefficients):
    doubled = jnp.concatenate([coefficients, coefficients], axis=1)
    return lax.dot_general(
        both, doubled, (((1,), (1,)), ((), ())), preferred_element_type=jnp.float32
    )


def landed(ids, offsets):
    lag = ids - offsets
    return (lag >= 0) & (lag < SHOT_BLK)


def head(records, offsets, me, owners, capacity, both):
    windows, block, rcv = records.shape
    shots = offsets.shape[0]
    shot_dev = shots // owners
    chunk = 8
    chunks = windows // chunk
    f32, bf16 = jnp.float32, jnp.bfloat16

    def body(
        me_ref, off_hbm, rec_hbm, both_hbm, out_ref, energy_hbm,
        off_ref, rec_ref, both_ref, sent_ref, energy_ref, table_ref, table_smem,
        small_sem, rec_sem, out_sem,
    ):
        get_off = pltpu.make_async_copy(off_hbm, off_ref, small_sem.at[0])
        get_both = pltpu.make_async_copy(both_hbm, both_ref, small_sem.at[1])
        get_rec = [
            pltpu.make_async_copy(
                rec_hbm.at[pl.ds(c * chunk, chunk)],
                rec_ref.at[pl.ds(c * chunk, chunk)],
                rec_sem.at[c],
            )
            for c in range(chunks)
        ]
        get_off.start()
        get_both.start()
        for copy in get_rec:
            copy.start()
        get_off.wait()

        ids = lax.broadcasted_iota(jnp.int32, (windows, shots), 0) * owners + me_ref[0]
        hits = jnp.where(landed(ids, off_ref[...]), 1.0, 0.0)
        cover = jnp.sum(hits, axis=1, keepdims=True)
        scale = 1.0 / jnp.maximum(cover, 1.0)

        shot = lax.broadcasted_iota(jnp.int32, (shots, owners), 0)
        first = lax.broadcasted_iota(jnp.int32, (shots, owners), 1) * shot_dev
        member = jnp.where((shot >= first) & (shot < first + shot_dev), 1.0, 0.0)
        counts = jnp.dot(hits.astype(bf16), member.astype(bf16), preferred_element_type=f32)
        present = jnp.where(counts > 0.5, 1.0, 0.0)
        after = lax.broadcasted_iota(jnp.int32, (windows, windows), 0)
        before = lax.broadcasted_iota(jnp.int32, (windows, windows), 1)
        lower = jnp.where(before < after, 1.0, 0.0)
        rank = jnp.dot(lower.astype(bf16), present.astype(bf16), preferred_element_type=f32)
        rank = rank.astype(jnp.int32)
        window = lax.broadcasted_iota(jnp.int32, (windows, owners), 0)
        for i in range(capacity):
            here = (rank == i) & (present > 0.5)
            table_ref[i : i + 1, :owners] = jnp.sum(
                jnp.where(here, window, 0), axis=0, keepdims=True
            )
        put_table = pltpu.make_async_copy(table_ref, table_smem, small_sem.at[2])
        put_table.start()

        get_both.wait()
        rows = []
        for c in range(chunks):
            get_rec[c].wait()
            for w in range(c * chunk, (c + 1) * chunk):
                spread = (rec_ref[w] * scale[w : w + 1, 0:1]).astype(bf16)
                coef = lax.dot_general(
                    spread, both_ref[:, :block], (((0,), (0,)), ((), ())),
                    preferred_element_type=f32,
                )
                sent_ref[w] = coef.astype(bf16)
                rows.append(jnp.sum(coef * coef, axis=0, keepdims=True))

        energy_ref[...] = jnp.concatenate(rows, axis=0).astype(bf16)
        put_energy = pltpu.make_async_copy(energy_ref, energy_hbm, small_sem.at[3])
        put_energy.start()
        put_table.wait()

        def send(h, i):
            return pltpu.make_async_copy(
                sent_ref.at[table_smem[i, h]],
                out_ref.at[h, pl.ds(i * rcv, rcv), :],
                out_sem.at[h * capacity + i],
            )

        for h in range(owners):
            for i in range(capacity):
                send(h, i).start()
        for h in range(owners):
            for i in range(capacity):
                send(h, i).wait()
        put_energy.wait()

    hbm = pl.BlockSpec(memory_space=pltpu.HBM)
    table_shape = (8, 128)
    return pl.pallas_call(
        body,
        in_specs=[full_smem(), hbm, hbm, hbm],
        out_specs=[pl.BlockSpec(memory_space=pl.ANY)] * 2,
        out_shape=[
            jax.ShapeDtypeStruct((owners, capacity * rcv, block), bf16),
            jax.ShapeDtypeStruct((windows, block), bf16),
        ],
        scratch_shapes=[
            pltpu.VMEM((1, shots), jnp.int32),
            pltpu.VMEM((windows, block, rcv), f32),
            pltpu.VMEM((block, 2 * block), bf16),
            pltpu.VMEM((windows, rcv, block), bf16),
            pltpu.VMEM((windows, block), bf16),
            pltpu.VMEM(table_shape, jnp.int32),
            pltpu.SMEM(table_shape, jnp.int32),
            pltpu.SemaphoreType.DMA((4,)),
            pltpu.SemaphoreType.DMA((chunks,)),
            pltpu.SemaphoreType.DMA((owners * capacity,)),
        ],
        compiler_params=params(HEAD_VMEM_BYTES),
        name="pack_coefficients",
    )(me[None], offsets[None, :], records, both)


def clipped_sum(coef, cut_ref, low, high, none):
    size = jnp.abs(coef)
    peel, unroll = 6, 2

    def term(row):
        return jnp.minimum(size, cut_ref[jnp.where(row < high, row, none)][None])

    total = term(low)
    for u in range(1, peel):
        total = total + term(low + u)

    def add(j, total):
        for u in range(unroll):
            total = total + term(low + peel + j * unroll + u)
        return total

    left = jnp.maximum(high - low - peel, 0)
    total = lax.fori_loop(0, lax.div(left + unroll - 1, unroll), add, total)
    return jnp.where(coef < 0, -total, total)


def shot_terms(coef, cut_ref, low, high, none):
    clipped = clipped_sum(coef, cut_ref, low, high, none)
    many = jnp.full((1, 8, coef.shape[2]), (high - low).astype(jnp.float32))
    scale = step_size / jnp.maximum(many, 1.0)
    diff = (1.0 + step_size - scale * many) * coef + scale * clipped
    return diff, step_size * coef, many * coef - clipped


def landed_energies(records, energies, hits, thresholds, numbers, both, groups, receivers):
    windows, block, rcv = records.shape
    tiles = rcv // 8
    none = hits.shape[0]
    shots = numbers.shape[0] - 2 * windows
    size = shots // groups

    def body(number_ref, rec_hbm, hit_ref, thr_ref, both_ref, *refs):
        refs, scratch = refs[:-6], refs[-6:]
        cuts_ref, rec_ref, diff_ref, base_ref, sum_ref, sem = scratch
        part_refs, (cut_ref, *energy_refs, shrunk_ref) = (
            refs[: len(energies)],
            refs[len(energies) :],
        )
        get_rec = pltpu.make_async_copy(rec_hbm, rec_ref, sem)
        get_rec.start()
        energy = jnp.concatenate([ref[...] for ref in part_refs], axis=0)
        sums = jnp.dot(hit_ref[...], energy, preferred_element_type=jnp.float32)
        cuts_ref[...] = thr_ref[...] * jnp.sqrt(sums / (SHOT_BLK * receivers) + epsilon)

        def widen(i, _):
            at = pl.multiple_of(i * 8, 8)
            cut_ref[pl.ds(at, 8)] = jnp.broadcast_to(
                cuts_ref[pl.ds(at, 8), :][:, None, :], (8, 8, block)
            )
            return 0

        lax.fori_loop(0, none // 8, widen, 0, unroll=2)
        cut_ref[none] = jnp.zeros((8, block), jnp.float32)
        sum_ref[...] = jnp.zeros_like(sum_ref)
        get_rec.wait()
        for w in range(windows):
            cover = (number_ref[windows + w] - number_ref[w]).astype(jnp.float32)
            scale = 1.0 / jnp.maximum(jnp.full((1, rcv), cover), 1.0)
            spread = (rec_ref[w] * scale).astype(jnp.bfloat16)
            base_ref[w] = forward(both_ref[...], spread).reshape(tiles, 8, block)

        def one_window(w, _):
            low, high = number_ref[w], number_ref[windows + w]
            diff_ref[w], base_ref[w], shrunk = shot_terms(base_ref[w], cut_ref, low, high, none)
            shrunk_ref[w] = shrunk.reshape(rcv, block).astype(jnp.bfloat16)
            return 0

        lax.fori_loop(0, windows, one_window, 0)
        def energies_of_window(w, _):
            diff, base = diff_ref[w], base_ref[w]

            def one_shot(row, _):
                cut = step_size * cut_ref[row][None]
                value = diff - jnp.minimum(jnp.maximum(base, -cut), cut)
                sum_ref[number_ref[2 * windows + row]] = jnp.sum(value * value, axis=0)
                return 0

            lax.fori_loop(number_ref[w], number_ref[windows + w], one_shot, 0)
            return 0

        lax.fori_loop(0, windows, energies_of_window, 0)
        for g in range(groups):
            energies_out = jnp.sum(sum_ref[g * size : (g + 1) * size], axis=1)
            energy_refs[g][...] = energies_out.astype(jnp.bfloat16)

    terms = pltpu.VMEM((windows, tiles, 8, block), jnp.float32)
    return pl.pallas_call(
        body,
        in_specs=[full_smem(), pl.BlockSpec(memory_space=pltpu.HBM)]
        + [full_vmem()] * (3 + len(energies)),
        out_specs=[full_vmem()] * (groups + 2),
        out_shape=[jax.ShapeDtypeStruct((none + 1, 8, block), jnp.float32)]
        + [jax.ShapeDtypeStruct((size, block), jnp.bfloat16)] * groups
        + [jax.ShapeDtypeStruct((windows, rcv, block), jnp.bfloat16)],
        scratch_shapes=[
            pltpu.VMEM((none, block), jnp.float32),
            pltpu.VMEM((windows, block, rcv), jnp.float32),
            terms,
            terms,
            pltpu.VMEM((shots, 8, block), jnp.float32),
            pltpu.SemaphoreType.DMA,
        ],
        compiler_params=params(),
        cost_estimate=pl.CostEstimate(flops=1, bytes_accessed=6 << 20, transcendentals=0),
        name="second_energies",
    )(numbers, records, hits, thresholds, both, *energies)


def remainder(records, sums, both):
    windows, block, rcv = records.shape
    chunk = 4
    chunks = windows // chunk

    def body(rec_hbm, sum_ref, both_ref, out_hbm, rec_ref, out_ref, sem):
        def copy(c, source, target, k):
            part = pl.ds(c * chunk, chunk)
            return pltpu.make_async_copy(source.at[part], target.at[part], sem.at[k])

        for c in range(chunks):
            copy(c, rec_hbm, rec_ref, c).start()
        for c in range(chunks):
            sums = sum_ref[c * chunk : (c + 1) * chunk].reshape(chunk * rcv, block)
            blended = backward(both_ref[...], sums)
            copy(c, rec_hbm, rec_ref, c).wait()
            for w in range(chunk):
                at = c * chunk + w
                out_ref[at] = rec_ref[at] - step_size * blended[:, w * rcv : (w + 1) * rcv]
            copy(c, out_ref, out_hbm, chunks + c).start()
        for c in range(chunks):
            copy(c, out_ref, out_hbm, chunks + c).wait()

    own = pltpu.VMEM((windows, block, rcv), jnp.float32)
    return pl.pallas_call(
        body,
        in_specs=[pl.BlockSpec(memory_space=pltpu.HBM), full_vmem(), full_vmem()],
        out_specs=pl.BlockSpec(memory_space=pl.ANY),
        out_shape=jax.ShapeDtypeStruct((windows, block, rcv), jnp.float32),
        scratch_shapes=[own, own, pltpu.SemaphoreType.DMA((2 * chunks,))],
        compiler_params=params(),
        cost_estimate=pl.CostEstimate(flops=1, bytes_accessed=4 << 20, transcendentals=0),
        name="residual_of_records",
    )(records, sums, both)


def second(arrived, cuts, numbers, capacity, shot_dev):
    owners, rows, block = arrived.shape
    rcv = rows // capacity
    tiles = rcv // 8
    count = owners * capacity
    none = cuts.shape[0] - 1
    shots = none - shot_dev

    def body(number_ref, in_ref, cut_ref, out_ref, diff_ref, base_ref):
        def one_block(place):
            slot = number_ref[place]
            owner = slot // capacity
            start = pl.multiple_of((slot - owner * capacity) * rcv, rcv)
            coef = in_ref[owner, pl.ds(start, rcv), :].astype(jnp.float32)
            diff_ref[slot], base_ref[slot], _ = shot_terms(
                coef.reshape(tiles, 8, block), cut_ref,
                number_ref[count + slot], number_ref[2 * count + slot], none,
            )

        def some_blocks(i, _):
            for u in range(BLOCKS_STEP):
                one_block(BLOCKS_STEP * i + u)
            return 0

        lax.fori_loop(0, number_ref[number_ref.shape[0] - 1], some_blocks, 0)

        def one_shot(shot, _):
            cut = step_size * cut_ref[shots + shot][None]
            for q in range(SHOT_BLK):
                entry = shot * SHOT_BLK + q
                slot = number_ref[3 * count + entry]
                value = diff_ref[slot] - jnp.minimum(jnp.maximum(base_ref[slot], -cut), cut)
                out_ref[entry] = value.reshape(rcv, block)
            return 0

        lax.fori_loop(0, shot_dev, one_shot, 0, unroll=4)

    terms = pltpu.VMEM((count, tiles, 8, block), jnp.float32)
    return pl.pallas_call(
        body,
        in_specs=[full_smem()] + [full_vmem()] * 2,
        out_specs=full_vmem(),
        out_shape=jax.ShapeDtypeStruct((shot_dev * SHOT_BLK, rcv, block), jnp.float32),
        scratch_shapes=[terms, terms],
        compiler_params=params(),
        cost_estimate=pl.CostEstimate(flops=1, bytes_accessed=8 << 20, transcendentals=0),
        name="second_coefficients",
    )(numbers, arrived, cuts)


def finish(values, energies, thresholds, both, receivers):
    entries, rcv, block = values.shape
    shot_dev = entries // SHOT_BLK
    step = min(2, shot_dev)

    def body(in_ref, thr_ref, both_ref, *refs):
        out_hbm, out_ref, sem = refs[-3:]
        energy = refs[0][...].astype(jnp.float32)
        for ref in refs[1:-3]:
            energy = energy + ref[...].astype(jnp.float32)
        cuts = thr_ref[...] * jnp.sqrt(energy / (SHOT_BLK * receivers) + epsilon)
        copies = []
        for at in range(0, shot_dev, step):
            for i in range(at, at + step):
                cut = cuts[i : i + 1, :]
                value = in_ref[i * SHOT_BLK : (i + 1) * SHOT_BLK].reshape(SHOT_BLK * rcv, block)
                shrunk = value - jnp.minimum(jnp.maximum(value, -cut), cut)
                model = lax.dot_general(
                    both_ref[:, :block], shrunk.astype(jnp.bfloat16), (((1,), (1,)), ((), ())),
                    preferred_element_type=jnp.float32,
                )
                for q in range(SHOT_BLK):
                    out_ref[i, q] = model[:, q * rcv : (q + 1) * rcv].astype(jnp.bfloat16)
            copy = pltpu.make_async_copy(
                out_ref.at[pl.ds(at, step)], out_hbm.at[pl.ds(at, step)], sem.at[at // step]
            )
            copy.start()
            copies.append(copy)
        for copy in copies:
            copy.wait()

    return pl.pallas_call(
        body,
        in_specs=[full_vmem()] * (3 + len(energies)),
        out_specs=pl.BlockSpec(memory_space=pl.ANY),
        out_shape=jax.ShapeDtypeStruct((shot_dev, SHOT_BLK, block, rcv), jnp.bfloat16),
        scratch_shapes=[
            pltpu.VMEM((shot_dev, SHOT_BLK, block, rcv), jnp.bfloat16),
            pltpu.SemaphoreType.DMA((shot_dev // step,)),
        ],
        compiler_params=params(),
        name="model_of_shots",
    )(values, thresholds, both, *energies)


def over_receivers(values):
    if lax.axis_size("rcv") == 2:
        return [values, lax.ppermute(values, "rcv", [(0, 1), (1, 0)])]
    return [lax.psum(values.astype(jnp.float32), "rcv").astype(values.dtype)]


def rotate(values, stride, by, size):
    n = lax.axis_size("shot")
    pairs = []
    for i in range(n):
        place = (i // stride) % size
        pairs.append((i, i + ((place + by) % size - place) * stride))
    return lax.ppermute(values, "shot", pairs)


def zorder(far):
    return list((2, 3, 1)) if far == 4 else list(range(1, far))


def local(record_data, offsets, thresholds):
    owners = lax.axis_size("shot")
    me = lax.axis_index("shot")
    windows, _, block, rcv = record_data.shape
    shots = offsets.shape[0]
    shot_dev = shots // owners
    pairs = shot_dev // 2
    pair_slots = min(pairs, owners // (SHOT_BLK + 1))
    capacity = (pairs + pair_slots - 1) // pair_slots
    receivers = rcv * lax.axis_size("rcv")

    high, low = split_bf16(jnp.asarray(cosine_table(block).T))
    both = jnp.concatenate([high, low], axis=1)
    records = record_data.reshape(windows, block, rcv)
    thr = thresholds[None, :]
    window_ids = jnp.arange(windows, dtype=jnp.int32)

    packed, energy = head(records, offsets, me, owners, capacity, both)
    packed, records, offsets, thr = lax.optimization_barrier((packed, records, offsets, thr))
    arrived = lax.all_to_all(packed, "shot", split_axis=0, concat_axis=0, tiled=True)

    near = min(4, owners)
    far = owners // near
    energy = jnp.concatenate([energy] + [rotate(energy, near, j, far) for j in zorder(far)])
    energy, offsets = lax.optimization_barrier((energy, offsets))
    energy = sum(part.astype(jnp.float32) for part in over_receivers(energy)).astype(jnp.bfloat16)
    energies = [energy] + [rotate(energy, 1, j, near) for j in range(1, near)]
    back = jnp.asarray([0] + zorder(far), jnp.int32)[None, :]
    side = jnp.arange(near, dtype=jnp.int32)[:, None]
    origin = (me // near - back + far) % far * near + (me % near - side + near) % near
    energy_ids = (window_ids * owners + origin[:, :, None]).reshape(-1)

    index = jnp.arange(shots, dtype=jnp.int32)
    ahead = (offsets[None, :] < offsets[:, None]) | (
        (offsets[None, :] == offsets[:, None]) & (index[None, :] < index[:, None])
    )
    place = jnp.sum(ahead.astype(jnp.int32), axis=1)
    ordered = jnp.sum(jnp.where(place[None, :] == index[:, None], offsets[None, :], 0), axis=1)
    mine = lax.dynamic_slice(offsets, (me * shot_dev,), (shot_dev,))
    all_offsets = jnp.concatenate([ordered, mine])
    grid_ids = window_ids[None, :] * owners + jnp.arange(owners, dtype=jnp.int32)[:, None]
    hits = landed(energy_ids[None, :], all_offsets[:, None]).astype(jnp.bfloat16)

    def bounds(ids):
        below = jnp.sum((offsets < ids[..., None] - (SHOT_BLK - 1)).astype(jnp.int32), axis=-1)
        upto = jnp.sum((offsets <= ids[..., None]).astype(jnp.int32), axis=-1)
        return below, upto

    own_lows, own_highs = bounds(window_ids * owners + me)

    slot_ids = jnp.arange(capacity, dtype=jnp.int32)
    held = jnp.max(landed(grid_ids[:, :, None], mine).astype(jnp.int32), axis=2)
    before = (window_ids[:, None] < window_ids[None, :]).astype(jnp.int32)
    held_rank = jnp.sum(held[:, :, None] * before, axis=1)
    taken = (held_rank[:, None, :] == slot_ids[None, :, None]) & (held[:, None, :] > 0)
    held_ids = jnp.sum(jnp.where(taken, grid_ids[:, None, :], 0), axis=2)
    valid = jnp.sum(taken.astype(jnp.int32), axis=2)
    lows, highs = bounds(held_ids)
    lows, highs = lows * valid, highs * valid
    targets = mine[:, None] + jnp.arange(SHOT_BLK, dtype=jnp.int32)[None, :]
    slot_of = jnp.arange(owners, dtype=jnp.int32)[:, None] * capacity + held_rank
    slots = jnp.sum(
        jnp.where(targets[:, :, None, None] == grid_ids[None, None], slot_of[None, None], 0),
        axis=(2, 3),
    )

    filled = valid.reshape(-1)
    count = jnp.arange(filled.shape[0], dtype=jnp.int32)
    nth = jnp.sum(jnp.where(count[None, :] < count[:, None], filled[None, :], 0), axis=1)
    chosen = (nth[None, :] == count[:, None]) & (filled[None, :] > 0)
    chosen = jnp.sum(jnp.where(chosen, count[None, :], 0), axis=1)
    steps = (jnp.sum(filled) + BLOCKS_STEP - 1) // BLOCKS_STEP
    numbers = jnp.concatenate(
        [chosen, lows.reshape(-1), highs.reshape(-1), slots.reshape(-1), steps[None]]
    )
    group = index // shot_dev
    away = (group % near - me % near + near) % near * far
    away = (away + (group // near - me // near + far) % far) * shot_dev + index % shot_dev
    order = jnp.sum(jnp.where(place[None, :] == index[:, None], away[None, :], 0), axis=1)
    own_numbers = jnp.concatenate([own_lows, own_highs, order])

    records = pltpu.with_memory_space_constraint(records, pltpu.HBM)
    hits, own_numbers, numbers = lax.optimization_barrier((hits, own_numbers, numbers))
    cuts, *landed_parts, sums = landed_energies(
        records, energies, hits, thr, own_numbers, both, near, receivers
    )
    residual = remainder(records, sums, both)
    plane = [landed_parts[0]] + [rotate(landed_parts[j], 1, j, near) for j in range(1, near)]
    *plane, residual = lax.optimization_barrier((*plane, residual))
    plane = sum(part.astype(jnp.float32) for part in plane).astype(jnp.bfloat16)
    plane = sum(part.astype(jnp.float32) for part in over_receivers(plane)).astype(jnp.bfloat16)
    energies = [plane[:shot_dev]] + [
        rotate(plane[j * shot_dev : (j + 1) * shot_dev], near, j, far) for j in range(1, far)
    ]
    values = second(arrived, cuts, numbers, capacity, shot_dev)
    model = finish(values, energies, thr, both, receivers)
    return (model, residual.reshape(windows, 1, block, rcv))


def solution(mesh):
    return jax.shard_map(
        local,
        mesh=mesh,
        in_specs=(P(None, "shot", None, "rcv"), P(), P()),
        out_specs=(P("shot", None, None, "rcv"), P(None, "shot", None, "rcv")),
        check_vma=False,
    )
```
